256 devices in a mesh: rows: 256 (over y, x, z, core).
Axes of the slice: x: 4, y: 4, z: 8, core: 2. Of those that a mesh axis runs over, the one named last changes fastest.
Arguments:
- start_states: float32 [262144, 128], P('rows'), may hold values from -0.01171875 to 0.01171875
- start_steps: float32 [262144, 128], P('rows'), may hold values from -0.005859375 to 0.005859375
- onsite: float32 [4096, 64, 64], P('rows'), may hold values from -0.75 to 0.75
- couplings: float32 [4096, 4, 64, 64], P('rows'), may hold values from -0.375 to 0.375
- columns: int32 [4096, 4], P('rows'), may hold values from 0 to 4095, as said below
Outputs:
- states: float32 [262144, 128], P('rows')
- steps: float32 [262144, 128], P('rows')
The draws below stay inside these ranges and needn't reach their ends.
Inputs may be any that keep to these rules, and one draw needn't show every extreme that they name: `columns`: for block row b every entry names a block row 1 to 2 ahead of b modulo 4096; slot 0 is exactly 2 ahead.
All inputs are finite; a program needn't handle non-finite values. Where the reference program divides by a largest or mean magnitude, that divisor is 1e-20 or more.
Results may differ from the reference program's by a relative error of at most 0.0003.
Values sent between devices are 32-bit elements; how exact they have to be, the bound alone decides.
No kernel may reach another device: no remote copies, remote signals or barrier semaphores. Data moves between devices by JAX's collectives and lax.ppermute only.
A program may use at most 320 MiB of HBM per device.

```python
import jax
import jax.numpy as jnp
from jax import lax

BLK = 64
STATES = 128
SLOTS = 4
REACH = 2
ITERS = 2
FILTER = 3
BASIS = 384
NB = 4096
ORDER = 262144


def draw_columns(key, part):
    key = jax.random.fold_in(key, 7)
    ahead = jax.random.randint(key, (NB, SLOTS), 1, REACH + 1).astype(jnp.int32)
    ahead = ahead.at[:, 0].set(REACH)
    row_index = jnp.arange(NB, dtype=jnp.int32)[:, None]
    return jnp.mod(row_index + ahead, NB).astype(jnp.int32)


def steps_of(stream_key, shape, shards, low, high):
    def one(dim, shards_of):
        draws = jax.random.uniform(jax.random.fold_in(jax.random.fold_in(stream_key, 6), dim), (shards_of,), jnp.float32, low / len(shards), high / len(shards))
        return jnp.repeat(jnp.exp(draws), shape[dim] // shards_of).reshape((-1,) + (1,) * (len(shape) - dim - 1))

    gain = one(*shards[0])
    for cut in shards[1:]:
        gain = gain * one(*cut)
    return gain


def noise(key, extent, scale, limit, shards=(), kind=jnp.bfloat16):
    values = jax.random.normal(key, extent, jnp.float32) * scale
    if len(shards) > 0:
        values = steps_of(key, extent, shards, -0.22, 0.18) * values
    return jnp.clip(values, min=-limit, max=limit).astype(kind)


def setup_inputs(seed: int = 0) -> dict:
    arg_keys = jax.random.split(jax.random.key(seed), 6)
    return {
        "start_states": noise(arg_keys[0], (ORDER, STATES), ORDER ** -0.5, 0.01171875, ((0, 256),), jnp.float32),
        "start_steps": noise(arg_keys[1], (ORDER, STATES), (4 * ORDER) ** -0.5, 0.005859375, ((0, 256),), jnp.float32),
        "onsite": noise(arg_keys[2], (NB, BLK, BLK), BLK ** -0.5, 0.75, ((0, 256),), jnp.float32),
        "couplings": noise(arg_keys[3], (NB, SLOTS, BLK, BLK), (BLK * SLOTS) ** -0.5, 0.375, ((0, 256),), jnp.float32),
        "columns": draw_columns(jax.random.fold_in(arg_keys[5], 71), 0),
    }


precise = lax.Precision.HIGHEST

def block_offsets(couplings, ahead):
    stacked = []
    for distance in range(1, REACH + 1):
        weights = (ahead == distance).astype(jnp.float32)
        stacked.append(jnp.einsum('bj,bjpq->bpq', weights, couplings, precision=precise))
    return stacked

def apply_global(vectors, symmetric, offsets):
    result = jnp.einsum('bpq,bqc->bpc', symmetric, vectors, precision=precise)
    for distance in range(1, REACH + 1):
        block = offsets[distance - 1]
        result = result + jnp.einsum('bpq,bqc->bpc', block, jnp.roll(vectors, -distance, axis=0), precision=precise)
        back = jnp.einsum('bqp,bqc->bpc', block, vectors, precision=precise)
        result = result + jnp.roll(back, distance, axis=0)
    return result

def lower_inverse(lower):
    size = lower.shape[0]
    return lax.linalg.triangular_solve(lower, jnp.eye(size, dtype=jnp.float32), left_side=True, lower=True)

def ritz_filter(projected):
    bound = jnp.max(jnp.sum(jnp.abs(projected), axis=1))
    shifted = jnp.eye(BASIS, dtype=jnp.float32) - projected / bound
    coeffs = jnp.eye(BASIS, STATES, dtype=jnp.float32)
    for power in range(FILTER):
        coeffs = jnp.dot(shifted, coeffs, precision=precise)
    lower = jnp.linalg.cholesky(jnp.dot(coeffs.T, coeffs, precision=precise))
    return jnp.dot(coeffs, lower_inverse(lower).T, precision=precise)

def reference(start_states, start_steps, onsite, couplings, columns):
    total = onsite.shape[0]
    ahead = jnp.mod(columns - jnp.arange(total, dtype=jnp.int32)[:, None], total)
    offsets = block_offsets(couplings, ahead)
    symmetric = onsite + jnp.swapaxes(onsite, 1, 2)
    states = start_states
    steps = start_steps
    for sweep in range(ITERS):
        image = apply_global(states.reshape(total, BLK, STATES), symmetric, offsets).reshape(-1, STATES)
        basis = jnp.concatenate([states, image, steps], axis=1)
        lower = jnp.linalg.cholesky(jnp.dot(basis.T, basis, precision=precise))
        inverse = lower_inverse(lower)
        ortho = jnp.dot(basis, inverse.T, precision=precise)
        moved = apply_global(ortho.reshape(total, BLK, BASIS), symmetric, offsets).reshape(-1, BASIS)
        projected = jnp.dot(ortho.T, moved, precision=precise)
        projected = 0.5 * (projected + projected.T)
        coeffs = ritz_filter(projected)
        states = jnp.dot(ortho, coeffs, precision=precise)
        steps = jnp.dot(ortho[:, STATES:], coeffs[STATES:], precision=precise)
    return (states, steps)
```

```python
import jax
import jax.numpy as jnp
from jax import lax
from jax.sharding import PartitionSpec as P
from jax.experimental import pallas as pl
from jax.experimental.pallas import tpu as pltpu

BLK = 64
STATES = 128
N = 256
hi = lax.Precision.HIGHEST

STRIDE={'core':1,'z':2,'x':16,'y':64}; SIZE={'core':2,'z':8,'x':4,'y':4}
def shift(axis,k):
    s,n=STRIDE[axis],SIZE[axis]
    out=[]
    for i in range(N):
        c=(i//s)%n
        out.append((i, i+((c+k)%n-c)*s))
    return out
def coord(axis):
    return (lax.axis_index("rows")//STRIDE[axis])%SIZE[axis]
VM=pl.BlockSpec(memory_space=pltpu.VMEM)
SM=pl.BlockSpec(memory_space=pltpu.SMEM)
def f32(*s): return jax.ShapeDtypeStruct(s,jnp.float32)
EX=8
def split_kernel(n,p, co, cur, *msgs):
    c=co[0]
    for k in range(1,n):
        q=lax.rem(c+k,n)
        msgs[k-1][0:p]=cur[pl.ds(pl.multiple_of(q*p,8),p)]
        msgs[k-1][p:p+EX]=cur[n*p:n*p+EX]
def first_split(cur, axis):
    n=SIZE[axis]; p=(cur.shape[0]-EX)//n
    return pl.pallas_call(lambda *a: split_kernel(n,p,*a), in_specs=[SM,VM], out_specs=[VM]*(n-1),
        out_shape=[f32(p+EX,128)]*(n-1), name="split_"+axis)(coord(axis)[None],cur)
def rs_step(cur, msgs, axis, nxt):
    n=SIZE[axis]; p=(cur.shape[0]-EX)//n
    n2=SIZE[nxt] if nxt else 1
    p2=p//n2
    def kern(co,cur_ref,*rest):
        ins=rest[:n-1]; new=rest[n-1]; out=rest[n:]
        c=co[0]
        acc=cur_ref[pl.ds(pl.multiple_of(c*p,8),p)]
        ex=cur_ref[n*p:n*p+EX]
        for r in ins:
            acc=acc+r[0:p]; ex=ex+r[p:p+EX]
        new[0:p]=acc; new[p:p+EX]=ex
        if nxt: split_kernel(n2,p2,co.at[1:2],new,*out)
    co=jnp.stack([coord(axis),coord(nxt) if nxt else coord(axis)])
    res=pl.pallas_call(kern,in_specs=[SM]+[VM]*n,out_specs=[VM]*n2,
        out_shape=[f32(p+EX,128)]+[f32(p2+EX,128)]*(n2-1), name="rs_"+axis)(co,cur,*msgs)
    return res[0],res[1:]
def sum_all(cur,msgs):
    def kern(a,*rest):
        acc=a[...]
        for r in rest[:-1]: acc=acc+r[...]
        rest[-1][...]=acc
    return pl.pallas_call(kern,in_specs=[VM]*(1+len(msgs)),out_specs=VM,out_shape=f32(*cur.shape),name="sum_all")(cur,*msgs)
def send(msgs,axis):
    return [lax.ppermute(m,"rows",shift(axis,k+1)) for k,m in enumerate(msgs)]
def gather(own,p,axis):
    n=SIZE[axis]
    rec=[lax.ppermute(own,"rows",shift(axis,k)) for k in range(1,n)]
    def kern(co,o,*rest):
        c=co[0]; out=rest[-1]
        out[pl.ds(pl.multiple_of(c*p,8),p)]=o[0:p]
        for k in range(1,n):
            q=lax.rem(c-k+n,n)
            out[pl.ds(pl.multiple_of(q*p,8),p)]=rest[k-1][0:p]
    return pl.pallas_call(kern,in_specs=[SM]+[VM]*n,out_specs=VM,out_shape=f32(n*p,128),name="ag_"+axis)(coord(axis)[None],own,*rec)
def allreduce(buf, order=('core','y','x')):
    cur=buf
    msgs=first_split(cur,order[0])
    for a,b in zip(order,order[1:]+(None,)):
        r=send(msgs,a)
        cur,msgs=rs_step(cur,r,a,b)
    r=[lax.ppermute(cur,"rows",shift('z',k)) for k in range(1,8)]
    cur=sum_all(cur,r)
    p=cur.shape[0]-EX
    ex=cur[p:]
    own=cur[:p]
    for a in order[::-1]:
        own=gather(own,own.shape[0],a)
    return own,ex


def mm(a,b): return jnp.dot(a,b,precision=hi)
def linv(l):
    return lax.linalg.triangular_solve(l, jnp.eye(l.shape[0],dtype=l.dtype), left_side=True, lower=True)
def filt(proj):
    n=proj.shape[0]
    bound=jnp.max(jnp.sum(jnp.abs(proj),axis=1))
    s=jnp.eye(n,dtype=proj.dtype)-proj/bound
    f=s[:,:128]
    f=mm(s,f); f=mm(s,f)
    return f
def asm(m0,m1,m2,n0,n1,r):
    return jnp.concatenate([jnp.concatenate([m0,m1,n0],1),jnp.concatenate([m1,m2,n1],1),jnp.concatenate([n0.T,n1.T,r],1)],0)
def sym(a): return 0.5*(a+a.T)
def dense(M,Nn,R):
    G=asm(M[0],M[1],M[2],Nn[0],Nn[1],R[0])
    A=[asm(M[k],M[k+1],M[k+2],Nn[k],Nn[k+1],R[k]) for k in (1,2,3)]
    Li=linv(jnp.linalg.cholesky(G))
    proj=sym(mm(mm(Li,A[0]),Li.T))
    F=filt(proj)
    F2=F.at[:128].set(0)
    cq=mm(Li.T,jnp.concatenate([F,F2],1))
    c=cq[:,:128]
    pf=mm(proj,jnp.concatenate([F,F2],1))
    FtF=mm(F.T,F); QQ=mm(F[128:].T,F[128:])
    cAc=mm(F.T,pf[:,:128]); cAq=mm(F.T,pf[:,128:]); qAq=mm(F2.T,pf[:,128:])
    a2=mm(A[1],cq); cA2=mm(c.T,a2); cA2c=cA2[:,:128]; cA2q=cA2[:,128:]
    cA3c=mm(c.T,mm(A[2],c))
    GU=asm(FtF,sym(cAc),sym(cA2c),QQ,cAq,QQ)
    AU=asm(sym(cAc),sym(cA2c),sym(cA3c),cAq,cA2q,sym(qAq))
    Ci=linv(jnp.linalg.cholesky(GU))
    proj2=sym(mm(mm(Ci,AU),Ci.T))
    F=filt(proj2)
    l2=linv(jnp.linalg.cholesky(mm(F.T,F)))
    Y=mm(F,l2.T)
    Y2=Y.at[:128].set(0)
    k=mm(Ci.T,jnp.concatenate([Y,Y2],1))
    kB=mm(cq,jnp.concatenate([k[:128],k[256:]],0))
    kH=mm(c,k[128:256])
    K=jnp.concatenate([kB[:128],kB[128:256]+kH[:128],kH[128:256],kB[256:],kH[256:]],0)
    return K


def next_to(block, distance):
    return lax.ppermute(block, "rows", [(i, (i + distance) % N) for i in range(N)])


def ein(a, b, c):
    return jnp.einsum(a, b, c, precision=hi)


def apply_rows(sym_rows, a1, a2, vec):
    n = sym_rows.shape[0]
    w = jnp.concatenate([jnp.swapaxes(a2[:n], 1, 2), jnp.swapaxes(a1[1:n + 1], 1, 2), sym_rows, a1[2:n + 2], a2[2:n + 2]], axis=2)
    v = jnp.concatenate([vec[k:k + n] for k in range(5)], axis=1)
    return ein("bpq,bqc->bpc", w, v)


def flat_dot(a, b):
    return jnp.dot(a.reshape(-1, a.shape[-1]).T, b.reshape(-1, b.shape[-1]), precision=hi)


def body(start_states, start_steps, onsite, couplings, columns):
    local = onsite.shape[0]
    first_row = lax.axis_index("rows") * local
    ahead = jnp.mod(columns - first_row - jnp.arange(local, dtype=jnp.int32)[:, None], local * N)
    a1, a2 = [ein("bj,bjpq->bpq", (ahead == d).astype(jnp.float32), couplings) for d in (1, 2)]
    s = onsite + jnp.swapaxes(onsite, 1, 2)
    xp = jnp.concatenate([start_states, start_steps], axis=1).reshape(local, BLK, 2 * STATES)
    before = next_to(xp[-4:], 1)
    after = next_to(xp[:6], -1)
    mats = jnp.concatenate([a1, a2, s], axis=2)
    mats_before = next_to(mats[-4:], 1)
    mats_after = next_to(mats[:4], -1)
    v0 = jnp.concatenate([before, xp, after], axis=0)
    m = jnp.concatenate([mats_before, mats, mats_after], axis=0)
    a1, a2, s = m[:, :, :64], m[:, :, 64:128], m[:, :, 128:]
    v1 = apply_rows(s[2:24], a1[2 - 2:24], a2[0:24], v0)
    v2 = apply_rows(s[4:22], a1[2:22], a2[2:22], v1)
    u0, u1, u2 = xp, v1[2:18], v2[:16]
    half = 0.5 * ein("bpq,bqc->bpc", s[4:20], v2[:16, :, :128]) + ein("bpq,bqc->bpc", a1[4:20], v2[1:17, :, :128]) \
        + ein("bpq,bqc->bpc", a2[4:20], v2[2:18, :, :128])
    t = [flat_dot(u0, u0), flat_dot(u0, u1), flat_dot(u1, u1), flat_dot(u1, u2), flat_dot(u2[:, :, :128], u2)]
    m5 = flat_dot(u2[:, :, :128], half)
    mk = [b[:128, :128] for b in t] + [m5 + m5.T]
    nk = [b[:128, 128:] for b in t]
    rk = [b[128:, 128:] for b in t[:4]]
    upper = jnp.triu(jnp.ones((128, 128), jnp.bool_))
    pairs = list(zip(mk[:4], rk)) + [(mk[4], mk[5])]
    packed = [jnp.where(upper, p, q.T) for p, q in pairs]
    diags = jnp.stack([jnp.diagonal(q) for _, q in pairs] + [jnp.zeros((128,), jnp.float32)] * 3)
    total, ex = allreduce(jnp.concatenate(packed + nk + [diags], axis=0))
    mk, rk = [], []
    eye = jnp.eye(128, dtype=jnp.bool_)
    for i in range(5):
        b = total[128 * i:128 * i + 128]
        mk.append(jnp.where(upper, b, b.T))
        low = jnp.where(upper, b.T, b)
        rk.append(jnp.where(eye, jnp.broadcast_to(ex[i][None], (128, 128)), low))
    mk.append(rk.pop())
    nk = [total[640 + 128 * i:768 + 128 * i] for i in range(5)]
    coefs = dense(mk, nk, rk)
    vecs = jnp.concatenate([start_states, u1[:, :, :128].reshape(-1, 128), u2[:, :, :128].reshape(-1, 128), start_steps,
                            u1[:, :, 128:].reshape(-1, 128)], axis=1)
    out = jnp.dot(vecs, coefs, precision=hi)
    return out[:, :128], out[:, 128:]


def solution(mesh):
    in_specs = (
        P("rows", None),
        P("rows", None),
        P("rows", None, None),
        P("rows", None, None, None),
        P("rows", None),
    )
    out_specs = (P("rows", None), P("rows", None))
    return jax.shard_map(body, mesh=mesh, in_specs=in_specs, out_specs=out_specs, check_vma=False)
```

```python
import jax
import jax.numpy as jnp
from jax import lax
from jax.sharding import PartitionSpec as P
from jax.experimental import pallas as pl
from jax.experimental.pallas import tpu as pltpu

N = 256

def parts(a, n):
    out = []
    for i in range(n):
        h = a.astype(jnp.bfloat16)
        out.append(h)
        if i < n - 1:
            a = a - h.astype(jnp.float32)
    return out

TERMS = {1: [(0, 0)], 2: [(0, 0), (0, 1), (1, 0)], 3: [(0, 0), (0, 1), (1, 0), (1, 1), (0, 2), (2, 0)]}

def dot(a, b, n=3, ca=1, cb=0):
    a = a if isinstance(a, list) else parts(a, n)
    b = b if isinstance(b, list) else parts(b, n)
    lhs = [a[i] for i, _ in TERMS[n]]
    rhs = [b[j] for _, j in TERMS[n]]
    lhs = lhs[0] if n == 1 else jnp.concatenate(lhs, axis=ca)
    rhs = rhs[0] if n == 1 else jnp.concatenate(rhs, axis=cb)
    return lax.dot_general(lhs, rhs, (((ca,), (cb,)), ((), ())), preferred_element_type=jnp.float32)

def iotas(n, m):
    return lax.broadcasted_iota(jnp.int32, (n, m), 0), lax.broadcasted_iota(jnp.int32, (n, m), 1)

def newton_factor(g, bad):
    row, col = iotas(128, 128)
    diag = row == col
    weight = jnp.where(row > col, 1.0, jnp.where(diag, 0.5, 0.0))
    dg = jnp.where(diag, g, 0.0)
    dr = lax.rsqrt(jnp.sum(dg, axis=0, keepdims=True))
    dc = lax.rsqrt(jnp.sum(dg, axis=1, keepdims=True))
    one = jnp.where(diag, 1.0, 0.0)
    g = g * dr * dc
    gp = parts(g, 3)
    z = one - weight * (g - one)
    zp = parts(z, 2)
    e = dot(dot(zp, gp[:2], 2), zp, 2, 1, 1) - one
    z = z - dot(weight * e, z, 1)
    zp = parts(z, 3)
    e = dot(dot(zp, gp, 3), zp, 3, 1, 1) - one
    z = z - dot(weight * e, z, 1)
    return z * dr, jnp.maximum(bad, jnp.sum(e * e, axis=0, keepdims=True))

def direct_factor(g, bad, a_ref, z_ref):
    row, col = iotas(128, 128)
    a_ref[...] = g
    z_ref[...] = jnp.where(row == col, 1.0, 0.0)
    def step(j, _):
        r = a_ref[pl.ds(j, 1), :]
        zr = z_ref[pl.ds(j, 1), :]
        a = a_ref[...]
        c = jnp.sum(jnp.where(col == j, a, 0.0), axis=1, keepdims=True)
        d = jnp.sum(jnp.where(col[:1] == j, r, 0.0), axis=1, keepdims=True)
        f = jnp.where(row[:, :1] > j, c / d, 0.0)
        a_ref[...] = a - f * r
        z_ref[...] = z_ref[...] - f * zr
        return 0
    lax.fori_loop(0, 128, step, 0)
    d = jnp.sum(jnp.where(row == col, a_ref[...], 0.0), axis=1, keepdims=True)
    return z_ref[...] / jnp.sqrt(d), bad

def cat(blocks):
    return jnp.concatenate([jnp.concatenate(r, axis=1) for r in blocks], axis=0)

def block_inverse(g, factor, bad):
    w1, bad = factor(g[0][0], bad)
    w1p = parts(w1, 3)
    l = dot(jnp.concatenate([g[1][0], g[2][0]], axis=0), w1p, 3, 1, 1)
    lp = parts(l, 3)
    p = dot(lp, lp, 3, 1, 1)
    w2, bad = factor(g[1][1] - p[:128, :128], bad)
    w2p = parts(w2, 3)
    l32 = dot(g[2][1] - p[128:, :128], w2p, 3, 1, 1)
    l32p = parts(l32, 3)
    w3, bad = factor(g[2][2] - p[128:, 128:] - dot(l32p, l32p, 3, 1, 1), bad)
    m = dot(lp, w1p)
    a21 = -dot(w2p, m[:128])
    t = m[128:] + dot(l32p, a21)
    s = dot(l32p, w2p)
    low = dot(w3, jnp.concatenate([t, s], axis=1))
    zero = jnp.zeros((128, 128), jnp.float32)
    return cat([[w1, zero, zero], [a21, w2, zero], [-low[:, :128], -low[:, 128:], w3]]), bad

def projected_filter(inv, a):
    ip = parts(inv, 3)
    t = dot(dot(ip, a), ip, 3, 1, 1)
    proj = 0.5 * (t + t.T)
    bound = jnp.max(jnp.sum(jnp.abs(proj), axis=0, keepdims=True), axis=1, keepdims=True)
    row, col = iotas(384, 384)
    s = jnp.where(row == col, 1.0, 0.0) - proj / bound
    sp = parts(s, 3)
    f = dot(sp, [q[:, :128] for q in sp])
    return proj, ip, dot(sp, f)

def sym(a):
    return 0.5 * (a + a.T)

def small(mk, nk, rk, factor, bad):
    def assemble(k):
        return [[mk[k], mk[k + 1], nk[k]], [mk[k + 1], mk[k + 2], nk[k + 1]], [nk[k].T, nk[k + 1].T, rk[k]]]
    inv, bad = block_inverse(assemble(0), factor, bad)
    proj, ip, f = projected_filter(inv, cat(assemble(1)))
    f2 = jnp.concatenate([jnp.zeros((128, 128), jnp.float32), f[128:]], axis=0)
    ff2 = jnp.concatenate([f, f2], axis=1)
    ffp = parts(ff2, 3)
    fp = [q[:, :128] for q in ffp]
    cq = dot(ip, ffp, 3, 0, 0)
    cqp = parts(cq, 3)
    cp = [q[:, :128] for q in cqp]
    gram = dot(ffp, ffp, 3, 0, 0)
    one = dot(ffp, dot(proj, ffp), 3, 0, 0)
    two = dot(cp, dot(cat(assemble(2)), cqp), 3, 0, 0)
    three = dot(cp, dot(cat(assemble(3)), cp), 3, 0, 0)
    ftf, qq = gram[:128, :128], gram[128:, 128:]
    b1, c1q, q1q = one[:128, :128], one[:128, 128:], one[128:, 128:]
    c2c, c2q = sym(two[:, :128]), two[:, 128:]
    b1 = sym(b1)
    gu = [[ftf, None, None], [b1, c2c, None], [qq, c1q.T, qq]]
    au = cat([[b1, c2c, c1q], [c2c, sym(three), c2q], [c1q.T, c2q.T, sym(q1q)]])
    inv, bad = block_inverse(gu, factor, bad)
    _, ip, f = projected_filter(inv, au)
    fp = parts(f, 3)
    w, bad = factor(dot(fp, fp, 3, 0, 0), bad)
    y = dot(fp, w, 3, 1, 1)
    y2 = jnp.concatenate([jnp.zeros((128, 128), jnp.float32), y[128:]], axis=0)
    k = dot(ip, jnp.concatenate([y, y2], axis=1), 3, 0, 0)
    kb = dot(cqp, jnp.concatenate([k[:128], k[256:]], axis=0))
    kh = dot(cp, k[128:256])
    return jnp.concatenate([kb[:128], kb[128:256] + kh[:128], kh[128:256], kb[256:], kh[256:]], axis=0), bad

def unpack(tot, ex):
    row, col = iotas(128, 128)
    mk, nk, rk = [], [], []
    for i in range(5):
        b = tot[128 * i:128 * i + 128]
        bt = b.T
        mk.append(jnp.where(row <= col, b, bt))
        rk.append(jnp.where(row == col, ex[i:i + 1], jnp.where(row <= col, bt, b)))
        nk.append(tot[640 + 128 * i:768 + 128 * i])
    mk.append(rk.pop())
    return mk, nk, rk

def dense_kernel(tot, ex, out, a_ref, z_ref):
    mk, nk, rk = unpack(tot, ex)
    res, bad = small(mk, nk, rk, newton_factor, jnp.zeros((1, 128), jnp.float32))
    out[...] = res
    worst = jnp.sum(bad)
    @pl.when(jnp.logical_not(worst < 1e-6))
    def _():
        mk, nk, rk = unpack(tot, ex)
        out[...] = small(mk, nk, rk, lambda g, b: direct_factor(g, b, a_ref, z_ref), None)[0]

def dense_call(tot, ex):
    vm = pl.BlockSpec(memory_space=pltpu.VMEM)
    return pl.pallas_call(dense_kernel, in_specs=[vm, vm], out_specs=vm, out_shape=jax.ShapeDtypeStruct((640, 256), jnp.float32),
        scratch_shapes=[pltpu.VMEM((128, 128), jnp.float32)] * 2, name="dense",
        compiler_params=pltpu.CompilerParams(vmem_limit_bytes=48 * 2**20))(tot, ex)


VM = pl.BlockSpec(memory_space=pltpu.VMEM)
SM = pl.BlockSpec(memory_space=pltpu.SMEM)

def f32(*shape):
    return jax.ShapeDtypeStruct(shape, jnp.float32)

def bf16(*shape):
    return jax.ShapeDtypeStruct(shape, jnp.bfloat16)

def mats_kernel(total, info, col, onsite, coup, m_ref, prev_ref, next_ref):
    first = info[0]
    def offsets(b):
        a1 = jnp.zeros((64, 64), jnp.float32)
        a2 = jnp.zeros((64, 64), jnp.float32)
        for j in range(4):
            ahead = lax.rem(col[b, j] - (first + b) + total, total)
            c = coup[b, j]
            a1 = a1 + jnp.where(ahead == 1, c, 0.0)
            a2 = a2 + jnp.where(ahead == 2, c, 0.0)
        return a1, a2
    zero = jnp.zeros((64, 64), jnp.float32)
    for p in range(8):
        a1, a2 = offsets(2 * p)
        b1, b2 = offsets(2 * p + 1)
        o0, o1 = onsite[2 * p], onsite[2 * p + 1]
        m_ref[p, 0, 0:64] = jnp.concatenate([a2, zero], axis=1)
        m_ref[p, 0, 64:128] = jnp.concatenate([b1, b2], axis=1)
        m_ref[p, 1, 0:64] = jnp.concatenate([o0 + o0.T, a1], axis=1)
        m_ref[p, 1, 64:128] = jnp.concatenate([a1.T, o1 + o1.T], axis=1)
    for p in range(2):
        for q in range(2):
            prev_ref[2 * p + q] = m_ref[p, q]
    next_ref[0] = m_ref[6, 0]
    next_ref[1] = m_ref[7, 0]
    next_ref[2] = m_ref[7, 1]

def mats_call(first_row, total, columns, onsite, couplings):
    return pl.pallas_call(lambda *a: mats_kernel(total, *a), in_specs=[SM, SM, VM, VM], out_specs=[VM] * 3,
        out_shape=[f32(8, 2, 128, 128), f32(4, 128, 128), f32(3, 128, 128)], name="blocks")(first_row[None], columns, onsite, couplings)

def local_kernel(core, x, p, xb, xa, m, mb, ma, buf, msg, v0h, v0m, v1h, v1m, v2h, v2m, e0h, e0m, e1h, e1m, e2h, e2m):
    def put(h, l, at, val):
        a, b = parts(val, 2)
        h[at * 128:at * 128 + 128] = a
        l[at * 128:at * 128 + 128] = b
    for i in range(2):
        put(e0h, e0m, i, jnp.concatenate([xb[128 * i:128 * i + 128], xb[256 + 128 * i:384 + 128 * i]], axis=1))
    for i in range(8):
        put(e0h, e0m, i + 2, jnp.concatenate([x[128 * i:128 * i + 128], p[128 * i:128 * i + 128]], axis=1))
    for i in range(3):
        put(e0h, e0m, i + 10, jnp.concatenate([xa[128 * i:128 * i + 128], xa[384 + 128 * i:512 + 128 * i]], axis=1))
    def mat(i, q):
        if i < 0:
            return mb[i + 2] if q == 0 else mb[2]
        return m[i, q] if i < 8 else ma[2 * (i - 8) + q]
    us = {i: parts(mat(i, 0), 2) for i in range(-2, 10)}
    ds = {i: parts(mat(i, 1), 2) for i in range(-1, 10)}
    ut = {i: [a.T for a in us[i]] for i in range(-2, 9)}
    def band(i):
        return [jnp.concatenate([ut[i - 1][k], ds[i][k], us[i][k]], axis=1) for k in range(2)]
    bands = {i: band(i) for i in range(-1, 10)}
    for i in range(-1, 10):
        s = slice((i + 1) * 128, (i + 4) * 128)
        put(e1h, e1m, i + 1, dot(bands[i], [e0h[s], e0m[s]], 2))
    for i in range(9):
        s = slice(i * 128, (i + 3) * 128)
        put(e2h, e2m, i, dot(bands[i], [e1h[s], e1m[s]], 2))
    v0h[...], v0m[...] = e0h[256:1280], e0m[256:1280]
    v1h[...], v1m[...] = e1h[128:1152], e1m[128:1152]
    v2h[...], v2m[...] = e2h[0:1024, 0:128], e2m[0:1024, 0:128]
    half = []
    for i in range(8):
        s = slice(i * 128, (i + 2) * 128)
        b = [jnp.concatenate([ds[i][k] * jnp.bfloat16(0.5), us[i][k]], axis=1) for k in range(2)]
        half.append(dot(b, [e2h[s, 0:128], e2m[s, 0:128]], 2))
    half = parts(jnp.concatenate(half, axis=0), 2)
    w0 = [v0h[...], v0m[...]]
    w1 = [v1h[...], v1m[...]]
    w2 = [e2h[0:1024], e2m[0:1024]]
    w2x = [v2h[...], v2m[...]]
    t = [dot(a, b, 2, 0, 0) for a, b in ((w0, w0), (w0, w1), (w1, w1), (w1, w2), (w2x, w2))]
    m5 = dot(w2x, half, 2, 0, 0)
    m5 = m5 + m5.T
    row, col = iotas(128, 128)
    pairs = [(b[:128, :128], b[128:, 128:]) for b in t[:4]] + [(t[4][:, :128], m5)]
    ex = []
    for i, (a, b) in enumerate(pairs):
        buf[128 * i:128 * i + 128] = jnp.where(row <= col, a, b)
        buf[640 + 128 * i:768 + 128 * i] = t[i][:128, 128:]
        ex.append(jnp.sum(jnp.where(row == col, b, 0.0), axis=0, keepdims=True))
    buf[1280:1288] = jnp.concatenate(ex + [jnp.zeros((3, 128), jnp.float32)], axis=0)
    other = pl.multiple_of((1 - core[0]) * 640, 128)
    msg[0:640] = buf[pl.ds(other, 640)]
    msg[640:648] = buf[1280:1288]

def local_call(core, x, p, xb, xa, m, mb, ma):
    return pl.pallas_call(local_kernel, in_specs=[SM] + [VM] * 7, out_specs=[VM] * 8,
        out_shape=[f32(1288, 128), f32(648, 128), bf16(1024, 256), bf16(1024, 256), bf16(1024, 256), bf16(1024, 256),
                   bf16(1024, 128), bf16(1024, 128)],
        scratch_shapes=[pltpu.VMEM((n * 128, 256), jnp.bfloat16) for n in (13, 13, 11, 11, 9, 9)], name="moments",
        compiler_params=pltpu.CompilerParams(vmem_limit_bytes=48 * 2**20))(core[None], x, p, xb, xa, m, mb, ma)

def final_kernel(k, v0h, v0m, v1h, v1m, v2h, v2m, states, steps):
    kk = parts(jnp.concatenate([k[0:128], k[384:512], k[128:256], k[512:640], k[256:384]], axis=0), 2)
    for i in range(4):
        s = slice(256 * i, 256 * i + 256)
        v = [jnp.concatenate([a[s], b[s], c[s]], axis=1) for a, b, c in ((v0h, v1h, v2h), (v0m, v1m, v2m))]
        out = dot(v, kk, 2)
        states[s] = out[:, :128]
        steps[s] = out[:, 128:]

def final_call(k, *v):
    return pl.pallas_call(final_kernel, in_specs=[VM] * 7, out_specs=[VM] * 2, out_shape=[f32(1024, 128), f32(1024, 128)],
        name="combine", compiler_params=pltpu.CompilerParams(vmem_limit_bytes=48 * 2**20))(k, *v)


STRIDE={'core':1,'z':2,'x':16,'y':64}; SIZE={'core':2,'z':8,'x':4,'y':4}
def shift(axis,k):
    s,n=STRIDE[axis],SIZE[axis]
    out=[]
    for i in range(N):
        c=(i//s)%n
        out.append((i, i+((c+k)%n-c)*s))
    return out
def coord(axis):
    return (lax.axis_index("rows")//STRIDE[axis])%SIZE[axis]
VM=pl.BlockSpec(memory_space=pltpu.VMEM)
SM=pl.BlockSpec(memory_space=pltpu.SMEM)
def f32(*s): return jax.ShapeDtypeStruct(s,jnp.float32)
EX=8
def split_kernel(n,p, co, cur, *msgs):
    c=co[0]
    for k in range(1,n):
        q=lax.rem(c+k,n)
        msgs[k-1][0:p]=cur[pl.ds(pl.multiple_of(q*p,8),p)]
        msgs[k-1][p:p+EX]=cur[n*p:n*p+EX]
def first_split(cur, axis):
    n=SIZE[axis]; p=(cur.shape[0]-EX)//n
    return pl.pallas_call(lambda *a: split_kernel(n,p,*a), in_specs=[SM,VM], out_specs=[VM]*(n-1),
        out_shape=[f32(p+EX,128)]*(n-1), name="split_"+axis)(coord(axis)[None],cur)
def rs_step(cur, msgs, axis, nxt):
    n=SIZE[axis]; p=(cur.shape[0]-EX)//n
    n2=SIZE[nxt] if nxt else 1
    p2=p//n2
    def kern(co,cur_ref,*rest):
        ins=rest[:n-1]; new=rest[n-1]; out=rest[n:]
        c=co[0]
        acc=cur_ref[pl.ds(pl.multiple_of(c*p,8),p)]
        ex=cur_ref[n*p:n*p+EX]
        for r in ins:
            acc=acc+r[0:p]; ex=ex+r[p:p+EX]
        new[0:p]=acc; new[p:p+EX]=ex
        if nxt: split_kernel(n2,p2,co.at[1:2],new,*out)
    co=jnp.stack([coord(axis),coord(nxt) if nxt else coord(axis)])
    res=pl.pallas_call(kern,in_specs=[SM]+[VM]*n,out_specs=[VM]*n2,
        out_shape=[f32(p+EX,128)]+[f32(p2+EX,128)]*(n2-1), name="rs_"+axis)(co,cur,*msgs)
    return res[0],res[1:]
def sum_all(cur,msgs):
    def kern(a,*rest):
        acc=a[...]
        for r in rest[:-1]: acc=acc+r[...]
        rest[-1][...]=acc
    return pl.pallas_call(kern,in_specs=[VM]*(1+len(msgs)),out_specs=VM,out_shape=f32(*cur.shape),name="sum_all")(cur,*msgs)
def send(msgs,axis):
    return [lax.ppermute(m,"rows",shift(axis,k+1)) for k,m in enumerate(msgs)]
def gather(own,p,axis):
    n=SIZE[axis]
    rec=[lax.ppermute(own,"rows",shift(axis,k)) for k in range(1,n)]
    def kern(co,o,*rest):
        c=co[0]; out=rest[-1]
        out[pl.ds(pl.multiple_of(c*p,8),p)]=o[0:p]
        for k in range(1,n):
            q=lax.rem(c-k+n,n)
            out[pl.ds(pl.multiple_of(q*p,8),p)]=rest[k-1][0:p]
    return pl.pallas_call(kern,in_specs=[SM]+[VM]*n,out_specs=VM,out_shape=f32(n*p,128),name="ag_"+axis)(coord(axis)[None],own,*rec)
def allreduce(buf, order=('core','y','x')):
    return allreduce_from(buf, first_split(buf,order[0]), order)
def allreduce_from(cur, msgs, order=('core','y','x')):
    for a,b in zip(order,order[1:]+(None,)):
        r=send(msgs,a)
        cur,msgs=rs_step(cur,r,a,b)
    r=[lax.ppermute(cur,"rows",shift('z',k)) for k in range(1,8)]
    cur=sum_all(cur,r)
    p=cur.shape[0]-EX
    ex=cur[p:]
    own=cur[:p]
    for a in order[::-1]:
        own=gather(own,own.shape[0],a)
    return own,ex


def next_to(block, distance):
    return lax.ppermute(block, "rows", [(i, (i + distance) % N) for i in range(N)])
def body(start_states, start_steps, onsite, couplings, columns):
    local = onsite.shape[0]
    me = lax.axis_index("rows")
    x, p = start_states, start_steps
    xa = next_to(jnp.concatenate([x[:384], p[:384]], axis=0), -1)
    xb = next_to(jnp.concatenate([x[768:], p[768:]], axis=0), 1)
    m, to_prev, to_next = mats_call(me * local, local * N, columns, onsite, couplings)
    ma = next_to(to_prev, -1)
    mb = next_to(to_next, 1)
    buf, msg, *vecs = local_call(me % 2, x, p, xb, xa, m, mb, ma)
    total, ex = allreduce_from(buf, [msg])
    return tuple(final_call(dense_call(total, ex), *vecs))
def solution(mesh):
    in_specs = (P("rows", None), P("rows", None), P("rows", None, None), P("rows", None, None, None), P("rows", None))
    out_specs = (P("rows", None), P("rows", None))
    return jax.shard_map(body, mesh=mesh, in_specs=in_specs, out_specs=out_specs, check_vma=False)
```

```python
import jax
import jax.numpy as jnp
from jax import lax
from jax.sharding import PartitionSpec as P
from jax.experimental import pallas as pl
from jax.experimental.pallas import tpu as pltpu

N = 256

def parts(a, n):
    out = []
    for i in range(n):
        h = a.astype(jnp.bfloat16)
        out.append(h)
        if i < n - 1:
            a = a - h.astype(jnp.float32)
    return out

TERMS = {1: [(0, 0)], 2: [(0, 0), (0, 1), (1, 0)], 3: [(0, 0), (0, 1), (1, 0), (1, 1), (0, 2), (2, 0)]}

def dot(a, b, n=3, ca=1, cb=0):
    a = a if isinstance(a, list) else parts(a, n)
    b = b if isinstance(b, list) else parts(b, n)
    lhs = [a[i] for i, _ in TERMS[n]]
    rhs = [b[j] for _, j in TERMS[n]]
    lhs = lhs[0] if n == 1 else jnp.concatenate(lhs, axis=ca)
    rhs = rhs[0] if n == 1 else jnp.concatenate(rhs, axis=cb)
    return lax.dot_general(lhs, rhs, (((ca,), (cb,)), ((), ())), preferred_element_type=jnp.float32)

def iotas(n, m):
    return lax.broadcasted_iota(jnp.int32, (n, m), 0), lax.broadcasted_iota(jnp.int32, (n, m), 1)

def newton_factor(g, bad):
    row, col = iotas(128, 128)
    diag = row == col
    weight = jnp.where(row > col, 1.0, jnp.where(diag, 0.5, 0.0))
    dg = jnp.where(diag, g, 0.0)
    dr = lax.rsqrt(jnp.sum(dg, axis=0, keepdims=True))
    dc = lax.rsqrt(jnp.sum(dg, axis=1, keepdims=True))
    one = jnp.where(diag, 1.0, 0.0)
    g = g * dr * dc
    gp = parts(g, 3)
    z = one - weight * (g - one)
    zp = parts(z, 2)
    e = dot(dot(zp, gp[:2], 2), zp, 2, 1, 1) - one
    z = z - dot(weight * e, z, 1)
    zp = parts(z, 3)
    e = dot(dot(zp, gp, 3), zp, 3, 1, 1) - one
    z = z - dot(weight * e, z, 1)
    return z * dr, jnp.maximum(bad, jnp.sum(e * e, axis=0, keepdims=True))

def direct_factor(g, bad, a_ref, z_ref):
    row, col = iotas(128, 128)
    a_ref[...] = g
    z_ref[...] = jnp.where(row == col, 1.0, 0.0)
    def step(j, _):
        r = a_ref[pl.ds(j, 1), :]
        zr = z_ref[pl.ds(j, 1), :]
        a = a_ref[...]
        c = jnp.sum(jnp.where(col == j, a, 0.0), axis=1, keepdims=True)
        d = jnp.sum(jnp.where(col[:1] == j, r, 0.0), axis=1, keepdims=True)
        f = jnp.where(row[:, :1] > j, c / d, 0.0)
        a_ref[...] = a - f * r
        z_ref[...] = z_ref[...] - f * zr
        return 0
    lax.fori_loop(0, 128, step, 0)
    d = jnp.sum(jnp.where(row == col, a_ref[...], 0.0), axis=1, keepdims=True)
    return z_ref[...] / jnp.sqrt(d), bad

def cat(blocks):
    return jnp.concatenate([jnp.concatenate(r, axis=1) for r in blocks], axis=0)

def block_inverse(g, factor, bad):
    w1, bad = factor(g[0][0], bad)
    w1p = parts(w1, 3)
    l = dot(jnp.concatenate([g[1][0], g[2][0]], axis=0), w1p, 3, 1, 1)
    lp = parts(l, 3)
    p = dot(lp, lp, 3, 1, 1)
    w2, bad = factor(g[1][1] - p[:128, :128], bad)
    w2p = parts(w2, 3)
    l32 = dot(g[2][1] - p[128:, :128], w2p, 3, 1, 1)
    l32p = parts(l32, 3)
    w3, bad = factor(g[2][2] - p[128:, 128:] - dot(l32p, l32p, 3, 1, 1), bad)
    m = dot(lp, w1p)
    a21 = -dot(w2p, m[:128])
    t = m[128:] + dot(l32p, a21)
    s = dot(l32p, w2p)
    low = dot(w3, jnp.concatenate([t, s], axis=1))
    zero = jnp.zeros((128, 128), jnp.float32)
    return cat([[w1, zero, zero], [a21, w2, zero], [-low[:, :128], -low[:, 128:], w3]]), bad

def projected_filter(inv, a):
    ip = parts(inv, 3)
    t = dot(dot(ip, a), ip, 3, 1, 1)
    proj = 0.5 * (t + t.T)
    bound = jnp.max(jnp.sum(jnp.abs(proj), axis=0, keepdims=True), axis=1, keepdims=True)
    row, col = iotas(384, 384)
    s = jnp.where(row == col, 1.0, 0.0) - proj / bound
    sp = parts(s, 3)
    f = dot(sp, [q[:, :128] for q in sp])
    return proj, ip, dot(sp, f)

def sym(a):
    return 0.5 * (a + a.T)

def small(mk, nk, rk, factor, bad):
    def assemble(k):
        return [[mk[k], mk[k + 1], nk[k]], [mk[k + 1], mk[k + 2], nk[k + 1]], [nk[k].T, nk[k + 1].T, rk[k]]]
    inv, bad = block_inverse(assemble(0), factor, bad)
    proj, ip, f = projected_filter(inv, cat(assemble(1)))
    f2 = jnp.concatenate([jnp.zeros((128, 128), jnp.float32), f[128:]], axis=0)
    ff2 = jnp.concatenate([f, f2], axis=1)
    ffp = parts(ff2, 3)
    fp = [q[:, :128] for q in ffp]
    cq = dot(ip, ffp, 3, 0, 0)
    cqp = parts(cq, 3)
    cp = [q[:, :128] for q in cqp]
    gram = dot(ffp, ffp, 3, 0, 0)
    one = dot(ffp, dot(proj, ffp), 3, 0, 0)
    two = dot(cp, dot(cat(assemble(2)), cqp), 3, 0, 0)
    three = dot(cp, dot(cat(assemble(3)), cp), 3, 0, 0)
    ftf, qq = gram[:128, :128], gram[128:, 128:]
    b1, c1q, q1q = one[:128, :128], one[:128, 128:], one[128:, 128:]
    c2c, c2q = sym(two[:, :128]), two[:, 128:]
    b1 = sym(b1)
    gu = [[ftf, None, None], [b1, c2c, None], [qq, c1q.T, qq]]
    au = cat([[b1, c2c, c1q], [c2c, sym(three), c2q], [c1q.T, c2q.T, sym(q1q)]])
    inv, bad = block_inverse(gu, factor, bad)
    _, ip, f = projected_filter(inv, au)
    fp = parts(f, 3)
    w, bad = factor(dot(fp, fp, 3, 0, 0), bad)
    y = dot(fp, w, 3, 1, 1)
    y2 = jnp.concatenate([jnp.zeros((128, 128), jnp.float32), y[128:]], axis=0)
    k = dot(ip, jnp.concatenate([y, y2], axis=1), 3, 0, 0)
    kb = dot(cqp, jnp.concatenate([k[:128], k[256:]], axis=0))
    kh = dot(cp, k[128:256])
    return jnp.concatenate([kb[:128], kb[128:256] + kh[:128], kh[128:256], kb[256:], kh[256:]], axis=0), bad

def unpack(mine, other):
    row, col = iotas(128, 128)
    first = lax.rem(lax.axis_index("rows"), 2) == 0
    ex = mine[pl.ds(5, 8, stride=8)]
    mk, nk, rk = [], [], []
    for i in range(5):
        a, c = mine[pl.ds(i, 128, stride=8)], other[pl.ds(i, 128, stride=8)]
        b = jnp.where(first, a, c)
        nk.append(jnp.where(first, c, a))
        bt = b.T
        mk.append(jnp.where(row <= col, b, bt))
        rk.append(jnp.where(row == col, ex[i:i + 1], jnp.where(row <= col, bt, b)))
    mk.append(rk.pop())
    return mk, nk, rk

def dense_kernel(mine, other, out, a_ref, z_ref):
    res, bad = small(*unpack(mine, other), newton_factor, jnp.zeros((1, 128), jnp.float32))
    out[...] = res
    worst = jnp.sum(bad)
    @pl.when(jnp.logical_not(worst < 1e-6))
    def _():
        out[...] = small(*unpack(mine, other), lambda g, b: direct_factor(g, b, a_ref, z_ref), None)[0]

def dense_call(mine, other):
    vm = pl.BlockSpec(memory_space=pltpu.VMEM)
    return pl.pallas_call(dense_kernel, in_specs=[vm, vm], out_specs=vm, out_shape=jax.ShapeDtypeStruct((640, 256), jnp.float32),
        scratch_shapes=[pltpu.VMEM((128, 128), jnp.float32)] * 2, name="dense",
        compiler_params=pltpu.CompilerParams(vmem_limit_bytes=24 * 2**20))(mine, other)


VM = pl.BlockSpec(memory_space=pltpu.VMEM)
SM = pl.BlockSpec(memory_space=pltpu.SMEM)

def f32(*shape):
    return jax.ShapeDtypeStruct(shape, jnp.float32)

def bf16(*shape):
    return jax.ShapeDtypeStruct(shape, jnp.bfloat16)

ANY = pl.BlockSpec(memory_space=pl.ANY)
DMA = pltpu.SemaphoreType.DMA


def halo_kernel(x, p, prev_ref, next_ref, sem):
    copies = [pltpu.make_async_copy(src, dst, sem.at[i]) for i, (src, dst) in enumerate((
        (x.at[0:384], prev_ref.at[0:384]), (p.at[0:384], prev_ref.at[384:768]),
        (x.at[768:1024], next_ref.at[0:256]), (p.at[768:1024], next_ref.at[256:512])))]
    for c in copies:
        c.start()
    for c in copies:
        c.wait()


def halo_call(x, p):
    return pl.pallas_call(halo_kernel, in_specs=[ANY] * 2, out_specs=[ANY] * 2, out_shape=[f32(768, 128), f32(512, 128)],
        scratch_shapes=[DMA((4,))], name="halo",
        compiler_params=pltpu.CompilerParams(vmem_limit_bytes=60 * 2**20))(x, p)


def mats_kernel(total, col, onsite, coup, m_ref, prev_ref, next_ref):
    first = lax.axis_index("rows") * 16
    ahead = lax.rem(col[...] - (first + lax.broadcasted_iota(jnp.int32, (4, 16), 1)) + total, total)
    one = jnp.where(ahead == 1, 1.0, 0.0)
    two = jnp.where(ahead == 2, 1.0, 0.0)
    def offsets(b):
        a1 = jnp.zeros((64, 64), jnp.float32)
        a2 = jnp.zeros((64, 64), jnp.float32)
        for j in range(4):
            c = coup[b, j]
            a1 = a1 + one[j:j + 1, b:b + 1] * c
            a2 = a2 + two[j:j + 1, b:b + 1] * c
        return a1, a2
    zero = jnp.zeros((64, 64), jnp.float32)
    for p in range(8):
        a1, a2 = offsets(2 * p)
        b1, b2 = offsets(2 * p + 1)
        o0, o1 = onsite[2 * p], onsite[2 * p + 1]
        m_ref[p, 0, 0:64] = jnp.concatenate([a2, zero], axis=1)
        m_ref[p, 0, 64:128] = jnp.concatenate([b1, b2], axis=1)
        m_ref[p, 1, 0:64] = jnp.concatenate([o0 + o0.T, a1], axis=1)
        m_ref[p, 1, 64:128] = jnp.concatenate([a1.T, o1 + o1.T], axis=1)
    for p in range(2):
        for q in range(2):
            prev_ref[2 * p + q] = m_ref[p, q]
    next_ref[0] = m_ref[6, 0]
    next_ref[1] = m_ref[7, 0]
    next_ref[2] = m_ref[7, 1]


def mats_call(total, columns, onsite, couplings):
    return pl.pallas_call(lambda *a: mats_kernel(total, *a), in_specs=[VM] * 3, out_specs=[VM] * 3,
        out_shape=[f32(8, 2, 128, 128), f32(4, 128, 128), f32(3, 128, 128)], name="blocks",
        compiler_params=pltpu.CompilerParams(vmem_limit_bytes=60 * 2**20))(columns.T, onsite, couplings)


def local_kernel(*refs):
    hbm, outs, keep = refs[:7], refs[7:9], refs[9:15]
    x, p, xb, xa, m, mb, ma = refs[15:22]
    v0h, v0m, v1h, v1m, v2h, v2m = refs[22:28]
    e0h, e0m, e1h, e1m, e2h, e2m, sem, out_sem = refs[28:36]
    fetch = [pltpu.make_async_copy(a, b, sem.at[i]) for i, (a, b) in enumerate(zip(hbm, refs[15:22]))]
    for c in fetch:
        c.start()
    store = [pltpu.make_async_copy(a, b, out_sem.at[i]) for i, (a, b) in enumerate(zip(refs[22:28], keep))]
    def put(h, l, at, val):
        a, b = parts(val, 2)
        h[at * 128:at * 128 + 128] = a
        l[at * 128:at * 128 + 128] = b
    fetch[0].wait()
    fetch[1].wait()
    for i in range(8):
        put(e0h, e0m, i + 2, jnp.concatenate([x[128 * i:128 * i + 128], p[128 * i:128 * i + 128]], axis=1))
    v0h[...], v0m[...] = e0h[256:1280], e0m[256:1280]
    store[0].start()
    store[1].start()
    for c in fetch[2:]:
        c.wait()
    for i in range(2):
        put(e0h, e0m, i, jnp.concatenate([xb[128 * i:128 * i + 128], xb[256 + 128 * i:384 + 128 * i]], axis=1))
    for i in range(3):
        put(e0h, e0m, i + 10, jnp.concatenate([xa[128 * i:128 * i + 128], xa[384 + 128 * i:512 + 128 * i]], axis=1))
    def mat(i, q):
        if i < 0:
            return mb[i + 2] if q == 0 else mb[2]
        return m[i, q] if i < 8 else ma[2 * (i - 8) + q]
    us = {i: parts(mat(i, 0), 2) for i in range(-2, 10)}
    ds = {i: parts(mat(i, 1), 2) for i in range(-1, 10)}
    ut = {i: [a.T for a in us[i]] for i in range(-2, 9)}
    def band(i):
        return [jnp.concatenate([ut[i - 1][k], ds[i][k], us[i][k]], axis=1) for k in range(2)]
    bands = {i: band(i) for i in range(-1, 10)}
    for i in range(-1, 10):
        s = slice((i + 1) * 128, (i + 4) * 128)
        put(e1h, e1m, i + 1, dot(bands[i], [e0h[s], e0m[s]], 2))
    for i in range(9):
        s = slice(i * 128, (i + 3) * 128)
        put(e2h, e2m, i, dot(bands[i], [e1h[s], e1m[s]], 2))
    v1h[...], v1m[...] = e1h[128:1152], e1m[128:1152]
    v2h[...], v2m[...] = e2h[0:1024, 0:128], e2m[0:1024, 0:128]
    for c in store[2:]:
        c.start()
    half = []
    for i in range(8):
        s = slice(i * 128, (i + 2) * 128)
        b = [jnp.concatenate([ds[i][k] * jnp.bfloat16(0.5), us[i][k]], axis=1) for k in range(2)]
        half.append(dot(b, [e2h[s, 0:128], e2m[s, 0:128]], 2))
    half = parts(jnp.concatenate(half, axis=0), 2)
    w0 = [v0h[...], v0m[...]]
    w1 = [v1h[...], v1m[...]]
    w2 = [e2h[0:1024], e2m[0:1024]]
    w2x = [v2h[...], v2m[...]]
    t = [dot(a, b, 2, 0, 0) for a, b in ((w0, w0), (w0, w1), (w1, w1), (w1, w2), (w2x, w2))]
    m5 = dot(w2x, half, 2, 0, 0)
    m5 = m5 + m5.T
    row, col = iotas(128, 128)
    pairs = [(b[:128, :128], b[128:, 128:]) for b in t[:4]] + [(t[4][:, :128], m5)]
    ex = [jnp.sum(jnp.where(row == col, b, 0.0), axis=0, keepdims=True) for _, b in pairs]
    ex = jnp.concatenate(ex + [jnp.zeros((123, 128), jnp.float32)], axis=0)
    zero = jnp.zeros((128, 128), jnp.float32)
    first = lax.rem(lax.axis_index("rows"), 2) == 0
    own, msg = outs
    for i, (a, b) in enumerate(pairs):
        c = jnp.where(row <= col, a, b)
        d = t[i][:128, 128:]
        own[pl.ds(i, 128, stride=8)] = jnp.where(first, c, d)
        msg[pl.ds(i, 128, stride=8)] = jnp.where(first, d, c)
    for ref in outs:
        ref[pl.ds(5, 128, stride=8)] = ex
        ref[pl.ds(6, 128, stride=8)] = zero
        ref[pl.ds(7, 128, stride=8)] = zero
    for c in store:
        c.wait()


def local_call(x, p, xb, xa, m, mb, ma):
    args = (x, p, xb, xa, m, mb, ma)
    keep = [(1024, 256)] * 4 + [(1024, 128)] * 2
    return pl.pallas_call(local_kernel, in_specs=[ANY] * 7, out_specs=[VM] * 2 + [ANY] * 6,
        out_shape=[f32(1024, 128)] * 2 + [bf16(*k) for k in keep],
        scratch_shapes=[pltpu.VMEM(a.shape, jnp.float32) for a in args] + [pltpu.VMEM(k, jnp.bfloat16) for k in keep]
        + [pltpu.VMEM((n * 128, 256), jnp.bfloat16) for n in (13, 13, 11, 11, 9, 9)] + [DMA((7,)), DMA((6,))], name="moments",
        compiler_params=pltpu.CompilerParams(vmem_limit_bytes=24 * 2**20))(*args)


def spread_kernel(a, out):
    out[...] = jnp.broadcast_to(jnp.sum(a[...], axis=0, keepdims=True), (128, 8, 128))


def spread_call(a):
    return pl.pallas_call(spread_kernel, in_specs=[VM], out_specs=VM, out_shape=f32(128, 8, 128), name="spread")(a)


def final_kernel(k, v0h, v0m, v1h, v1m, v2h, v2m, states, steps):
    kk = parts(jnp.concatenate([k[0:128], k[384:512], k[128:256], k[512:640], k[256:384]], axis=0), 2)
    for i in range(4):
        s = slice(256 * i, 256 * i + 256)
        v = [jnp.concatenate([a[s], b[s], c[s]], axis=1) for a, b, c in ((v0h, v1h, v2h), (v0m, v1m, v2m))]
        out = dot(v, kk, 2)
        states[s] = out[:, :128]
        steps[s] = out[:, 128:]

def final_call(k, *v):
    return pl.pallas_call(final_kernel, in_specs=[VM] * 7, out_specs=[VM] * 2, out_shape=[f32(1024, 128), f32(1024, 128)],
        name="combine", compiler_params=pltpu.CompilerParams(vmem_limit_bytes=24 * 2**20))(k, *v)


def next_to(block, distance):
    return lax.ppermute(block, "rows", [(i, (i + distance) % N) for i in range(N)])
def across_chip(block):
    return lax.ppermute(block, "rows", [(i, i ^ 1) for i in range(N)])
def same_core(block):
    return lax.all_to_all(block, "rows", 0, 0, axis_index_groups=[list(range(c, N, 2)) for c in range(2)])
def reduce_all(own, msg):
    own = (own + across_chip(msg)).reshape(128, 8, 128)
    own = same_core(spread_call(same_core(own))).reshape(1024, 128)
    return own, across_chip(own)
def body(start_states, start_steps, onsite, couplings, columns):
    local = onsite.shape[0]
    x, p = start_states, start_steps
    to_prev, to_next = halo_call(x, p)
    xa = next_to(to_prev, -1)
    xb = next_to(to_next, 1)
    m, to_prev, to_next = mats_call(local * N, columns, onsite, couplings)
    ma = next_to(to_prev, -1)
    mb = next_to(to_next, 1)
    own, msg, *vecs = local_call(x, p, xb, xa, m, mb, ma)
    mine, other = reduce_all(own, msg)
    return tuple(final_call(dense_call(mine, other), *vecs))
def solution(mesh):
    in_specs = (P("rows", None), P("rows", None), P("rows", None, None), P("rows", None, None, None), P("rows", None))
    out_specs = (P("rows", None), P("rows", None))
    return jax.shard_map(body, mesh=mesh, in_specs=in_specs, out_specs=out_specs, check_vma=False)
```

```python
import jax
import jax.numpy as jnp
from jax import lax
from jax.sharding import PartitionSpec as P
from jax.experimental import pallas as pl
from jax.experimental.pallas import tpu as pltpu

N = 256

def parts(a, n):
    out = []
    for i in range(n):
        h = a.astype(jnp.bfloat16)
        out.append(h)
        if i < n - 1:
            a = a - h.astype(jnp.float32)
    return out

TERMS = {1: [(0, 0)], 2: [(0, 0), (0, 1), (1, 0)], 3: [(0, 0), (0, 1), (1, 0), (1, 1), (0, 2), (2, 0)]}

def dot(a, b, n=2, ca=1, cb=0):
    a = a if isinstance(a, list) else parts(a, n)
    b = b if isinstance(b, list) else parts(b, n)
    lhs = [a[i] for i, _ in TERMS[n]]
    rhs = [b[j] for _, j in TERMS[n]]
    lhs = lhs[0] if n == 1 else jnp.concatenate(lhs, axis=ca)
    rhs = rhs[0] if n == 1 else jnp.concatenate(rhs, axis=cb)
    return lax.dot_general(lhs, rhs, (((ca,), (cb,)), ((), ())), preferred_element_type=jnp.float32)

def iotas(n, m):
    return lax.broadcasted_iota(jnp.int32, (n, m), 0), lax.broadcasted_iota(jnp.int32, (n, m), 1)

def newton_factor(g, bad):
    row, col = iotas(128, 128)
    diag = row == col
    weight = jnp.where(row > col, 1.0, jnp.where(diag, 0.5, 0.0))
    dg = jnp.where(diag, g, 0.0)
    dr = lax.rsqrt(jnp.sum(dg, axis=0, keepdims=True))
    dc = lax.rsqrt(jnp.sum(dg, axis=1, keepdims=True))
    one = jnp.where(diag, 1.0, 0.0)
    g = g * dr * dc
    gp = parts(g, 3)
    z = one - weight * (g - one)
    zp = parts(z, 2)
    e = dot(dot(zp, gp[:2], 2), zp, 2, 1, 1) - one
    z = z - dot(weight * e, z, 1)
    zp = parts(z, 3)
    e = dot(dot(zp, gp[:2], 2), zp, 2, 1, 1) - one
    z = z - dot(weight * e, z, 1)
    return z * dr, jnp.maximum(bad, jnp.sum(e * e, axis=0, keepdims=True))

def direct_factor(g, bad, a_ref, z_ref):
    row, col = iotas(128, 128)
    a_ref[...] = g
    z_ref[...] = jnp.where(row == col, 1.0, 0.0)
    def step(j, _):
        r = a_ref[pl.ds(j, 1), :]
        zr = z_ref[pl.ds(j, 1), :]
        a = a_ref[...]
        c = jnp.sum(jnp.where(col == j, a, 0.0), axis=1, keepdims=True)
        d = jnp.sum(jnp.where(col[:1] == j, r, 0.0), axis=1, keepdims=True)
        f = jnp.where(row[:, :1] > j, c / d, 0.0)
        a_ref[...] = a - f * r
        z_ref[...] = z_ref[...] - f * zr
        return 0
    lax.fori_loop(0, 128, step, 0)
    d = jnp.sum(jnp.where(row == col, a_ref[...], 0.0), axis=1, keepdims=True)
    return z_ref[...] / jnp.sqrt(d), bad

def cat(blocks):
    return jnp.concatenate([jnp.concatenate(r, axis=1) for r in blocks], axis=0)

def block_inverse(g, factor, bad):
    w1, bad = factor(g[0][0], bad)
    w1p = parts(w1, 3)
    l = dot(jnp.concatenate([g[1][0], g[2][0]], axis=0), w1p, 3, 1, 1)
    lp = parts(l, 3)
    p = dot(lp, lp, 3, 1, 1)
    w2, bad = factor(g[1][1] - p[:128, :128], bad)
    w2p = parts(w2, 3)
    l32 = dot(g[2][1] - p[128:, :128], w2p, 3, 1, 1)
    l32p = parts(l32, 3)
    w3, bad = factor(g[2][2] - p[128:, 128:] - dot(l32p, l32p, 3, 1, 1), bad)
    m = dot(lp, w1p)
    a21 = -dot(w2p, m[:128])
    t = m[128:] + dot(l32p, a21)
    s = dot(l32p, w2p)
    low = dot(w3, jnp.concatenate([t, s], axis=1))
    zero = jnp.zeros((128, 128), jnp.float32)
    return cat([[w1, zero, zero], [a21, w2, zero], [-low[:, :128], -low[:, 128:], w3]]), bad

def projected_filter(inv, a):
    ip = parts(inv, 3)
    t = dot(dot(ip, a), ip, 2, 1, 1)
    proj = 0.5 * (t + t.T)
    bound = jnp.max(jnp.sum(jnp.abs(proj), axis=0, keepdims=True), axis=1, keepdims=True)
    row, col = iotas(384, 384)
    s = jnp.where(row == col, 1.0, 0.0) - proj / bound
    sp = parts(s, 3)
    f = dot(sp, [q[:, :128] for q in sp])
    return proj, ip, dot(sp, f)

def sym(a):
    return 0.5 * (a + a.T)

def small(mk, nk, rk, factor, bad):
    def assemble(k):
        return [[mk[k], mk[k + 1], nk[k]], [mk[k + 1], mk[k + 2], nk[k + 1]], [nk[k].T, nk[k + 1].T, rk[k]]]
    inv, bad = block_inverse(assemble(0), factor, bad)
    proj, ip, f = projected_filter(inv, cat(assemble(1)))
    f2 = jnp.concatenate([jnp.zeros((128, 128), jnp.float32), f[128:]], axis=0)
    ff2 = jnp.concatenate([f, f2], axis=1)
    ffp = parts(ff2, 3)
    fp = [q[:, :128] for q in ffp]
    cq = dot(ip, ffp, 3, 0, 0)
    cqp = parts(cq, 3)
    cp = [q[:, :128] for q in cqp]
    gram = dot(ffp, ffp, 3, 0, 0)
    one = dot(ffp, dot(proj, ffp), 3, 0, 0)
    two = dot(cp, dot(cat(assemble(2)), cqp), 3, 0, 0)
    three = dot(cp, dot(cat(assemble(3)), cp), 3, 0, 0)
    ftf, qq = gram[:128, :128], gram[128:, 128:]
    b1, c1q, q1q = one[:128, :128], one[:128, 128:], one[128:, 128:]
    c2c, c2q = sym(two[:, :128]), two[:, 128:]
    b1 = sym(b1)
    gu = [[ftf, None, None], [b1, c2c, None], [qq, c1q.T, qq]]
    au = cat([[b1, c2c, c1q], [c2c, sym(three), c2q], [c1q.T, c2q.T, sym(q1q)]])
    inv, bad = block_inverse(gu, factor, bad)
    _, ip, f = projected_filter(inv, au)
    fp = parts(f, 3)
    w, bad = factor(dot(fp, fp, 3, 0, 0), bad)
    y = dot(fp, w, 2, 1, 1)
    y2 = jnp.concatenate([jnp.zeros((128, 128), jnp.float32), y[128:]], axis=0)
    k = dot(ip, jnp.concatenate([y, y2], axis=1), 2, 0, 0)
    kb = dot(cqp, jnp.concatenate([k[:128], k[256:]], axis=0))
    kh = dot(cp, k[128:256])
    return jnp.concatenate([kb[:128], kb[128:256] + kh[:128], kh[128:256], kb[256:], kh[256:]], axis=0), bad

def unpack(mine, other):
    row, col = iotas(128, 128)
    first = lax.rem(lax.axis_index("rows"), 2) == 0
    ex = mine[pl.ds(5, 8, stride=8)]
    mk, nk, rk = [], [], []
    for i in range(5):
        a, c = mine[pl.ds(i, 128, stride=8)], other[pl.ds(i, 128, stride=8)]
        b = jnp.where(first, a, c)
        nk.append(jnp.where(first, c, a))
        bt = b.T
        mk.append(jnp.where(row <= col, b, bt))
        rk.append(jnp.where(row == col, ex[i:i + 1], jnp.where(row <= col, bt, b)))
    mk.append(rk.pop())
    return mk, nk, rk

def dense_kernel(mine, other, out, a_ref, z_ref):
    res, bad = small(*unpack(mine, other), newton_factor, jnp.zeros((1, 128), jnp.float32))
    out[...] = res
    worst = jnp.sum(bad)
    @pl.when(jnp.logical_not(worst < 1e-6))
    def _():
        out[...] = small(*unpack(mine, other), lambda g, b: direct_factor(g, b, a_ref, z_ref), None)[0]

def dense_call(mine, other):
    vm = pl.BlockSpec(memory_space=pltpu.VMEM)
    return pl.pallas_call(dense_kernel, in_specs=[vm, vm], out_specs=vm, out_shape=jax.ShapeDtypeStruct((640, 256), jnp.float32),
        scratch_shapes=[pltpu.VMEM((128, 128), jnp.float32)] * 2, name="dense",
        compiler_params=pltpu.CompilerParams(vmem_limit_bytes=24 * 2**20))(mine, other)


VM = pl.BlockSpec(memory_space=pltpu.VMEM)
SM = pl.BlockSpec(memory_space=pltpu.SMEM)

def f32(*shape):
    return jax.ShapeDtypeStruct(shape, jnp.float32)

def bf16(*shape):
    return jax.ShapeDtypeStruct(shape, jnp.bfloat16)

ANY = pl.BlockSpec(memory_space=pl.ANY)
DMA = pltpu.SemaphoreType.DMA


def mats_kernel(total, col, onsite, coup, x, p, m_ref, a_ref, b_ref, sem):
    me = lax.axis_index("rows")
    first = me * 16
    odd = lax.rem(me, 2)
    copies = []
    for ref, at in ((a_ref, 1 - odd), (b_ref, odd)):
        for k, v in enumerate((x, p)):
            copies.append(pltpu.make_async_copy(v.at[pl.ds(pl.multiple_of(at * 640, 128), 384)], ref.at[384 * k:384 * k + 384],
                                                sem.at[len(copies)]))
    for c in copies:
        c.start()
    ahead = lax.rem(col[...] - (first + lax.broadcasted_iota(jnp.int32, (4, 16), 1)) + total, total)
    one = jnp.where(ahead == 1, 1.0, 0.0)
    two = jnp.where(ahead == 2, 1.0, 0.0)
    def offsets(b):
        a1 = jnp.zeros((64, 64), jnp.float32)
        a2 = jnp.zeros((64, 64), jnp.float32)
        for j in range(4):
            c = coup[b, j]
            a1 = a1 + one[j:j + 1, b:b + 1] * c
            a2 = a2 + two[j:j + 1, b:b + 1] * c
        return a1, a2
    zero = jnp.zeros((64, 64), jnp.float32)
    for i in range(8):
        a1, a2 = offsets(2 * i)
        b1, b2 = offsets(2 * i + 1)
        o0, o1 = onsite[2 * i], onsite[2 * i + 1]
        m_ref[i, 0, 0:64] = jnp.concatenate([a2, zero], axis=1)
        m_ref[i, 0, 64:128] = jnp.concatenate([b1, b2], axis=1)
        m_ref[i, 1, 0:64] = jnp.concatenate([o0 + o0.T, a1], axis=1)
        m_ref[i, 1, 64:128] = jnp.concatenate([a1.T, o1 + o1.T], axis=1)
    for ref, at in ((a_ref, 1 - odd), (b_ref, odd)):
        for i in range(2):
            for j in range(2):
                k = 768 + 128 * (2 * i + j)
                ref[k:k + 128] = m_ref[at * 6 + i, j]
    for c in copies:
        c.wait()


def mats_call(total, columns, onsite, couplings, x, p):
    return pl.pallas_call(lambda *a: mats_kernel(total, *a), in_specs=[VM] * 3 + [ANY] * 2, out_specs=[VM] * 3,
        out_shape=[f32(8, 2, 128, 128), f32(1280, 128), f32(1280, 128)], scratch_shapes=[DMA((4,))], name="blocks",
        compiler_params=pltpu.CompilerParams(vmem_limit_bytes=60 * 2**20))(columns.T, onsite, couplings, x, p)


def local_kernel(*refs):
    hbm, outs, keep = refs[:5], refs[5:7], refs[7:13]
    x, p, m, r = refs[13:17]
    v0h, v0m, v1h, v1m, v2h, v2m = refs[17:23]
    e0h, e0m, e1h, e1m, e2h, e2m, sem, out_sem = refs[23:31]
    odd = lax.rem(lax.axis_index("rows"), 2)
    fetch = [pltpu.make_async_copy(a, b, sem.at[i]) for i, (a, b) in enumerate(zip(hbm, (x, p, m, r.at[0], r.at[1])))]
    for c in fetch:
        c.start()
    store = [pltpu.make_async_copy(a, b, out_sem.at[i]) for i, (a, b) in enumerate(zip(refs[17:23], keep))]
    def put(h, l, at, val):
        a, b = parts(val, 2)
        h[at * 128:at * 128 + 128] = a
        l[at * 128:at * 128 + 128] = b
    fetch[0].wait()
    fetch[1].wait()
    for i in range(8):
        put(e0h, e0m, i + 2, jnp.concatenate([x[128 * i:128 * i + 128], p[128 * i:128 * i + 128]], axis=1))
    v0h[...], v0m[...] = e0h[256:1280], e0m[256:1280]
    store[0].start()
    store[1].start()
    for c in fetch[2:]:
        c.wait()
    for i in range(2):
        put(e0h, e0m, i, jnp.concatenate([r[1 - odd, 128 + 128 * i:256 + 128 * i], r[1 - odd, 512 + 128 * i:640 + 128 * i]], axis=1))
    for i in range(3):
        put(e0h, e0m, i + 10, jnp.concatenate([r[odd, 128 * i:128 * i + 128], r[odd, 384 + 128 * i:512 + 128 * i]], axis=1))
    def mat(i, q):
        if 0 <= i < 8:
            return m[i, q]
        k = 768 + 128 * (2 * (i % 8 % 6) + q)
        return r[1 - odd if i < 0 else odd, k:k + 128]
    us = {i: parts(mat(i, 0), 2) for i in range(-2, 10)}
    ds = {i: parts(mat(i, 1), 2) for i in range(-1, 10)}
    ut = {i: [a.T for a in us[i]] for i in range(-2, 9)}
    def band(i):
        return [jnp.concatenate([ut[i - 1][k], ds[i][k], us[i][k]], axis=1) for k in range(2)]
    bands = {i: band(i) for i in range(-1, 10)}
    for i in range(-1, 10):
        s = slice((i + 1) * 128, (i + 4) * 128)
        put(e1h, e1m, i + 1, dot(bands[i], [e0h[s], e0m[s]], 2))
    for i in range(9):
        s = slice(i * 128, (i + 3) * 128)
        put(e2h, e2m, i, dot(bands[i], [e1h[s], e1m[s]], 2))
    v1h[...], v1m[...] = e1h[128:1152], e1m[128:1152]
    v2h[...], v2m[...] = e2h[0:1024, 0:128], e2m[0:1024, 0:128]
    for c in store[2:]:
        c.start()
    half = []
    for i in range(8):
        s = slice(i * 128, (i + 2) * 128)
        b = [jnp.concatenate([ds[i][k] * jnp.bfloat16(0.5), us[i][k]], axis=1) for k in range(2)]
        half.append(dot(b, [e2h[s, 0:128], e2m[s, 0:128]], 2))
    half = parts(jnp.concatenate(half, axis=0), 2)
    w0 = [v0h[...], v0m[...]]
    w1 = [v1h[...], v1m[...]]
    w2 = [e2h[0:1024], e2m[0:1024]]
    w2x = [v2h[...], v2m[...]]
    t = [dot(a, b, 2, 0, 0) for a, b in ((w0, w0), (w0, w1), (w1, w1), (w1, w2), (w2x, w2))]
    m5 = dot(w2x, half, 2, 0, 0)
    m5 = m5 + m5.T
    row, col = iotas(128, 128)
    pairs = [(b[:128, :128], b[128:, 128:]) for b in t[:4]] + [(t[4][:, :128], m5)]
    ex = [jnp.sum(jnp.where(row == col, b, 0.0), axis=0, keepdims=True) for _, b in pairs]
    ex = jnp.concatenate(ex + [jnp.zeros((123, 128), jnp.float32)], axis=0)
    zero = jnp.zeros((128, 128), jnp.float32)
    first = odd == 0
    own, msg = outs
    for i, (a, b) in enumerate(pairs):
        c = jnp.where(row <= col, a, b)
        d = t[i][:128, 128:]
        own[pl.ds(i, 128, stride=8)] = jnp.where(first, c, d)
        msg[pl.ds(i, 128, stride=8)] = jnp.where(first, d, c)
    for ref in outs:
        ref[pl.ds(5, 128, stride=8)] = ex
        ref[pl.ds(6, 128, stride=8)] = zero
        ref[pl.ds(7, 128, stride=8)] = zero
    for c in store:
        c.wait()


def local_call(x, p, m, a, b):
    args = (x, p, m, a, b)
    keep = [(1024, 256)] * 4 + [(1024, 128)] * 2
    return pl.pallas_call(local_kernel, in_specs=[ANY] * 5, out_specs=[VM] * 2 + [ANY] * 6,
        out_shape=[f32(1024, 128)] * 2 + [bf16(*k) for k in keep],
        scratch_shapes=[pltpu.VMEM(k, jnp.float32) for k in (x.shape, p.shape, m.shape, (2, 1280, 128))] + [pltpu.VMEM(k, jnp.bfloat16) for k in keep]
        + [pltpu.VMEM((n * 128, 256), jnp.bfloat16) for n in (13, 13, 11, 11, 9, 9)] + [DMA((5,)), DMA((6,))], name="moments",
        compiler_params=pltpu.CompilerParams(vmem_limit_bytes=24 * 2**20))(*args)


def spread_kernel(a, out):
    out[...] = jnp.broadcast_to(jnp.sum(a[...], axis=0, keepdims=True), (128, 8, 128))


def spread_call(a):
    return pl.pallas_call(spread_kernel, in_specs=[VM], out_specs=VM, out_shape=f32(128, 8, 128), name="spread")(a)


def final_kernel(k, v0h, v0m, v1h, v1m, v2h, v2m, states, steps):
    kk = parts(jnp.concatenate([k[0:128], k[384:512], k[128:256], k[512:640], k[256:384]], axis=0), 2)
    for i in range(4):
        s = slice(256 * i, 256 * i + 256)
        v = [jnp.concatenate([a[s], b[s], c[s]], axis=1) for a, b, c in ((v0h, v1h, v2h), (v0m, v1m, v2m))]
        out = dot(v, kk, 2)
        states[s] = out[:, :128]
        steps[s] = out[:, 128:]

def final_call(k, *v):
    return pl.pallas_call(final_kernel, in_specs=[VM] * 7, out_specs=[VM] * 2, out_shape=[f32(1024, 128), f32(1024, 128)],
        name="combine", compiler_params=pltpu.CompilerParams(vmem_limit_bytes=24 * 2**20))(k, *v)


def next_chip(block):
    return lax.ppermute(block, "rows", [(i, (i + 1) % N if i % 2 else (i - 1) % N) for i in range(N)])
def across_chip(block):
    return lax.ppermute(block, "rows", [(i, i ^ 1) for i in range(N)])
def same_core(block):
    return lax.all_to_all(block, "rows", 0, 0, axis_index_groups=[list(range(c, N, 2)) for c in range(2)])
def reduce_all(own, msg):
    own = (own + across_chip(msg)).reshape(128, 8, 128)
    own = same_core(spread_call(same_core(own))).reshape(1024, 128)
    return own, across_chip(own)
def body(start_states, start_steps, onsite, couplings, columns):
    local = onsite.shape[0]
    x, p = start_states, start_steps
    m, to_core, to_chip = mats_call(local * N, columns, onsite, couplings, x, p)
    from_chip = next_chip(to_chip)
    from_core = across_chip(to_core)
    own, msg, *vecs = local_call(x, p, m, from_core, from_chip)
    mine, other = reduce_all(own, msg)
    return tuple(final_call(dense_call(mine, other), *vecs))
def solution(mesh):
    in_specs = (P("rows", None), P("rows", None), P("rows", None, None), P("rows", None, None, None), P("rows", None))
    out_specs = (P("rows", None), P("rows", None))
    return jax.shard_map(body, mesh=mesh, in_specs=in_specs, out_specs=out_specs, check_vma=False)
```

```python
import jax
import jax.numpy as jnp
from jax import lax
from jax.sharding import PartitionSpec as P
from jax.experimental import pallas as pl
from jax.experimental.pallas import tpu as pltpu

N = 256

def parts(a, n):
    out = []
    for i in range(n):
        h = a.astype(jnp.bfloat16)
        out.append(h)
        if i < n - 1:
            a = a - h.astype(jnp.float32)
    return out

TERMS = {1: [(0, 0)], 2: [(0, 0), (0, 1), (1, 0)], 3: [(0, 0), (0, 1), (1, 0), (1, 1), (0, 2), (2, 0)]}

def dot(a, b, n=2, ca=1, cb=0):
    a = a if isinstance(a, list) else parts(a, n)
    b = b if isinstance(b, list) else parts(b, n)
    lhs = [a[i] for i, _ in TERMS[n]]
    rhs = [b[j] for _, j in TERMS[n]]
    lhs = lhs[0] if n == 1 else jnp.concatenate(lhs, axis=ca)
    rhs = rhs[0] if n == 1 else jnp.concatenate(rhs, axis=cb)
    return lax.dot_general(lhs, rhs, (((ca,), (cb,)), ((), ())), preferred_element_type=jnp.float32)

def iotas(n, m):
    return lax.broadcasted_iota(jnp.int32, (n, m), 0), lax.broadcasted_iota(jnp.int32, (n, m), 1)

def newton_factor(g, bad):
    row, col = iotas(128, 128)
    diag = row == col
    weight = jnp.where(row > col, 1.0, jnp.where(diag, 0.5, 0.0))
    dg = jnp.where(diag, g, 0.0)
    dr = lax.rsqrt(jnp.sum(dg, axis=0, keepdims=True))
    dc = lax.rsqrt(jnp.sum(dg, axis=1, keepdims=True))
    one = jnp.where(diag, 1.0, 0.0)
    g = g * dr * dc
    gp = parts(g, 3)
    z = one - weight * (g - one)
    zp = parts(z, 2)
    e = dot(dot(zp, gp[:2], 2), zp, 2, 1, 1) - one
    z = z - dot(weight * e, z, 1)
    zp = parts(z, 3)
    e = dot(dot(zp, gp[:2], 2), zp, 2, 1, 1) - one
    z = z - dot(weight * e, z, 1)
    return z * dr, jnp.maximum(bad, jnp.sum(e * e, axis=0, keepdims=True))

def direct_factor(g, bad, a_ref, z_ref):
    row, col = iotas(128, 128)
    a_ref[...] = g
    z_ref[...] = jnp.where(row == col, 1.0, 0.0)
    def step(j, _):
        r = a_ref[pl.ds(j, 1), :]
        zr = z_ref[pl.ds(j, 1), :]
        a = a_ref[...]
        c = jnp.sum(jnp.where(col == j, a, 0.0), axis=1, keepdims=True)
        d = jnp.sum(jnp.where(col[:1] == j, r, 0.0), axis=1, keepdims=True)
        f = jnp.where(row[:, :1] > j, c / d, 0.0)
        a_ref[...] = a - f * r
        z_ref[...] = z_ref[...] - f * zr
        return 0
    lax.fori_loop(0, 128, step, 0)
    d = jnp.sum(jnp.where(row == col, a_ref[...], 0.0), axis=1, keepdims=True)
    return z_ref[...] / jnp.sqrt(d), bad

def cat(blocks):
    return jnp.concatenate([jnp.concatenate(r, axis=1) for r in blocks], axis=0)

def block_inverse(g, factor, bad):
    w1, bad = factor(g[0][0], bad)
    w1p = parts(w1, 3)
    l = dot(jnp.concatenate([g[1][0], g[2][0]], axis=0), w1p, 3, 1, 1)
    lp = parts(l, 3)
    p = dot(lp, lp, 3, 1, 1)
    w2, bad = factor(g[1][1] - p[:128, :128], bad)
    w2p = parts(w2, 3)
    l32 = dot(g[2][1] - p[128:, :128], w2p, 3, 1, 1)
    l32p = parts(l32, 3)
    w3, bad = factor(g[2][2] - p[128:, 128:] - dot(l32p, l32p, 3, 1, 1), bad)
    m = dot(lp, w1p)
    a21 = -dot(w2p, m[:128])
    t = m[128:] + dot(l32p, a21)
    s = dot(l32p, w2p)
    low = dot(w3, jnp.concatenate([t, s], axis=1))
    zero = jnp.zeros((128, 128), jnp.float32)
    return cat([[w1, zero, zero], [a21, w2, zero], [-low[:, :128], -low[:, 128:], w3]]), bad

def projected_filter(inv, a):
    ip = parts(inv, 3)
    t = dot(dot(ip, a), ip, 2, 1, 1)
    proj = 0.5 * (t + t.T)
    bound = jnp.max(jnp.sum(jnp.abs(proj), axis=0, keepdims=True), axis=1, keepdims=True)
    row, col = iotas(384, 384)
    s = jnp.where(row == col, 1.0, 0.0) - proj / bound
    sp = parts(s, 3)
    f = dot(sp, [q[:, :128] for q in sp])
    return proj, ip, dot(sp, f)

def sym(a):
    return 0.5 * (a + a.T)

def small(mk, nk, rk, factor, bad):
    def assemble(k):
        return [[mk[k], mk[k + 1], nk[k]], [mk[k + 1], mk[k + 2], nk[k + 1]], [nk[k].T, nk[k + 1].T, rk[k]]]
    inv, bad = block_inverse(assemble(0), factor, bad)
    proj, ip, f = projected_filter(inv, cat(assemble(1)))
    f2 = jnp.concatenate([jnp.zeros((128, 128), jnp.float32), f[128:]], axis=0)
    ff2 = jnp.concatenate([f, f2], axis=1)
    ffp = parts(ff2, 3)
    fp = [q[:, :128] for q in ffp]
    cq = dot(ip, ffp, 3, 0, 0)
    cqp = parts(cq, 3)
    cp = [q[:, :128] for q in cqp]
    gram = dot(ffp, ffp, 3, 0, 0)
    one = dot(ffp, dot(proj, ffp), 3, 0, 0)
    two = dot(cp, dot(cat(assemble(2)), cqp), 3, 0, 0)
    three = dot(cp, dot(cat(assemble(3)), cp), 3, 0, 0)
    ftf, qq = gram[:128, :128], gram[128:, 128:]
    b1, c1q, q1q = one[:128, :128], one[:128, 128:], one[128:, 128:]
    c2c, c2q = sym(two[:, :128]), two[:, 128:]
    b1 = sym(b1)
    gu = [[ftf, None, None], [b1, c2c, None], [qq, c1q.T, qq]]
    au = cat([[b1, c2c, c1q], [c2c, sym(three), c2q], [c1q.T, c2q.T, sym(q1q)]])
    inv, bad = block_inverse(gu, factor, bad)
    _, ip, f = projected_filter(inv, au)
    fp = parts(f, 3)
    w, bad = factor(dot(fp, fp, 3, 0, 0), bad)
    y = dot(fp, w, 2, 1, 1)
    y2 = jnp.concatenate([jnp.zeros((128, 128), jnp.float32), y[128:]], axis=0)
    k = dot(ip, jnp.concatenate([y, y2], axis=1), 2, 0, 0)
    kb = dot(cqp, jnp.concatenate([k[:128], k[256:]], axis=0))
    kh = dot(cp, k[128:256])
    return jnp.concatenate([kb[:128], kb[128:256] + kh[:128], kh[128:256], kb[256:], kh[256:]], axis=0), bad

def unpack(mine, other):
    row, col = iotas(128, 128)
    even = lax.rem(lax.axis_index("rows"), 2) == 0
    ex = mine[0, 40:48]
    mk, nk, rk = [], [], []
    for i in range(5):
        a, c = [q[:, 8 * i:8 * i + 8].reshape(128, 128) for q in (mine, other)]
        b = jnp.where(even, a, c)
        nk.append(jnp.where(even, c, a))
        bt = b.T
        mk.append(jnp.where(row <= col, b, bt))
        rk.append(jnp.where(row == col, ex[i:i + 1], jnp.where(row <= col, bt, b)))
    mk.append(rk.pop())
    return mk, nk, rk

def dense_kernel(*refs):
    mine, other = refs[:2]
    kept = refs[2:12]
    states, steps = refs[12:14]
    k_ref, a_ref, z_ref, out_ref = refs[14:18]
    v0h, v0m, v1h, v1m, v2h, v2m, f1h, f1m, f2h, f2m = refs[18:28]
    sem, out_sem = refs[28:30]
    fetch = [pltpu.make_async_copy(a, b, sem.at[i]) for i, (a, b) in enumerate(zip(kept, refs[18:28]))]
    for c in fetch:
        c.start()
    res, bad = small(*unpack(mine, other), newton_factor, jnp.zeros((1, 128), jnp.float32))
    k_ref[...] = res
    worst = jnp.sum(bad)
    @pl.when(jnp.logical_not(worst < 1e-6))
    def _():
        k_ref[...] = small(*unpack(mine, other), lambda g, b: direct_factor(g, b, a_ref, z_ref), None)[0]
    kk = parts(jnp.concatenate([k_ref[0:128], k_ref[384:512], k_ref[128:256], k_ref[512:640], k_ref[256:384]], axis=0), 2)
    for c in fetch:
        c.wait()
    def rows(at):
        return slice(128 * at, 128 * at + 128)
    def pair(i, v0, v1, v2, f1, f2):
        one = v1[rows(i - 1)] if 1 <= i <= 6 else f1[rows(i // 7)]
        two = v2[rows(i - 2), 0:128] if 2 <= i <= 5 else f2[rows(i if i < 2 else i - 4)]
        return jnp.concatenate([v0[rows(i)], one, two], axis=1)
    copies = []
    for i in range(4):
        v = [jnp.concatenate([pair(2 * i + j, *q) for j in range(2)], axis=0)
             for q in ((v0h, v1h, v2h, f1h, f2h), (v0m, v1m, v2m, f1m, f2m))]
        out = dot(v, kk, 2)
        for j, ref in enumerate((states, steps)):
            out_ref[j, 256 * i:256 * i + 256] = out[:, 128 * j:128 * j + 128]
            copies.append(pltpu.make_async_copy(out_ref.at[j, 256 * i:256 * i + 256], ref.at[256 * i:256 * i + 256], out_sem.at[len(copies)]))
            copies[-1].start()
    for c in copies:
        c.wait()

def dense_call(mine, other, *kept):
    vm = pl.BlockSpec(memory_space=pltpu.VMEM)
    hbm = pl.BlockSpec(memory_space=pl.ANY)
    square = pltpu.VMEM((128, 128), jnp.float32)
    return pl.pallas_call(dense_kernel, in_specs=[vm] * 2 + [hbm] * 10, out_specs=[hbm] * 2,
        out_shape=[jax.ShapeDtypeStruct((1024, 128), jnp.float32)] * 2,
        scratch_shapes=[pltpu.VMEM((640, 256), jnp.float32), square, square, pltpu.VMEM((2, 1024, 128), jnp.float32)]
        + [pltpu.VMEM(v.shape, v.dtype) for v in kept] + [pltpu.SemaphoreType.DMA((10,)), pltpu.SemaphoreType.DMA((8,))],
        name="dense", compiler_params=pltpu.CompilerParams(vmem_limit_bytes=24 * 2**20))(mine, other, *kept)


VM = pl.BlockSpec(memory_space=pltpu.VMEM)
ANY = pl.BlockSpec(memory_space=pl.ANY)
DMA = pltpu.SemaphoreType.DMA


def f32(*shape):
    return jax.ShapeDtypeStruct(shape, jnp.float32)


def bf16(*shape):
    return jax.ShapeDtypeStruct(shape, jnp.bfloat16)


def params(mib):
    return pltpu.CompilerParams(vmem_limit_bytes=mib * 2**20)


def weights(total, col):
    row = lax.axis_index("rows") * 16 + lax.broadcasted_iota(jnp.int32, (4, 16), 1)
    ahead = lax.rem(col[...] - row + total, total)
    return jnp.where(ahead == 1, 1.0, 0.0), jnp.where(ahead == 2, 1.0, 0.0)


def pair_blocks(one, two, onsite, coup, pair, at):
    def offsets(b, k):
        a1 = jnp.zeros((64, 64), jnp.float32)
        a2 = jnp.zeros((64, 64), jnp.float32)
        for j in range(4):
            c = coup[k, j]
            a1 = a1 + one[j:j + 1, b:b + 1] * c
            a2 = a2 + two[j:j + 1, b:b + 1] * c
        return a1, a2
    a1, a2 = offsets(2 * pair, at)
    b1, b2 = offsets(2 * pair + 1, at + 1)
    o0, o1 = onsite[at], onsite[at + 1]
    u = jnp.concatenate([jnp.concatenate([a2, jnp.zeros((64, 64), jnp.float32)], axis=1), jnp.concatenate([b1, b2], axis=1)], axis=0)
    d = jnp.concatenate([jnp.concatenate([o0 + o0.T, a1], axis=1), jnp.concatenate([a1.T, o1 + o1.T], axis=1)], axis=0)
    return u, d


def edge_kernel(total, col, onsite, coup, x, p, a_ref, b_ref, on_v, co_v, sem):
    odd = lax.rem(lax.axis_index("rows"), 2)
    pairs = [(onsite.at[0:4], on_v.at[0:4]), (onsite.at[12:16], on_v.at[4:8]), (coup.at[0:4], co_v.at[0:4]), (coup.at[12:16], co_v.at[4:8])]
    for ref, at in ((a_ref, 1 - odd), (b_ref, odd)):
        for k, v in enumerate((x, p)):
            pairs.append((v.at[pl.ds(pl.multiple_of(at * 640, 128), 384)], ref.at[384 * k:384 * k + 384]))
    copies = [pltpu.make_async_copy(a, b, sem.at[i]) for i, (a, b) in enumerate(pairs)]
    for c in copies:
        c.start()
    one, two = weights(total, col)
    for c in copies[:4]:
        c.wait()
    even = odd == 0
    for i in range(2):
        first = pair_blocks(one, two, on_v, co_v, i, 2 * i)
        last = pair_blocks(one, two, on_v, co_v, 6 + i, 4 + 2 * i)
        for j in range(2):
            k = 768 + 128 * (2 * i + j)
            a_ref[k:k + 128] = jnp.where(even, last[j], first[j])
            b_ref[k:k + 128] = jnp.where(even, first[j], last[j])
    for c in copies[4:]:
        c.wait()


def edge_call(total, columns, onsite, couplings, x, p):
    return pl.pallas_call(lambda *a: edge_kernel(total, *a), in_specs=[VM] + [ANY] * 4, out_specs=[VM] * 2,
        out_shape=[f32(1280, 128)] * 2,
        scratch_shapes=[pltpu.VMEM((8, 64, 64), jnp.float32), pltpu.VMEM((8, 4, 64, 64), jnp.float32), DMA((8,))], name="edge",
        compiler_params=params(60))(columns, onsite, couplings, x, p)


def put(h, l, at, val):
    a, b = parts(val, 2)
    h[at * 128:at * 128 + 128] = a
    l[at * 128:at * 128 + 128] = b


def band(lower, diag, upper):
    return [jnp.concatenate([lower[k], diag[k], upper[k]], axis=1) for k in range(2)]


def half_product(diag, upper, h, l, at):
    s = slice(at * 128, at * 128 + 256)
    b = [jnp.concatenate([diag[k] * jnp.bfloat16(0.5), upper[k]], axis=1) for k in range(2)]
    return dot(b, [h[s, 0:128], l[s, 0:128]], 2)


def inner_kernel(total, col, onsite, coup, x, p, uh, um, dh, dm, v0h, v0m, v1h, v1m, v2h, v2m, t0, t1, t2, t3, t4, t5):
    one, two = weights(total, col)
    for i in range(8):
        u, d = pair_blocks(one, two, onsite, coup, i, 2 * i)
        uh[i], um[i] = parts(u, 2)
        dh[i], dm[i] = parts(d, 2)
        s = slice(128 * i, 128 * i + 128)
        put(v0h, v0m, i, jnp.concatenate([x[s], p[s]], axis=1))
    us = [[uh[i], um[i]] for i in range(8)]
    ds = [[dh[i], dm[i]] for i in range(8)]
    bands = {i: band([a.T for a in us[i - 1]], ds[i], us[i]) for i in range(1, 7)}
    for i in range(1, 7):
        s = slice((i - 1) * 128, (i + 2) * 128)
        put(v1h, v1m, i - 1, dot(bands[i], [v0h[s], v0m[s]], 2))
    for i in range(2, 6):
        s = slice((i - 2) * 128, (i + 1) * 128)
        put(v2h, v2m, i - 2, dot(bands[i], [v1h[s], v1m[s]], 2))
    w0 = [v0h[...], v0m[...]]
    w0i = [v0h[128:896], v0m[128:896]]
    w1 = [v1h[...], v1m[...]]
    w1i = [v1h[128:640], v1m[128:640]]
    w2 = [v2h[...], v2m[...]]
    w2x = [v2h[:, 0:128], v2m[:, 0:128]]
    t0[...] = dot(w0, w0, 2, 0, 0)
    t1[...] = dot(w0i, w1, 2, 0, 0)
    t2[...] = dot(w1, w1, 2, 0, 0)
    t3[...] = dot(w1i, w2, 2, 0, 0)
    t4[...] = dot(w2x, w2, 2, 0, 0)
    half = jnp.concatenate([half_product(ds[i], us[i], v2h, v2m, i - 2) for i in range(2, 5)], axis=0)
    t5[...] = dot([a[0:384] for a in w2x], half, 2, 0, 0)


def inner_call(total, columns, onsite, couplings, x, p):
    return pl.pallas_call(lambda *a: inner_kernel(total, *a), in_specs=[VM] * 5, out_specs=[VM] * 16,
        out_shape=[bf16(8, 128, 128)] * 4 + [bf16(1024, 256)] * 2 + [bf16(768, 256)] * 2 + [bf16(512, 256)] * 2
        + [f32(256, 256)] * 4 + [f32(128, 256), f32(128, 128)], name="inner",
        compiler_params=params(24))(columns, onsite, couplings, x, p)


def outer_kernel(ra, rb, uh, um, dh, dm, v0h, v0m, v1h, v1m, v2h, v2m, t0, t1, t2, t3, t4, t5, own, msg, f1h, f1m, f2h, f2m,
                 e0h, e0m, e1h, e1m, e2h, e2m):
    odd = lax.rem(lax.axis_index("rows"), 2)
    even = odd == 0
    def before(s):
        return jnp.where(even, rb[s], ra[s])
    def after(s):
        return jnp.where(even, ra[s], rb[s])
    def rows(at, n=1):
        return slice(at * 128, (at + n) * 128)
    for i in range(2):
        put(e0h, e0m, i, jnp.concatenate([before(rows(1 + i)), before(rows(4 + i))], axis=1))
    for i in range(3):
        put(e0h, e0m, i + 8, jnp.concatenate([after(rows(i)), after(rows(3 + i))], axis=1))
    for e, v in ((e0h, v0h), (e0m, v0m)):
        e[rows(2, 3)] = v[rows(0, 3)]
        e[rows(5, 3)] = v[rows(5, 3)]
    us = {i: [uh[i], um[i]] for i in range(8)}
    ds = {i: [dh[i], dm[i]] for i in range(8)}
    us[-2], us[-1] = [parts(before(rows(6 + k)), 2) for k in (0, 2)]
    ds[-1] = parts(before(rows(9)), 2)
    us[8], us[9] = [parts(after(rows(6 + k)), 2) for k in (0, 2)]
    ds[8], ds[9] = [parts(after(rows(7 + k)), 2) for k in (0, 2)]
    bands = {i: band([a.T for a in us[i - 1]], ds[i], us[i]) for i in (-1, 0, 1, 6, 7, 8, 9)}
    for i, at, src in ((-1, 0, 0), (0, 1, 1), (7, 6, 6), (8, 7, 7), (9, 8, 8)):
        s = rows(src, 3)
        put(e1h, e1m, at, dot(bands[i], [e0h[s], e0m[s]], 2))
    for e, v in ((e1h, v1h), (e1m, v1m)):
        e[rows(2, 2)] = v[rows(0, 2)]
        e[rows(4, 2)] = v[rows(4, 2)]
    for i, at, src in ((0, 0, 0), (1, 1, 1), (6, 4, 4), (7, 5, 5), (8, 6, 6)):
        s = rows(src, 3)
        put(e2h, e2m, at, dot(bands[i], [e1h[s], e1m[s]], 2))
    for e, v in ((e2h, v2h), (e2m, v2m)):
        e[rows(2)] = v[rows(0)]
        e[rows(3)] = v[rows(3)]
    def join(a, b, i, n, j, m):
        return [jnp.concatenate([q[rows(i, n)], q[rows(j, m)]], axis=0) for q in (a, b)]
    w0 = join(v0h, v0m, 0, 1, 7, 1)
    w1 = join(e1h, e1m, 1, 1, 6, 1)
    w1w = join(e1h, e1m, 1, 2, 5, 2)
    w2 = join(e2h, e2m, 0, 2, 4, 2)
    w2x = [a[:, 0:128] for a in w2]
    for i, (f, v) in enumerate(((f1h, w1[0]), (f1m, w1[1]), (f2h, w2x[0]), (f2m, w2x[1]))):
        f[...] = v
    half = jnp.concatenate([half_product(ds[i], us[i], e2h, e2m, at) for i, at in ((0, 0), (1, 1), (5, 3), (6, 4), (7, 5))], axis=0)
    wh = [jnp.concatenate([q[rows(0, 2)], q[rows(3, 3)]], axis=0)[:, 0:128] for q in (e2h, e2m)]
    t = [t0[...], t1[...] + dot(w0, w1, 2, 0, 0), t2[...] + dot(w1, w1, 2, 0, 0), t3[...] + dot(w1w, w2, 2, 0, 0),
         t4[...] + dot(w2x, w2, 2, 0, 0)]
    m5 = t5[...] + dot(wh, half, 2, 0, 0)
    m5 = m5 + m5.T
    row, col = iotas(128, 128)
    pairs = [(b[:128, :128], b[128:, 128:]) for b in t[:4]] + [(t[4][:, :128], m5)]
    ex = [jnp.sum(jnp.where(row == col, b, 0.0), axis=0, keepdims=True) for _, b in pairs]
    ex = jnp.broadcast_to(jnp.concatenate(ex + [jnp.zeros((3, 128), jnp.float32)], axis=0)[None], (16, 8, 128))
    for i, (a, b) in enumerate(pairs):
        c = jnp.where(row <= col, a, b)
        d = t[i][:128, 128:]
        own[:, 8 * i:8 * i + 8] = jnp.where(even, c, d).reshape(16, 8, 128)
        msg[:, 8 * i:8 * i + 8] = jnp.where(even, d, c).reshape(16, 8, 128)
    own[:, 40:48] = ex
    msg[:, 40:48] = ex


def outer_call(*args):
    return pl.pallas_call(outer_kernel, in_specs=[VM] * 18, out_specs=[VM] * 6,
        out_shape=[f32(16, 48, 128)] * 2 + [bf16(256, 256)] * 2 + [bf16(512, 128)] * 2,
        scratch_shapes=[pltpu.VMEM((n * 128, 256), jnp.bfloat16) for n in (11, 11, 9, 9, 7, 7)],
        name="outer", compiler_params=params(24))(*args)


def groups(key):
    found = {}
    for i in range(N):
        found.setdefault(key(i), []).append(i)
    return list(found.values())


def next_chip(block):
    return lax.ppermute(block, "rows", [(i, (i + 1) % N if i % 2 else (i - 1) % N) for i in range(N)])


def across_chip(block):
    return lax.ppermute(block, "rows", [(i, i ^ 1) for i in range(N)])


def in_plane(block):
    return lax.all_to_all(block, "rows", 0, 0, axis_index_groups=groups(lambda i: i % 16))


def along_z(block):
    return lax.all_to_all(block, "rows", 0, 0, axis_index_groups=groups(lambda i: (i // 16, i % 2)))


def copies(block, n):
    return jnp.broadcast_to(block[None], (n,) + block.shape)


def reduce_all(own, msg):
    part = jnp.sum(in_plane(own + across_chip(msg)), axis=0)
    part = jnp.sum(along_z(copies(part, 8)), axis=0)
    own = in_plane(copies(part, 16))
    return own, across_chip(own)


def body(start_states, start_steps, onsite, couplings, columns):
    total = onsite.shape[0] * N
    arrays = (total, columns.T, onsite, couplings, start_states, start_steps)
    to_core, to_chip = edge_call(*arrays)
    from_chip = next_chip(to_chip)
    from_core = across_chip(to_core)
    made = inner_call(*arrays)
    own, msg, *edges = outer_call(from_core, from_chip, *made)
    mine, other = reduce_all(own, msg)
    return tuple(dense_call(mine, other, *made[4:10], *edges))


def solution(mesh):
    in_specs = (P("rows", None), P("rows", None), P("rows", None, None), P("rows", None, None, None), P("rows", None))
    out_specs = (P("rows", None), P("rows", None))
    return jax.shard_map(body, mesh=mesh, in_specs=in_specs, out_specs=out_specs, check_vma=False)
```

```python
import jax
import jax.numpy as jnp
from jax import lax
from jax.sharding import PartitionSpec as P
from jax.experimental import pallas as pl
from jax.experimental.pallas import tpu as pltpu

N = 256

def parts(a, n):
    out = []
    for i in range(n):
        h = a.astype(jnp.bfloat16)
        out.append(h)
        if i < n - 1:
            a = a - h.astype(jnp.float32)
    return out

TERMS = {1: [(0, 0)], 2: [(0, 0), (0, 1), (1, 0)], 3: [(0, 0), (0, 1), (1, 0), (1, 1), (0, 2), (2, 0)]}

def dot(a, b, n=2, ca=1, cb=0):
    a = a if isinstance(a, list) else parts(a, n)
    b = b if isinstance(b, list) else parts(b, n)
    lhs = [a[i] for i, _ in TERMS[n]]
    rhs = [b[j] for _, j in TERMS[n]]
    lhs = lhs[0] if n == 1 else jnp.concatenate(lhs, axis=ca)
    rhs = rhs[0] if n == 1 else jnp.concatenate(rhs, axis=cb)
    return lax.dot_general(lhs, rhs, (((ca,), (cb,)), ((), ())), preferred_element_type=jnp.float32)

def iotas(n, m):
    return lax.broadcasted_iota(jnp.int32, (n, m), 0), lax.broadcasted_iota(jnp.int32, (n, m), 1)

def newton_factor(g, bad):
    row, col = iotas(128, 128)
    diag = row == col
    weight = jnp.where(row > col, 1.0, jnp.where(diag, 0.5, 0.0))
    dg = jnp.where(diag, g, 0.0)
    dr = lax.rsqrt(jnp.sum(dg, axis=0, keepdims=True))
    dc = lax.rsqrt(jnp.sum(dg, axis=1, keepdims=True))
    one = jnp.where(diag, 1.0, 0.0)
    g = g * dr * dc
    f = jnp.where(row > col, g, 0.0)
    fp = parts(f, 1)
    z = one - f + dot(fp, fp, 1) + weight * dot(fp, fp, 1, 1, 1)
    zp = parts(z, 2)
    e = dot(dot(zp, g, 2), zp, 2, 1, 1) - one
    z = z - dot(weight * e, zp[:1], 1)
    return z * dr, jnp.maximum(bad, jnp.sum(e * e, axis=0, keepdims=True))

def direct_factor(g, bad, a_ref, z_ref):
    row, col = iotas(128, 128)
    a_ref[...] = g
    z_ref[...] = jnp.where(row == col, 1.0, 0.0)
    def step(j, _):
        r = a_ref[pl.ds(j, 1), :]
        zr = z_ref[pl.ds(j, 1), :]
        a = a_ref[...]
        c = jnp.sum(jnp.where(col == j, a, 0.0), axis=1, keepdims=True)
        d = jnp.sum(jnp.where(col[:1] == j, r, 0.0), axis=1, keepdims=True)
        f = jnp.where(row[:, :1] > j, c / d, 0.0)
        a_ref[...] = a - f * r
        z_ref[...] = z_ref[...] - f * zr
        return 0
    lax.fori_loop(0, 128, step, 0)
    d = jnp.sum(jnp.where(row == col, a_ref[...], 0.0), axis=1, keepdims=True)
    return z_ref[...] / jnp.sqrt(d), bad

def cat(blocks):
    return jnp.concatenate([jnp.concatenate(r, axis=1) for r in blocks], axis=0)

def block_inverse(g, factor, bad):
    w1, bad = factor(g[0][0], bad)
    w1p = parts(w1, 3)
    l = dot(jnp.concatenate([g[1][0], g[2][0]], axis=0), w1p, 3, 1, 1)
    lp = parts(l, 3)
    p = dot(lp, lp, 3, 1, 1)
    w2, bad = factor(g[1][1] - p[:128, :128], bad)
    w2p = parts(w2, 3)
    l32 = dot(g[2][1] - p[128:, :128], w2p, 3, 1, 1)
    l32p = parts(l32, 3)
    w3, bad = factor(g[2][2] - p[128:, 128:] - dot(l32p, l32p, 3, 1, 1), bad)
    m = dot(lp, w1p)
    a21 = -dot(w2p, m[:128])
    t = m[128:] + dot(l32p, a21)
    s = dot(l32p, w2p)
    low = dot(w3, jnp.concatenate([t, s], axis=1))
    zero = jnp.zeros((128, 128), jnp.float32)
    return cat([[w1, zero, zero], [a21, w2, zero], [-low[:, :128], -low[:, 128:], w3]]), bad

def projected_filter(inv, a):
    def at(i, n=1):
        return slice(128 * i, 128 * i + 128 * n)
    ip = parts(inv, 2)
    ap = parts(a, 2)
    t = [dot([q[at(i), at(0, i + 1)] for q in ip], [q[at(0, i + 1)] for q in ap]) for i in range(3)]
    tp = parts(jnp.concatenate(t, axis=0), 2)
    c = [dot([q[at(j, 3 - j), at(0, j + 1)] for q in tp], [q[at(j), at(0, j + 1)] for q in ip], 2, 1, 1) for j in range(3)]
    p10, p20, p21 = c[0][at(1)], c[0][at(2)], c[1][at(1)]
    proj = cat([[sym(c[0][at(0)]), p10.T, p20.T], [p10, sym(c[1][at(0)]), p21.T], [p20, p21, sym(c[2])]])
    bound = jnp.max(jnp.sum(jnp.abs(proj), axis=0, keepdims=True), axis=1, keepdims=True)
    row, col = iotas(384, 384)
    s = jnp.where(row == col, 1.0, 0.0) - proj / bound
    sp = parts(s, 2)
    f = dot(sp, [q[:, :128] for q in sp])
    return proj, ip, dot(sp, f)

def back(ip, f):
    fp = parts(f, 2)
    part = dot([q[128:] for q in ip], [q[128:] for q in fp], 2, 0, 0)
    head = dot([q[:128, :128] for q in ip], [q[:128] for q in fp], 2, 0, 0)
    return jnp.concatenate([jnp.concatenate([part[:128] + head, part[128:]], axis=0), part], axis=1)

def sym(a):
    return 0.5 * (a + a.T)

def small(mk, nk, rk, factor, bad):
    def assemble(k):
        return [[mk[k], mk[k + 1], nk[k]], [mk[k + 1], mk[k + 2], nk[k + 1]], [nk[k].T, nk[k + 1].T, rk[k]]]
    inv, bad = block_inverse(assemble(0), factor, bad)
    proj, ip, f = projected_filter(inv, cat(assemble(1)))
    f2 = jnp.concatenate([jnp.zeros((128, 128), jnp.float32), f[128:]], axis=0)
    ff2 = jnp.concatenate([f, f2], axis=1)
    ffp = parts(ff2, 3)
    fp = [q[:, :128] for q in ffp]
    cq = back(ip, f)
    cqp = parts(cq, 3)
    cp = [q[:, :128] for q in cqp]
    gram = dot(ffp, ffp, 3, 0, 0)
    one = dot(ffp, dot(proj, ffp), 3, 0, 0)
    two = dot(cp, dot(cat(assemble(2)), cqp), 3, 0, 0)
    three = dot(cp, dot(cat(assemble(3)), cp), 3, 0, 0)
    ftf, qq = gram[:128, :128], gram[128:, 128:]
    b1, c1q, q1q = one[:128, :128], one[:128, 128:], one[128:, 128:]
    c2c, c2q = sym(two[:, :128]), two[:, 128:]
    b1 = sym(b1)
    gu = [[ftf, None, None], [b1, c2c, None], [qq, c1q.T, qq]]
    au = cat([[b1, c2c, c1q], [c2c, sym(three), c2q], [c1q.T, c2q.T, sym(q1q)]])
    inv, bad = block_inverse(gu, factor, bad)
    _, ip, f = projected_filter(inv, au)
    fp = parts(f, 3)
    w, bad = factor(dot(fp, fp, 3, 0, 0), bad)
    y = dot(fp, w, 2, 1, 1)
    k = back(ip, y)
    kb = dot(cqp, jnp.concatenate([k[:128], k[256:]], axis=0))
    kh = dot(cp, k[128:256])
    return jnp.concatenate([kb[:128], kb[128:256] + kh[:128], kh[128:256], kb[256:], kh[256:]], axis=0), bad

def unpack(mine, other):
    row, col = iotas(128, 128)
    even = lax.rem(lax.axis_index("rows"), 2) == 0
    ex = mine[0, 40:48]
    mk, nk, rk = [], [], []
    for i in range(5):
        a, c = [q[:, 8 * i:8 * i + 8].reshape(128, 128) for q in (mine, other)]
        b = jnp.where(even, a, c)
        nk.append(jnp.where(even, c, a))
        bt = b.T
        mk.append(jnp.where(row <= col, b, bt))
        rk.append(jnp.where(row == col, ex[i:i + 1], jnp.where(row <= col, bt, b)))
    mk.append(rk.pop())
    return mk, nk, rk

def dense_kernel(*refs):
    mine, other = refs[:2]
    v0h, v0m, v1h, v1m, v2h, v2m, f1h, f1m, f2h, f2m = refs[2:12]
    states, steps = refs[12:14]
    k_ref, a_ref, z_ref, out_ref, out_sem = refs[14:19]
    res, bad = small(*unpack(mine, other), newton_factor, jnp.zeros((1, 128), jnp.float32))
    k_ref[...] = res
    worst = jnp.sum(bad)
    @pl.when(jnp.logical_not(worst < 4e-5))
    def _():
        k_ref[...] = small(*unpack(mine, other), lambda g, b: direct_factor(g, b, a_ref, z_ref), None)[0]
    kk = parts(jnp.concatenate([k_ref[0:128], k_ref[384:512], k_ref[128:256], k_ref[512:640], k_ref[256:384]], axis=0), 2)
    def rows(at):
        return slice(128 * at, 128 * at + 128)
    def pair(i, v0, v1, v2, f1, f2):
        one = v1[rows(i - 1)] if 1 <= i <= 6 else f1[rows(i // 7)]
        two = v2[rows(i - 2), 0:128] if 2 <= i <= 5 else f2[rows(i if i < 2 else i - 4)]
        return jnp.concatenate([v0[rows(i)], one, two], axis=1)
    copies = []
    for i in range(4):
        v = [jnp.concatenate([pair(2 * i + j, *q) for j in range(2)], axis=0)
             for q in ((v0h, v1h, v2h, f1h, f2h), (v0m, v1m, v2m, f1m, f2m))]
        out = dot(v, kk, 2)
        for j, ref in enumerate((states, steps)):
            out_ref[j, 256 * i:256 * i + 256] = out[:, 128 * j:128 * j + 128]
            copies.append(pltpu.make_async_copy(out_ref.at[j, 256 * i:256 * i + 256], ref.at[256 * i:256 * i + 256], out_sem.at[len(copies)]))
            copies[-1].start()
    for c in copies:
        c.wait()

def dense_call(mine, other, *kept):
    vm = pl.BlockSpec(memory_space=pltpu.VMEM)
    hbm = pl.BlockSpec(memory_space=pl.ANY)
    square = pltpu.VMEM((128, 128), jnp.float32)
    return pl.pallas_call(dense_kernel, in_specs=[vm] * 12, out_specs=[hbm] * 2,
        out_shape=[jax.ShapeDtypeStruct((1024, 128), jnp.float32)] * 2,
        scratch_shapes=[pltpu.VMEM((640, 256), jnp.float32), square, square, pltpu.VMEM((2, 1024, 128), jnp.float32)]
        + [pltpu.SemaphoreType.DMA((8,))],
        name="dense", compiler_params=pltpu.CompilerParams(vmem_limit_bytes=24 * 2**20))(mine, other, *kept)


VM = pl.BlockSpec(memory_space=pltpu.VMEM)
ANY = pl.BlockSpec(memory_space=pl.ANY)
DMA = pltpu.SemaphoreType.DMA


def f32(*shape):
    return jax.ShapeDtypeStruct(shape, jnp.float32)


def bf16(*shape):
    return jax.ShapeDtypeStruct(shape, jnp.bfloat16)


def params(mib):
    return pltpu.CompilerParams(vmem_limit_bytes=mib * 2**20)


def weights(total, col):
    row = lax.axis_index("rows") * 16 + lax.broadcasted_iota(jnp.int32, (4, 16), 1)
    ahead = lax.rem(col[...] - row + total, total)
    return jnp.where(ahead == 1, 1.0, 0.0), jnp.where(ahead == 2, 1.0, 0.0)


def pair_blocks(one, two, onsite, coup, pair, at):
    def offsets(b, k):
        a1 = jnp.zeros((64, 64), jnp.float32)
        a2 = jnp.zeros((64, 64), jnp.float32)
        for j in range(4):
            c = coup[k, j]
            a1 = a1 + one[j:j + 1, b:b + 1] * c
            a2 = a2 + two[j:j + 1, b:b + 1] * c
        return a1, a2
    a1, a2 = offsets(2 * pair, at)
    b1, b2 = offsets(2 * pair + 1, at + 1)
    o0, o1 = onsite[at], onsite[at + 1]
    u = jnp.concatenate([jnp.concatenate([a2, jnp.zeros((64, 64), jnp.float32)], axis=1), jnp.concatenate([b1, b2], axis=1)], axis=0)
    d = jnp.concatenate([jnp.concatenate([o0 + o0.T, a1], axis=1), jnp.concatenate([a1.T, o1 + o1.T], axis=1)], axis=0)
    return u, d


def edge_kernel(total, col, onsite, coup, x, p, a_ref, b_ref, on_v, co_v, a_v, b_v, sem, out_sem):
    odd = lax.rem(lax.axis_index("rows"), 2)
    pairs = [(onsite.at[0:4], on_v.at[0:4]), (onsite.at[12:16], on_v.at[4:8]), (coup.at[0:4], co_v.at[0:4]), (coup.at[12:16], co_v.at[4:8])]
    for ref, at in ((a_v, 1 - odd), (b_v, odd)):
        pairs.append((x.at[pl.ds(pl.multiple_of(at * 640, 128), 384)], ref.at[0:384]))
        pairs.append((p.at[pl.ds(pl.multiple_of(at * 768, 128), 256)], ref.at[384:640]))
    fetch = [pltpu.make_async_copy(a, b, sem.at[i]) for i, (a, b) in enumerate(pairs)]
    store = [pltpu.make_async_copy(v.at[s], ref.at[s], out_sem.at[i]) for i, (v, ref, s) in enumerate(
        (v, ref, s) for s in (slice(0, 640), slice(640, 1024)) for v, ref in ((a_v, a_ref), (b_v, b_ref)))]
    for c in fetch:
        c.start()
    one, two = weights(total, col)
    for c in fetch:
        c.wait()
    for c in store[:2]:
        c.start()
    even = odd == 0
    row, lane = iotas(128, 128)
    corner = (row < 64) & (lane >= 64)
    for i in range(2):
        packed = []
        for pair, at in ((i, 2 * i), (6 + i, 4 + 2 * i)):
            u, d = pair_blocks(one, two, on_v, co_v, pair, at)
            below = jnp.concatenate([d[64:], d[64:]], axis=0)
            packed.append((jnp.where(corner, below, u), d[:64]))
        k = 640 + 192 * i
        for j, s in enumerate((slice(k, k + 128), slice(k + 128, k + 192))):
            a_v[s] = jnp.where(even, packed[1][j], packed[0][j])
            b_v[s] = jnp.where(even, packed[0][j], packed[1][j])
    for c in store[2:]:
        c.start()
    for c in store:
        c.wait()


def unpack_blocks(u, top):
    row, lane = iotas(128, 128)
    low = jnp.concatenate([top[:, 64:].T, u[:64, 64:]], axis=1)
    return jnp.where((row < 64) & (lane >= 64), 0.0, u), jnp.concatenate([top, low], axis=0)


def edge_call(total, columns, onsite, couplings, x, p):
    return pl.pallas_call(lambda *a: edge_kernel(total, *a), in_specs=[VM] + [ANY] * 4, out_specs=[ANY] * 2,
        out_shape=[f32(1024, 128)] * 2,
        scratch_shapes=[pltpu.VMEM((8, 64, 64), jnp.float32), pltpu.VMEM((8, 4, 64, 64), jnp.float32),
                        pltpu.VMEM((1024, 128), jnp.float32), pltpu.VMEM((1024, 128), jnp.float32), DMA((8,)), DMA((4,))], name="edge",
        compiler_params=params(60))(columns, onsite, couplings, x, p)


def put(h, l, at, val):
    a, b = parts(val, 2)
    h[at * 128:at * 128 + 128] = a
    l[at * 128:at * 128 + 128] = b


def band(lower, diag, upper):
    return [jnp.concatenate([lower[k], diag[k], upper[k]], axis=1) for k in range(2)]


def half_product(diag, upper, h, l, at):
    s = slice(at * 128, at * 128 + 256)
    b = [jnp.concatenate([diag[k] * jnp.bfloat16(0.5), upper[k]], axis=1) for k in range(2)]
    return dot(b, [h[s, 0:128], l[s, 0:128]], 2)


def inner_kernel(total, col, onsite, coup, x, p, uh, um, dh, dm, v0h, v0m, v1h, v1m, v2h, v2m, t0, t1, t2, t3, t4, t5):
    one, two = weights(total, col)
    for i in range(8):
        u, d = pair_blocks(one, two, onsite, coup, i, 2 * i)
        uh[i], um[i] = parts(u, 2)
        dh[i], dm[i] = parts(d, 2)
        s = slice(128 * i, 128 * i + 128)
        put(v0h, v0m, i, jnp.concatenate([x[s], p[s]], axis=1))
    us = [[uh[i], um[i]] for i in range(8)]
    ds = [[dh[i], dm[i]] for i in range(8)]
    bands = {i: band([a.T for a in us[i - 1]], ds[i], us[i]) for i in range(1, 7)}
    for i in range(1, 7):
        s = slice((i - 1) * 128, (i + 2) * 128)
        put(v1h, v1m, i - 1, dot(bands[i], [v0h[s], v0m[s]], 2))
    for i in range(2, 6):
        s = slice((i - 2) * 128, (i + 1) * 128)
        put(v2h, v2m, i - 2, dot(bands[i], [v1h[s], v1m[s]], 2))
    w0 = [v0h[...], v0m[...]]
    w0i = [v0h[128:896], v0m[128:896]]
    w1 = [v1h[...], v1m[...]]
    w1i = [v1h[128:640], v1m[128:640]]
    w2 = [v2h[...], v2m[...]]
    w2x = [v2h[:, 0:128], v2m[:, 0:128]]
    t0[...] = dot(w0, w0, 2, 0, 0)
    t1[...] = dot(w0i, w1, 2, 0, 0)
    t2[...] = dot(w1, w1, 2, 0, 0)
    t3[...] = dot(w1i, w2, 2, 0, 0)
    t4[...] = dot(w2x, w2, 2, 0, 0)
    half = jnp.concatenate([half_product(ds[i], us[i], v2h, v2m, i - 2) for i in range(2, 5)], axis=0)
    t5[...] = dot([a[0:384] for a in w2x], half, 2, 0, 0)


def inner_call(total, columns, onsite, couplings, x, p):
    return pl.pallas_call(lambda *a: inner_kernel(total, *a), in_specs=[VM] * 5, out_specs=[VM] * 16,
        out_shape=[bf16(8, 128, 128)] * 4 + [bf16(1024, 256)] * 2 + [bf16(768, 256)] * 2 + [bf16(512, 256)] * 2
        + [f32(256, 256)] * 4 + [f32(128, 256), f32(128, 128)], name="inner",
        compiler_params=params(24))(columns, onsite, couplings, x, p)


def outer_kernel(ra, rb, uh, um, dh, dm, v0h, v0m, v1h, v1m, v2h, v2m, t0, t1, t2, t3, t4, t5, own, msg, f1h, f1m, f2h, f2m,
                 e0h, e0m, e1h, e1m, e2h, e2m):
    odd = lax.rem(lax.axis_index("rows"), 2)
    even = odd == 0
    def before(s):
        return jnp.where(even, rb[s], ra[s])
    def after(s):
        return jnp.where(even, ra[s], rb[s])
    def rows(at, n=1):
        return slice(at * 128, (at + n) * 128)
    for i in range(2):
        put(e0h, e0m, i, jnp.concatenate([before(rows(1 + i)), before(rows(3 + i))], axis=1))
    for i in range(3):
        last = after(rows(3 + i)) if i < 2 else jnp.zeros((128, 128), jnp.float32)
        put(e0h, e0m, i + 8, jnp.concatenate([after(rows(i)), last], axis=1))
    for e, v in ((e0h, v0h), (e0m, v0m)):
        e[rows(2, 3)] = v[rows(0, 3)]
        e[rows(5, 3)] = v[rows(5, 3)]
    us = {i: [uh[i], um[i]] for i in range(8)}
    ds = {i: [dh[i], dm[i]] for i in range(8)}
    for i, side, k in ((-2, before, 640), (-1, before, 832), (8, after, 640), (9, after, 832)):
        us[i], ds[i] = [parts(a, 2) for a in unpack_blocks(side(slice(k, k + 128)), side(slice(k + 128, k + 192)))]
    bands = {i: band([a.T for a in us[i - 1]], ds[i], us[i]) for i in (-1, 0, 1, 6, 7, 8, 9)}
    for i, at, src in ((-1, 0, 0), (0, 1, 1), (7, 6, 6), (8, 7, 7), (9, 8, 8)):
        s = rows(src, 3)
        put(e1h, e1m, at, dot(bands[i], [e0h[s], e0m[s]], 2))
    for e, v in ((e1h, v1h), (e1m, v1m)):
        e[rows(2, 2)] = v[rows(0, 2)]
        e[rows(4, 2)] = v[rows(4, 2)]
    for i, at, src in ((0, 0, 0), (1, 1, 1), (6, 4, 4), (7, 5, 5), (8, 6, 6)):
        s = rows(src, 3)
        put(e2h, e2m, at, dot(bands[i], [e1h[s], e1m[s]], 2))
    for e, v in ((e2h, v2h), (e2m, v2m)):
        e[rows(2)] = v[rows(0)]
        e[rows(3)] = v[rows(3)]
    def join(a, b, i, n, j, m):
        return [jnp.concatenate([q[rows(i, n)], q[rows(j, m)]], axis=0) for q in (a, b)]
    w0 = join(v0h, v0m, 0, 1, 7, 1)
    w1 = join(e1h, e1m, 1, 1, 6, 1)
    w1w = join(e1h, e1m, 1, 2, 5, 2)
    w2 = join(e2h, e2m, 0, 2, 4, 2)
    w2x = [a[:, 0:128] for a in w2]
    for f, v in ((f1h, w1[0]), (f1m, w1[1]), (f2h, w2x[0]), (f2m, w2x[1])):
        f[...] = v
    half = jnp.concatenate([half_product(ds[i], us[i], e2h, e2m, at) for i, at in ((0, 0), (1, 1), (5, 3), (6, 4), (7, 5))], axis=0)
    wh = [jnp.concatenate([q[rows(0, 2)], q[rows(3, 3)]], axis=0)[:, 0:128] for q in (e2h, e2m)]
    t = [t0[...], t1[...] + dot(w0, w1, 2, 0, 0), t2[...] + dot(w1, w1, 2, 0, 0), t3[...] + dot(w1w, w2, 2, 0, 0),
         t4[...] + dot(w2x, w2, 2, 0, 0)]
    m5 = t5[...] + dot(wh, half, 2, 0, 0)
    m5 = m5 + m5.T
    row, col = iotas(128, 128)
    pairs = [(b[:128, :128], b[128:, 128:]) for b in t[:4]] + [(t[4][:, :128], m5)]
    ex = [jnp.sum(jnp.where(row == col, b, 0.0), axis=0, keepdims=True) for _, b in pairs]
    ex = jnp.broadcast_to(jnp.concatenate(ex + [jnp.zeros((3, 128), jnp.float32)], axis=0)[None], (16, 8, 128))
    for i, (a, b) in enumerate(pairs):
        c = jnp.where(row <= col, a, b)
        d = t[i][:128, 128:]
        own[:, 8 * i:8 * i + 8] = jnp.where(even, c, d).reshape(16, 8, 128)
        msg[:, 8 * i:8 * i + 8] = jnp.where(even, d, c).reshape(16, 8, 128)
    own[:, 40:48] = ex
    msg[:, 40:48] = ex


def outer_call(*args):
    return pl.pallas_call(outer_kernel, in_specs=[VM] * 18, out_specs=[VM] * 6,
        out_shape=[f32(16, 48, 128)] * 2 + [bf16(256, 256)] * 2 + [bf16(512, 128)] * 2,
        scratch_shapes=[pltpu.VMEM((n * 128, 256), jnp.bfloat16) for n in (11, 11, 9, 9, 7, 7)],
        name="outer", compiler_params=params(24))(*args)


def groups(key):
    found = {}
    for i in range(N):
        found.setdefault(key(i), []).append(i)
    return list(found.values())


def next_chip(block):
    return lax.ppermute(block, "rows", [(i, (i + 1) % N if i % 2 else (i - 1) % N) for i in range(N)])


def across_chip(block):
    return lax.ppermute(block, "rows", [(i, i ^ 1) for i in range(N)])


def in_plane(block):
    return lax.all_to_all(block, "rows", 0, 0, axis_index_groups=groups(lambda i: i % 16))


def along_z(block):
    return lax.all_to_all(block, "rows", 0, 0, axis_index_groups=groups(lambda i: (i // 16, i % 2)))


def copies(block, n):
    return jnp.broadcast_to(block[None], (n,) + block.shape)


def reduce_all(own, msg):
    part = jnp.sum(in_plane(own + across_chip(msg)), axis=0)
    part = jnp.sum(along_z(copies(part, 8)), axis=0)
    own = in_plane(copies(part, 16))
    return own, across_chip(own)


def body(start_states, start_steps, onsite, couplings, columns):
    total = onsite.shape[0] * N
    arrays = (total, columns.T, onsite, couplings, start_states, start_steps)
    to_core, to_chip = edge_call(*arrays)
    from_chip = next_chip(to_chip)
    from_core = across_chip(to_core)
    made = inner_call(*arrays)
    own, msg, *edges = outer_call(from_core, from_chip, *made)
    mine, other = reduce_all(own, msg)
    return tuple(dense_call(mine, other, *made[4:10], *edges))


def solution(mesh):
    in_specs = (P("rows", None), P("rows", None), P("rows", None, None), P("rows", None, None, None), P("rows", None))
    out_specs = (P("rows", None), P("rows", None))
    return jax.shard_map(body, mesh=mesh, in_specs=in_specs, out_specs=out_specs, check_vma=False)
```

```python
import jax
import jax.numpy as jnp
from jax import lax
from jax.sharding import PartitionSpec as P
from jax.experimental import pallas as pl
from jax.experimental.pallas import tpu as pltpu

N = 256

def parts(a, n):
    out = []
    for i in range(n):
        h = a.astype(jnp.bfloat16)
        out.append(h)
        if i < n - 1:
            a = a - h.astype(jnp.float32)
    return out

TERMS = {1: [(0, 0)], 2: [(0, 0), (0, 1), (1, 0)], 3: [(0, 0), (0, 1), (1, 0), (1, 1), (0, 2), (2, 0)]}

def dot(a, b, n=2, ca=1, cb=0):
    a = a if isinstance(a, list) else parts(a, n)
    b = b if isinstance(b, list) else parts(b, n)
    lhs = [a[i] for i, _ in TERMS[n]]
    rhs = [b[j] for _, j in TERMS[n]]
    lhs = lhs[0] if n == 1 else jnp.concatenate(lhs, axis=ca)
    rhs = rhs[0] if n == 1 else jnp.concatenate(rhs, axis=cb)
    return lax.dot_general(lhs, rhs, (((ca,), (cb,)), ((), ())), preferred_element_type=jnp.float32)

def iotas(n, m):
    return lax.broadcasted_iota(jnp.int32, (n, m), 0), lax.broadcasted_iota(jnp.int32, (n, m), 1)

def newton_factor(g, bad):
    row, col = iotas(128, 128)
    diag = row == col
    weight = jnp.where(row > col, 1.0, jnp.where(diag, 0.5, 0.0))
    dg = jnp.where(diag, g, 0.0)
    dr = lax.rsqrt(jnp.sum(dg, axis=0, keepdims=True))
    dc = lax.rsqrt(jnp.sum(dg, axis=1, keepdims=True))
    one = jnp.where(diag, 1.0, 0.0)
    g = g * dr * dc
    f = jnp.where(row > col, g, 0.0)
    fp = parts(f, 1)
    z = one - f + dot(fp, fp, 1) + weight * dot(fp, fp, 1, 1, 1)
    zp = parts(z, 2)
    e = dot(dot(zp, g, 2), zp, 2, 1, 1) - one
    z = z - dot(weight * e, zp[:1], 1)
    return z * dr, jnp.maximum(bad, jnp.sum(e * e, axis=0, keepdims=True))

def direct_factor(g, bad, a_ref, z_ref):
    row, col = iotas(128, 128)
    a_ref[...] = g
    z_ref[...] = jnp.where(row == col, 1.0, 0.0)
    def step(j, _):
        r = a_ref[pl.ds(j, 1), :]
        zr = z_ref[pl.ds(j, 1), :]
        a = a_ref[...]
        c = jnp.sum(jnp.where(col == j, a, 0.0), axis=1, keepdims=True)
        d = jnp.sum(jnp.where(col[:1] == j, r, 0.0), axis=1, keepdims=True)
        f = jnp.where(row[:, :1] > j, c / d, 0.0)
        a_ref[...] = a - f * r
        z_ref[...] = z_ref[...] - f * zr
        return 0
    lax.fori_loop(0, 128, step, 0)
    d = jnp.sum(jnp.where(row == col, a_ref[...], 0.0), axis=1, keepdims=True)
    return z_ref[...] / jnp.sqrt(d), bad

def cat(blocks):
    return jnp.concatenate([jnp.concatenate(r, axis=1) for r in blocks], axis=0)

def block_inverse(g, factor, bad):
    w1, bad = factor(g[0][0], bad)
    w1p = parts(w1, 3)
    l = dot(jnp.concatenate([g[1][0], g[2][0]], axis=0), w1p, 3, 1, 1)
    lp = parts(l, 3)
    p = dot(lp, lp, 3, 1, 1)
    w2, bad = factor(g[1][1] - p[:128, :128], bad)
    w2p = parts(w2, 3)
    l32 = dot(g[2][1] - p[128:, :128], w2p, 3, 1, 1)
    l32p = parts(l32, 3)
    w3, bad = factor(g[2][2] - p[128:, 128:] - dot(l32p, l32p, 3, 1, 1), bad)
    m = dot(lp, w1p)
    a21 = -dot(w2p, m[:128])
    t = m[128:] + dot(l32p, a21)
    s = dot(l32p, w2p)
    low = dot(w3, jnp.concatenate([t, s], axis=1))
    zero = jnp.zeros((128, 128), jnp.float32)
    return cat([[w1, zero, zero], [a21, w2, zero], [-low[:, :128], -low[:, 128:], w3]]), bad

def projected_filter(inv, a):
    def at(i, n=1):
        return slice(128 * i, 128 * i + 128 * n)
    ip = parts(inv, 2)
    ap = parts(a, 2)
    t = [dot([q[at(i), at(0, i + 1)] for q in ip], [q[at(0, i + 1)] for q in ap]) for i in range(3)]
    tp = parts(jnp.concatenate(t, axis=0), 2)
    c = [dot([q[at(j, 3 - j), at(0, j + 1)] for q in tp], [q[at(j), at(0, j + 1)] for q in ip], 2, 1, 1) for j in range(3)]
    p10, p20, p21 = c[0][at(1)], c[0][at(2)], c[1][at(1)]
    proj = cat([[sym(c[0][at(0)]), p10.T, p20.T], [p10, sym(c[1][at(0)]), p21.T], [p20, p21, sym(c[2])]])
    bound = jnp.max(jnp.sum(jnp.abs(proj), axis=0, keepdims=True), axis=1, keepdims=True)
    row, col = iotas(384, 384)
    s = jnp.where(row == col, 1.0, 0.0) - proj / bound
    sp = parts(s, 2)
    f = dot(sp, [q[:, :128] for q in sp])
    return proj, ip, dot(sp, f)

def back(ip, f):
    fp = parts(f, 2)
    part = dot([q[128:] for q in ip], [q[128:] for q in fp], 2, 0, 0)
    head = dot([q[:128, :128] for q in ip], [q[:128] for q in fp], 2, 0, 0)
    return jnp.concatenate([jnp.concatenate([part[:128] + head, part[128:]], axis=0), part], axis=1)

def sym(a):
    return 0.5 * (a + a.T)

def small(mk, nk, rk, factor, bad):
    def assemble(k):
        return [[mk[k], mk[k + 1], nk[k]], [mk[k + 1], mk[k + 2], nk[k + 1]], [nk[k].T, nk[k + 1].T, rk[k]]]
    inv, bad = block_inverse(assemble(0), factor, bad)
    proj, ip, f = projected_filter(inv, cat(assemble(1)))
    f2 = jnp.concatenate([jnp.zeros((128, 128), jnp.float32), f[128:]], axis=0)
    ff2 = jnp.concatenate([f, f2], axis=1)
    ffp = parts(ff2, 3)
    fp = [q[:, :128] for q in ffp]
    cq = back(ip, f)
    cqp = parts(cq, 3)
    cp = [q[:, :128] for q in cqp]
    gram = dot(ffp, ffp, 3, 0, 0)
    one = dot(ffp, dot(proj, ffp), 3, 0, 0)
    two = dot(cp, dot(cat(assemble(2)), cqp), 3, 0, 0)
    three = dot(cp, dot(cat(assemble(3)), cp), 3, 0, 0)
    ftf, qq = gram[:128, :128], gram[128:, 128:]
    b1, c1q, q1q = one[:128, :128], one[:128, 128:], one[128:, 128:]
    c2c, c2q = sym(two[:, :128]), two[:, 128:]
    b1 = sym(b1)
    gu = [[ftf, None, None], [b1, c2c, None], [qq, c1q.T, qq]]
    au = cat([[b1, c2c, c1q], [c2c, sym(three), c2q], [c1q.T, c2q.T, sym(q1q)]])
    inv, bad = block_inverse(gu, factor, bad)
    _, ip, f = projected_filter(inv, au)
    fp = parts(f, 3)
    w, bad = factor(dot(fp, fp, 3, 0, 0), bad)
    y = dot(fp, w, 2, 1, 1)
    k = back(ip, y)
    kb = dot(cqp, jnp.concatenate([k[:128], k[256:]], axis=0))
    kh = dot(cp, k[128:256])
    return jnp.concatenate([kb[:128], kb[128:256] + kh[:128], kh[128:256], kb[256:], kh[256:]], axis=0), bad

def unpack(mine, other):
    row, col = iotas(128, 128)
    even = lax.rem(lax.axis_index("rows"), 2) == 0
    ex = mine[0, 40:48]
    mk, nk, rk = [], [], []
    for i in range(5):
        a, c = [q[:, 8 * i:8 * i + 8].reshape(128, 128) for q in (mine, other)]
        b = jnp.where(even, a, c)
        nk.append(jnp.where(even, c, a))
        bt = b.T
        mk.append(jnp.where(row <= col, b, bt))
        rk.append(jnp.where(row == col, ex[i:i + 1], jnp.where(row <= col, bt, b)))
    mk.append(rk.pop())
    return mk, nk, rk

def dense_kernel(*refs):
    mine, other = refs[:2]
    v0h, v0m, v1h, v1m, v2h, v2m, f1h, f1m, f2h, f2m = refs[2:12]
    states, steps = refs[12:14]
    k_ref, a_ref, z_ref, out_ref, out_sem = refs[14:19]
    res, bad = small(*unpack(mine, other), newton_factor, jnp.zeros((1, 128), jnp.float32))
    k_ref[...] = res
    worst = jnp.sum(bad)
    @pl.when(jnp.logical_not(worst < 4e-5))
    def _():
        k_ref[...] = small(*unpack(mine, other), lambda g, b: direct_factor(g, b, a_ref, z_ref), None)[0]
    kk = parts(jnp.concatenate([k_ref[0:128], k_ref[384:512], k_ref[128:256], k_ref[512:640], k_ref[256:384]], axis=0), 2)
    def rows(at):
        return slice(128 * at, 128 * at + 128)
    def pair(i, v0, v1, v2, f1, f2):
        one = v1[rows(i - 1)] if 1 <= i <= 6 else f1[rows(i // 7)]
        two = v2[rows(i - 2), 0:128] if 2 <= i <= 5 else f2[rows(i if i < 2 else i - 4)]
        return jnp.concatenate([v0[rows(i)], one, two], axis=1)
    copies = []
    for i in range(4):
        v = [jnp.concatenate([pair(2 * i + j, *q) for j in range(2)], axis=0)
             for q in ((v0h, v1h, v2h, f1h, f2h), (v0m, v1m, v2m, f1m, f2m))]
        out = dot(v, kk, 2)
        for j, ref in enumerate((states, steps)):
            out_ref[j, 256 * i:256 * i + 256] = out[:, 128 * j:128 * j + 128]
            copies.append(pltpu.make_async_copy(out_ref.at[j, 256 * i:256 * i + 256], ref.at[256 * i:256 * i + 256], out_sem.at[len(copies)]))
            copies[-1].start()
    for c in copies:
        c.wait()

def dense_call(mine, other, *kept):
    vm = pl.BlockSpec(memory_space=pltpu.VMEM)
    hbm = pl.BlockSpec(memory_space=pl.ANY)
    square = pltpu.VMEM((128, 128), jnp.float32)
    return pl.pallas_call(dense_kernel, in_specs=[vm] * 12, out_specs=[hbm] * 2,
        out_shape=[jax.ShapeDtypeStruct((1024, 128), jnp.float32)] * 2,
        scratch_shapes=[pltpu.VMEM((640, 256), jnp.float32), square, square, pltpu.VMEM((2, 1024, 128), jnp.float32)]
        + [pltpu.SemaphoreType.DMA((8,))],
        name="dense", compiler_params=pltpu.CompilerParams(vmem_limit_bytes=24 * 2**20))(mine, other, *kept)


VM = pl.BlockSpec(memory_space=pltpu.VMEM)
ANY = pl.BlockSpec(memory_space=pl.ANY)
DMA = pltpu.SemaphoreType.DMA


def f32(*shape):
    return jax.ShapeDtypeStruct(shape, jnp.float32)


def bf16(*shape):
    return jax.ShapeDtypeStruct(shape, jnp.bfloat16)


def params(mib):
    return pltpu.CompilerParams(vmem_limit_bytes=mib * 2**20)


def weights(total, col):
    row = lax.axis_index("rows") * 16 + lax.broadcasted_iota(jnp.int32, (4, 16), 1)
    ahead = lax.rem(col[...] - row + total, total)
    return jnp.where(ahead == 1, 1.0, 0.0), jnp.where(ahead == 2, 1.0, 0.0)


def pair_blocks(one, two, onsite, coup, pair, at):
    def offsets(b, k):
        a1 = jnp.zeros((64, 64), jnp.float32)
        a2 = jnp.zeros((64, 64), jnp.float32)
        for j in range(4):
            c = coup[k, j]
            a1 = a1 + one[j:j + 1, b:b + 1] * c
            a2 = a2 + two[j:j + 1, b:b + 1] * c
        return a1, a2
    a1, a2 = offsets(2 * pair, at)
    b1, b2 = offsets(2 * pair + 1, at + 1)
    o0, o1 = onsite[at], onsite[at + 1]
    u = jnp.concatenate([jnp.concatenate([a2, jnp.zeros((64, 64), jnp.float32)], axis=1), jnp.concatenate([b1, b2], axis=1)], axis=0)
    d = jnp.concatenate([jnp.concatenate([o0 + o0.T, a1], axis=1), jnp.concatenate([a1.T, o1 + o1.T], axis=1)], axis=0)
    return u, d


def packed(u, d):
    row, lane = iotas(128, 128)
    below = jnp.concatenate([d[64:], d[64:]], axis=0)
    return jnp.where((row < 64) & (lane >= 64), below, u), d[:64]


def edge_kernel(total, col, onsite, coup, x, p, out, on_v, co_v, out_v, sem, out_sem):
    odd = lax.rem(lax.axis_index("rows"), 2)
    pairs = [(onsite.at[pl.ds(odd * 12, 4)], on_v), (coup.at[pl.ds(odd * 12, 4)], co_v),
             (x.at[pl.ds(pl.multiple_of(odd * 640, 128), 384)], out_v.at[0:384]),
             (p.at[pl.ds(pl.multiple_of(odd * 768, 128), 256)], out_v.at[384:640])]
    fetch = [pltpu.make_async_copy(a, b, sem.at[i]) for i, (a, b) in enumerate(pairs)]
    store = [pltpu.make_async_copy(out_v.at[s], out.at[s], out_sem.at[i]) for i, s in enumerate((slice(0, 640), slice(640, 1024)))]
    for c in fetch:
        c.start()
    one, two = [jnp.where(odd == 0, w[:, 0:4], w[:, 12:16]) for w in weights(total, col)]
    for c in fetch:
        c.wait()
    store[0].start()
    for i in range(2):
        k = 640 + 192 * i
        out_v[k:k + 128], out_v[k + 128:k + 192] = packed(*pair_blocks(one, two, on_v, co_v, i, 2 * i))
    store[1].start()
    for c in store:
        c.wait()


def unpack_blocks(u, top):
    row, lane = iotas(128, 128)
    low = jnp.concatenate([top[:, 64:].T, u[:64, 64:]], axis=1)
    return jnp.where((row < 64) & (lane >= 64), 0.0, u), jnp.concatenate([top, low], axis=0)


def edge_call(total, columns, onsite, couplings, x, p):
    return pl.pallas_call(lambda *a: edge_kernel(total, *a), in_specs=[VM] + [ANY] * 4, out_specs=ANY, out_shape=f32(1024, 128),
        scratch_shapes=[pltpu.VMEM((4, 64, 64), jnp.float32), pltpu.VMEM((4, 4, 64, 64), jnp.float32),
                        pltpu.VMEM((1024, 128), jnp.float32), DMA((4,)), DMA((2,))], name="edge",
        compiler_params=params(60))(columns, onsite, couplings, x, p)


def put(h, l, at, val):
    a, b = parts(val, 2)
    h[at * 128:at * 128 + 128] = a
    l[at * 128:at * 128 + 128] = b


def band(lower, diag, upper):
    return [jnp.concatenate([lower[k], diag[k], upper[k]], axis=1) for k in range(2)]


def half_product(diag, upper, h, l, at):
    s = slice(at * 128, at * 128 + 256)
    b = [jnp.concatenate([diag[k] * jnp.bfloat16(0.5), upper[k]], axis=1) for k in range(2)]
    return dot(b, [h[s, 0:128], l[s, 0:128]], 2)


def inner_kernel(total, col, onsite, coup, x, p, side, uh, um, dh, dm, v0h, v0m, v1h, v1m, v2h, v2m, t0, t1, t2, t3, t4, t5):
    one, two = weights(total, col)
    even = lax.rem(lax.axis_index("rows"), 2) == 0
    side[0:384] = jnp.where(even, x[640:1024], x[0:384])
    side[384:640] = jnp.where(even, p[768:1024], p[0:256])
    ends = {}
    for i in range(8):
        u, d = pair_blocks(one, two, onsite, coup, i, 2 * i)
        if i not in range(2, 6):
            ends[i] = packed(u, d)
        uh[i], um[i] = parts(u, 2)
        dh[i], dm[i] = parts(d, 2)
        s = slice(128 * i, 128 * i + 128)
        put(v0h, v0m, i, jnp.concatenate([x[s], p[s]], axis=1))
    for i in range(2):
        k = 640 + 192 * i
        side[k:k + 128], side[k + 128:k + 192] = [jnp.where(even, a, b) for a, b in zip(ends[6 + i], ends[i])]
    us = [[uh[i], um[i]] for i in range(8)]
    ds = [[dh[i], dm[i]] for i in range(8)]
    bands = {i: band([a.T for a in us[i - 1]], ds[i], us[i]) for i in range(1, 7)}
    for i in range(1, 7):
        s = slice((i - 1) * 128, (i + 2) * 128)
        put(v1h, v1m, i - 1, dot(bands[i], [v0h[s], v0m[s]], 2))
    for i in range(2, 6):
        s = slice((i - 2) * 128, (i + 1) * 128)
        put(v2h, v2m, i - 2, dot(bands[i], [v1h[s], v1m[s]], 2))
    w0 = [v0h[...], v0m[...]]
    w0i = [v0h[128:896], v0m[128:896]]
    w1 = [v1h[...], v1m[...]]
    w1i = [v1h[128:640], v1m[128:640]]
    w2 = [v2h[...], v2m[...]]
    w2x = [v2h[:, 0:128], v2m[:, 0:128]]
    t0[...] = dot(w0, w0, 2, 0, 0)
    t1[...] = dot(w0i, w1, 2, 0, 0)
    t2[...] = dot(w1, w1, 2, 0, 0)
    t3[...] = dot(w1i, w2, 2, 0, 0)
    t4[...] = dot(w2x, w2, 2, 0, 0)
    half = jnp.concatenate([half_product(ds[i], us[i], v2h, v2m, i - 2) for i in range(2, 5)], axis=0)
    t5[...] = dot([a[0:384] for a in w2x], half, 2, 0, 0)


def inner_call(total, columns, onsite, couplings, x, p):
    return pl.pallas_call(lambda *a: inner_kernel(total, *a), in_specs=[VM] * 5, out_specs=[VM] * 17,
        out_shape=[f32(1024, 128)] + [bf16(8, 128, 128)] * 4 + [bf16(1024, 256)] * 2 + [bf16(768, 256)] * 2 + [bf16(512, 256)] * 2
        + [f32(256, 256)] * 4 + [f32(128, 256), f32(128, 128)], name="inner",
        compiler_params=params(24))(columns, onsite, couplings, x, p)


def outer_kernel(ra, rb, uh, um, dh, dm, v0h, v0m, v1h, v1m, v2h, v2m, t0, t1, t2, t3, t4, t5, own, msg, f1h, f1m, f2h, f2m,
                 e0h, e0m, e1h, e1m, e2h, e2m):
    odd = lax.rem(lax.axis_index("rows"), 2)
    even = odd == 0
    def before(s):
        return jnp.where(even, rb[s], ra[s])
    def after(s):
        return jnp.where(even, ra[s], rb[s])
    def rows(at, n=1):
        return slice(at * 128, (at + n) * 128)
    for i in range(2):
        put(e0h, e0m, i, jnp.concatenate([before(rows(1 + i)), before(rows(3 + i))], axis=1))
    for i in range(3):
        last = after(rows(3 + i)) if i < 2 else jnp.zeros((128, 128), jnp.float32)
        put(e0h, e0m, i + 8, jnp.concatenate([after(rows(i)), last], axis=1))
    for e, v in ((e0h, v0h), (e0m, v0m)):
        e[rows(2, 3)] = v[rows(0, 3)]
        e[rows(5, 3)] = v[rows(5, 3)]
    us = {i: [uh[i], um[i]] for i in range(8)}
    ds = {i: [dh[i], dm[i]] for i in range(8)}
    for i, side, k in ((-2, before, 640), (-1, before, 832), (8, after, 640), (9, after, 832)):
        us[i], ds[i] = [parts(a, 2) for a in unpack_blocks(side(slice(k, k + 128)), side(slice(k + 128, k + 192)))]
    bands = {i: band([a.T for a in us[i - 1]], ds[i], us[i]) for i in (-1, 0, 1, 6, 7, 8, 9)}
    for i, at, src in ((-1, 0, 0), (0, 1, 1), (7, 6, 6), (8, 7, 7), (9, 8, 8)):
        s = rows(src, 3)
        put(e1h, e1m, at, dot(bands[i], [e0h[s], e0m[s]], 2))
    for e, v in ((e1h, v1h), (e1m, v1m)):
        e[rows(2, 2)] = v[rows(0, 2)]
        e[rows(4, 2)] = v[rows(4, 2)]
    for i, at, src in ((0, 0, 0), (1, 1, 1), (6, 4, 4), (7, 5, 5), (8, 6, 6)):
        s = rows(src, 3)
        put(e2h, e2m, at, dot(bands[i], [e1h[s], e1m[s]], 2))
    for e, v in ((e2h, v2h), (e2m, v2m)):
        e[rows(2)] = v[rows(0)]
        e[rows(3)] = v[rows(3)]
    def join(a, b, i, n, j, m):
        return [jnp.concatenate([q[rows(i, n)], q[rows(j, m)]], axis=0) for q in (a, b)]
    w0 = join(v0h, v0m, 0, 1, 7, 1)
    w1 = join(e1h, e1m, 1, 1, 6, 1)
    w1w = join(e1h, e1m, 1, 2, 5, 2)
    w2 = join(e2h, e2m, 0, 2, 4, 2)
    w2x = [a[:, 0:128] for a in w2]
    for f, v in ((f1h, w1[0]), (f1m, w1[1]), (f2h, w2x[0]), (f2m, w2x[1])):
        f[...] = v
    half = jnp.concatenate([half_product(ds[i], us[i], e2h, e2m, at) for i, at in ((0, 0), (1, 1), (5, 3), (6, 4), (7, 5))], axis=0)
    wh = [jnp.concatenate([q[rows(0, 2)], q[rows(3, 3)]], axis=0)[:, 0:128] for q in (e2h, e2m)]
    t = [t0[...], t1[...] + dot(w0, w1, 2, 0, 0), t2[...] + dot(w1, w1, 2, 0, 0), t3[...] + dot(w1w, w2, 2, 0, 0),
         t4[...] + dot(w2x, w2, 2, 0, 0)]
    m5 = t5[...] + dot(wh, half, 2, 0, 0)
    m5 = m5 + m5.T
    row, col = iotas(128, 128)
    pairs = [(b[:128, :128], b[128:, 128:]) for b in t[:4]] + [(t[4][:, :128], m5)]
    ex = [jnp.sum(jnp.where(row == col, b, 0.0), axis=0, keepdims=True) for _, b in pairs]
    ex = jnp.broadcast_to(jnp.concatenate(ex + [jnp.zeros((3, 128), jnp.float32)], axis=0)[None], (16, 8, 128))
    for i, (a, b) in enumerate(pairs):
        c = jnp.where(row <= col, a, b)
        d = t[i][:128, 128:]
        own[:, 8 * i:8 * i + 8] = jnp.where(even, c, d).reshape(16, 8, 128)
        msg[:, 8 * i:8 * i + 8] = jnp.where(even, d, c).reshape(16, 8, 128)
    own[:, 40:48] = ex
    msg[:, 40:48] = ex


def outer_call(*args):
    return pl.pallas_call(outer_kernel, in_specs=[VM] * 18, out_specs=[VM] * 6,
        out_shape=[f32(16, 48, 128)] * 2 + [bf16(256, 256)] * 2 + [bf16(512, 128)] * 2,
        scratch_shapes=[pltpu.VMEM((n * 128, 256), jnp.bfloat16) for n in (11, 11, 9, 9, 7, 7)],
        name="outer", compiler_params=params(24))(*args)


def groups(key):
    found = {}
    for i in range(N):
        found.setdefault(key(i), []).append(i)
    return list(found.values())


def next_chip(block):
    return lax.ppermute(block, "rows", [(i, (i + 1) % N if i % 2 else (i - 1) % N) for i in range(N)])


def across_chip(block):
    return lax.ppermute(block, "rows", [(i, i ^ 1) for i in range(N)])


def in_plane(block):
    return lax.all_to_all(block, "rows", 0, 0, axis_index_groups=groups(lambda i: i % 16))


def along_z(block):
    return lax.all_to_all(block, "rows", 0, 0, axis_index_groups=groups(lambda i: (i // 16, i % 2)))


def copies(block, n):
    return jnp.broadcast_to(block[None], (n,) + block.shape)


def reduce_all(own, msg):
    part = jnp.sum(in_plane(own + across_chip(msg)), axis=0)
    part = jnp.sum(along_z(copies(part, 8)), axis=0)
    own = in_plane(copies(part, 16))
    return own, across_chip(own)


def body(start_states, start_steps, onsite, couplings, columns):
    total = onsite.shape[0] * N
    arrays = (total, columns.T, onsite, couplings, start_states, start_steps)
    from_chip = next_chip(edge_call(*arrays))
    to_core, *made = inner_call(*arrays)
    from_core = across_chip(to_core)
    own, msg, *edges = outer_call(from_core, from_chip, *made)
    mine, other = reduce_all(own, msg)
    return tuple(dense_call(mine, other, *made[4:10], *edges))


def solution(mesh):
    in_specs = (P("rows", None), P("rows", None), P("rows", None, None), P("rows", None, None, None), P("rows", None))
    out_specs = (P("rows", None), P("rows", None))
    return jax.shard_map(body, mesh=mesh, in_specs=in_specs, out_specs=out_specs, check_vma=False)
```

```python
import functools

import jax
import jax.numpy as jnp
from jax import lax
from jax.sharding import PartitionSpec as P
from jax.experimental import pallas as pl
from jax.experimental.pallas import tpu as pltpu

N = 256

def parts(a, n):
    out = []
    for i in range(n):
        h = a.astype(jnp.bfloat16)
        out.append(h)
        if i < n - 1:
            a = a - h.astype(jnp.float32)
    return out

TERMS = {1: [(0, 0)], 2: [(0, 0), (0, 1), (1, 0)], 3: [(0, 0), (0, 1), (1, 0), (1, 1), (0, 2), (2, 0)]}

def square_terms(a, b, cb):
    rows = a[0].shape[0]
    both = lax.dot_general(jnp.concatenate(a[:2], axis=0), jnp.concatenate(b[:2], axis=1 - cb), (((1,), (cb,)), ((), ())),
                           preferred_element_type=jnp.float32)
    return both[:rows, :128] + (both[:rows, 128:] + both[rows:, :128] + both[rows:, 128:])

def dot(a, b, n=2, ca=1, cb=0):
    a = a if isinstance(a, list) else parts(a, n)
    b = b if isinstance(b, list) else parts(b, n)
    if ca == 0:
        a, ca = flipped(a[:n]), 1
    narrow = b[0].shape[1 - cb] == 128
    if n == 2 and narrow:
        return square_terms(a, b, cb)
    lhs = [a[i] for i, _ in TERMS[n]]
    rhs = [b[j] for _, j in TERMS[n]]
    lhs = lhs[0] if n == 1 else jnp.concatenate(lhs, axis=ca)
    rhs = rhs[0] if n == 1 else jnp.concatenate(rhs, axis=cb)
    return lax.dot_general(lhs, rhs, (((ca,), (cb,)), ((), ())), preferred_element_type=jnp.float32)

def flipped(a):
    return [q.T for q in a]

def iotas(n, m):
    return lax.broadcasted_iota(jnp.int32, (n, m), 0), lax.broadcasted_iota(jnp.int32, (n, m), 1)

def newton_factor(g, bad, panel=None, right=None):
    row, col = iotas(128, 128)
    diag = row == col
    weight = jnp.where(row > col, 1.0, jnp.where(diag, 0.5, 0.0))
    dg = jnp.where(diag, g, 0.0)
    dr = lax.rsqrt(jnp.sum(dg, axis=0, keepdims=True))
    dc = lax.rsqrt(jnp.sum(dg, axis=1, keepdims=True))
    one = jnp.where(diag, 1.0, 0.0)
    g = g * dr * dc
    f = jnp.where(row > col, g, 0.0)
    fp = parts(f, 1)
    z = one - f + dot(fp, fp, 1) + weight * dot(fp, fp, 1, 1, 1)
    zp = parts(z, 3)
    e = dot(dot(zp, g, 2), zp, 2, 1, 1) - one
    step = parts(weight * e, 1)
    if panel is not None:
        with_it = dot(panel * dr, zp, 3, 1, 1)
        with_it = with_it - dot(with_it, step, 1, 1, 1)
    if right is not None:
        with_it = dot(zp, right * dc, 2)
        with_it = with_it - dot(step, with_it, 1)
    z = z - dot(step, zp, 1)
    return z * dr, with_it, jnp.maximum(bad, jnp.sum(e * e, axis=0, keepdims=True))

def direct_factor(a_ref, z_ref, g, bad, panel=None, right=None):
    row, col = iotas(128, 128)
    a_ref[...] = g
    z_ref[...] = jnp.where(row == col, 1.0, 0.0)
    def step(j, _):
        r = a_ref[pl.ds(j, 1), :]
        zr = z_ref[pl.ds(j, 1), :]
        a = a_ref[...]
        c = jnp.sum(jnp.where(col == j, a, 0.0), axis=1, keepdims=True)
        d = jnp.sum(jnp.where(col[:1] == j, r, 0.0), axis=1, keepdims=True)
        f = jnp.where(row[:, :1] > j, c / d, 0.0)
        a_ref[...] = a - f * r
        z_ref[...] = z_ref[...] - f * zr
        return 0
    lax.fori_loop(0, 128, step, 0)
    d = jnp.sum(jnp.where(row == col, a_ref[...], 0.0), axis=1, keepdims=True)
    w = z_ref[...] / jnp.sqrt(d)
    return w, dot(w, right, 3) if panel is None else dot(panel, w, 3, 1, 1), bad

def cat(blocks):
    return jnp.concatenate([jnp.concatenate(r, axis=1) for r in blocks], axis=0)

def block_inverse(g, factor, bad):
    w1, l, bad = factor(g[0][0], bad, panel=jnp.concatenate([g[1][0], g[2][0]], axis=0))
    lp = parts(l, 3)
    p = dot(lp, lp, 3, 1, 1)
    w2, l32, bad = factor(g[1][1] - p[:128, :128], bad, panel=g[2][1] - p[128:, :128])
    m = dot(lp, w1)
    a21 = -dot(w2, m[:128])
    l32p = parts(l32, 3)
    t = m[128:] + dot(l32p, a21)
    s = dot(l32p, w2)
    w3, low, bad = factor(g[2][2] - p[128:, 128:] - dot(l32p, l32p, 3, 1, 1), bad, right=jnp.concatenate([t, s], axis=1))
    zero = jnp.zeros((128, 128), jnp.float32)
    return cat([[w1, zero, zero], [a21, w2, zero], [-low[:, :128], -low[:, 128:], w3]]), bad

def projected_filter(inv, a):
    def at(i, n=1):
        return slice(128 * i, 128 * i + 128 * n)
    ip = parts(inv, 2)
    ap = parts(a, 2)
    t = [dot([q[at(i), at(0, i + 1)] for q in ip], [q[at(0, i + 1)] for q in ap]) for i in range(3)]
    tp = parts(jnp.concatenate(t, axis=0), 2)
    c = [dot([q[at(j, 3 - j), at(0, j + 1)] for q in tp], [q[at(j), at(0, j + 1)] for q in ip], 2, 1, 1) for j in range(3)]
    p10, p20, p21 = c[0][at(1)], c[0][at(2)], c[1][at(1)]
    proj = cat([[sym(c[0][at(0)]), p10.T, p20.T], [p10, sym(c[1][at(0)]), p21.T], [p20, p21, sym(c[2])]])
    bound = jnp.max(jnp.sum(jnp.abs(proj), axis=0, keepdims=True), axis=1, keepdims=True)
    row, col = iotas(384, 384)
    s = jnp.where(row == col, 1.0, 0.0) - proj / bound
    sp = parts(s, 2)
    f = dot(sp, [q[:, :128] for q in sp])
    return proj, ip, dot(sp, f)

def back(ip, f):
    fp = parts(f, 2)
    it = flipped([q[128:] for q in ip])
    part = dot(it, [q[128:] for q in fp], 2)
    head = dot([q[:128, :128] for q in ip], [q[:128] for q in fp], 2, 0, 0)
    return jnp.concatenate([jnp.concatenate([part[:128] + head, part[128:]], axis=0), part], axis=1)

def sym(a):
    return 0.5 * (a + a.T)

def small(mk, nk, rk, factor, bad):
    def assemble(k):
        return [[mk[k], mk[k + 1], nk[k]], [mk[k + 1], mk[k + 2], nk[k + 1]], [nk[k].T, nk[k + 1].T, rk[k]]]
    inv, bad = block_inverse(assemble(0), factor, bad)
    proj, ip, f = projected_filter(inv, cat(assemble(1)))
    f2 = jnp.concatenate([jnp.zeros((128, 128), jnp.float32), f[128:]], axis=0)
    ff2 = jnp.concatenate([f, f2], axis=1)
    ffp = parts(ff2, 3)
    fp = [q[:, :128] for q in ffp]
    cq = back(ip, f)
    cqp = parts(cq, 3)
    cp = [q[:, :128] for q in cqp]
    fft, ct = flipped(ffp), flipped(cp)
    gram = dot(fft, ffp, 3)
    one = dot(fft, dot(proj, ffp), 2)
    two = dot(ct, dot(cat(assemble(2)), cqp), 2)
    three = dot(ct, dot(cat(assemble(3)), cp), 2)
    ftf, qq = gram[:128, :128], gram[128:, 128:]
    b1, c1q, q1q = one[:128, :128], one[:128, 128:], one[128:, 128:]
    c2c, c2q = sym(two[:, :128]), two[:, 128:]
    b1 = sym(b1)
    gu = [[ftf, None, None], [b1, c2c, None], [qq, c1q.T, qq]]
    au = cat([[b1, c2c, c1q], [c2c, sym(three), c2q], [c1q.T, c2q.T, sym(q1q)]])
    inv, bad = block_inverse(gu, factor, bad)
    _, ip, f = projected_filter(inv, au)
    fp = parts(f, 3)
    _, y, bad = factor(dot(fp, fp, 3, 0, 0), bad, panel=f)
    k = back(ip, y)
    kb = dot(cqp, jnp.concatenate([k[:128], k[256:]], axis=0))
    kh = dot(cp, k[128:256])
    return jnp.concatenate([kb[:128], kb[128:256] + kh[:128], kh[128:256], kb[256:], kh[256:]], axis=0), bad

def unpack(mine, other):
    row, col = iotas(128, 128)
    even = lax.rem(lax.axis_index("rows"), 2) == 0
    ex = mine[0, 40:48]
    mk, nk, rk = [], [], []
    for i in range(5):
        a, c = [q[:, 8 * i:8 * i + 8].reshape(128, 128) for q in (mine, other)]
        b = jnp.where(even, a, c)
        nk.append(jnp.where(even, c, a))
        bt = b.T
        mk.append(jnp.where(row <= col, b, bt))
        rk.append(jnp.where(row == col, ex[i:i + 1], jnp.where(row <= col, bt, b)))
    mk.append(rk.pop())
    return mk, nk, rk

def dense_kernel(*refs):
    mine, other = refs[:2]
    v0h, v0m, v1h, v1m, v2h, v2m, f1h, f1m, f2h, f2m = refs[2:12]
    states, steps = refs[12:14]
    k_ref, a_ref, z_ref, out_ref, out_sem = refs[14:19]
    res, bad = small(*unpack(mine, other), newton_factor, jnp.zeros((1, 128), jnp.float32))
    k_ref[...] = res
    worst = jnp.sum(bad)
    @pl.when(jnp.logical_not(worst < 4e-5))
    def _():
        k_ref[...] = small(*unpack(mine, other), functools.partial(direct_factor, a_ref, z_ref), None)[0]
    kk = parts(jnp.concatenate([k_ref[0:128], k_ref[384:512], k_ref[128:256], k_ref[512:640], k_ref[256:384]], axis=0), 2)
    def rows(at):
        return slice(128 * at, 128 * at + 128)
    def pair(i, v0, v1, v2, f1, f2):
        one = v1[rows(i - 1)] if 1 <= i <= 6 else f1[rows(i // 7)]
        two = v2[rows(i - 2), 0:128] if 2 <= i <= 5 else f2[rows(i if i < 2 else i - 4)]
        return jnp.concatenate([v0[rows(i)], one, two], axis=1)
    copies = []
    for i in range(4):
        v = [jnp.concatenate([pair(2 * i + j, *q) for j in range(2)], axis=0)
             for q in ((v0h, v1h, v2h, f1h, f2h), (v0m, v1m, v2m, f1m, f2m))]
        out = dot(v, kk, 2)
        for j, ref in enumerate((states, steps)):
            out_ref[j, 256 * i:256 * i + 256] = out[:, 128 * j:128 * j + 128]
            copies.append(pltpu.make_async_copy(out_ref.at[j, 256 * i:256 * i + 256], ref.at[256 * i:256 * i + 256], out_sem.at[len(copies)]))
            copies[-1].start()
    for c in copies:
        c.wait()

def dense_call(mine, other, *kept):
    vm = pl.BlockSpec(memory_space=pltpu.VMEM)
    hbm = pl.BlockSpec(memory_space=pl.ANY)
    square = pltpu.VMEM((128, 128), jnp.float32)
    return pl.pallas_call(dense_kernel, in_specs=[vm] * 12, out_specs=[hbm] * 2,
        out_shape=[jax.ShapeDtypeStruct((1024, 128), jnp.float32)] * 2,
        scratch_shapes=[pltpu.VMEM((640, 256), jnp.float32), square, square, pltpu.VMEM((2, 1024, 128), jnp.float32)]
        + [pltpu.SemaphoreType.DMA((8,))],
        name="dense", compiler_params=pltpu.CompilerParams(vmem_limit_bytes=24 * 2**20))(mine, other, *kept)


VM = pl.BlockSpec(memory_space=pltpu.VMEM)
ANY = pl.BlockSpec(memory_space=pl.ANY)
DMA = pltpu.SemaphoreType.DMA


def f32(*shape):
    return jax.ShapeDtypeStruct(shape, jnp.float32)


def bf16(*shape):
    return jax.ShapeDtypeStruct(shape, jnp.bfloat16)


def params(mib):
    return pltpu.CompilerParams(vmem_limit_bytes=mib * 2**20)


def weights(total, col):
    row = lax.axis_index("rows") * 16 + lax.broadcasted_iota(jnp.int32, (4, 16), 1)
    ahead = lax.rem(col[...] - row + total, total)
    return jnp.where(ahead == 1, 1.0, 0.0), jnp.where(ahead == 2, 1.0, 0.0)


def pair_blocks(one, two, onsite, coup, pair, at):
    def offsets(b, k):
        a1 = jnp.zeros((64, 64), jnp.float32)
        a2 = jnp.zeros((64, 64), jnp.float32)
        for j in range(4):
            c = coup[k, j]
            a1 = a1 + one[j:j + 1, b:b + 1] * c
            a2 = a2 + two[j:j + 1, b:b + 1] * c
        return a1, a2
    a1, a2 = offsets(2 * pair, at)
    b1, b2 = offsets(2 * pair + 1, at + 1)
    o0, o1 = onsite[at], onsite[at + 1]
    u = jnp.concatenate([jnp.concatenate([a2, jnp.zeros((64, 64), jnp.float32)], axis=1), jnp.concatenate([b1, b2], axis=1)], axis=0)
    d = jnp.concatenate([jnp.concatenate([o0 + o0.T, a1], axis=1), jnp.concatenate([a1.T, o1 + o1.T], axis=1)], axis=0)
    return u, d


def packed(u, d):
    row, lane = iotas(128, 128)
    below = jnp.concatenate([d[64:], d[64:]], axis=0)
    return jnp.where((row < 64) & (lane >= 64), below, u), d[:64]


def edge_kernel(total, col, onsite, coup, x, p, out, on_v, co_v, out_v, sem, out_sem):
    odd = lax.rem(lax.axis_index("rows"), 2)
    pairs = [(onsite.at[pl.ds(odd * 12, 4)], on_v), (coup.at[pl.ds(odd * 12, 4)], co_v),
             (x.at[pl.ds(pl.multiple_of(odd * 640, 128), 384)], out_v.at[0:384]),
             (p.at[pl.ds(pl.multiple_of(odd * 768, 128), 256)], out_v.at[384:640])]
    fetch = [pltpu.make_async_copy(a, b, sem.at[i]) for i, (a, b) in enumerate(pairs)]
    store = [pltpu.make_async_copy(out_v.at[s], out.at[s], out_sem.at[i]) for i, s in enumerate((slice(0, 640), slice(640, 1024)))]
    for c in fetch:
        c.start()
    one, two = [jnp.where(odd == 0, w[:, 0:4], w[:, 12:16]) for w in weights(total, col)]
    for c in fetch:
        c.wait()
    store[0].start()
    for i in range(2):
        k = 640 + 192 * i
        out_v[k:k + 128], out_v[k + 128:k + 192] = packed(*pair_blocks(one, two, on_v, co_v, i, 2 * i))
    store[1].start()
    for c in store:
        c.wait()


def unpack_blocks(u, top):
    row, lane = iotas(128, 128)
    low = jnp.concatenate([top[:, 64:].T, u[:64, 64:]], axis=1)
    return jnp.where((row < 64) & (lane >= 64), 0.0, u), jnp.concatenate([top, low], axis=0)


def edge_call(total, columns, onsite, couplings, x, p):
    return pl.pallas_call(lambda *a: edge_kernel(total, *a), in_specs=[VM] + [ANY] * 4, out_specs=ANY, out_shape=f32(1024, 128),
        scratch_shapes=[pltpu.VMEM((4, 64, 64), jnp.float32), pltpu.VMEM((4, 4, 64, 64), jnp.float32),
                        pltpu.VMEM((1024, 128), jnp.float32), DMA((4,)), DMA((2,))], name="edge",
        compiler_params=params(60))(columns, onsite, couplings, x, p)


def put(h, l, at, val):
    a, b = parts(val, 2)
    h[at * 128:at * 128 + 128] = a
    l[at * 128:at * 128 + 128] = b


def band(lower, diag, upper):
    return [jnp.concatenate([lower[k], diag[k], upper[k]], axis=1) for k in range(2)]


def half_product(diag, upper, h, l, at):
    s = slice(at * 128, at * 128 + 256)
    b = [jnp.concatenate([diag[k] * jnp.bfloat16(0.5), upper[k]], axis=1) for k in range(2)]
    return dot(b, [h[s, 0:128], l[s, 0:128]], 2)


def inner_kernel(total, col, onsite, coup, x, p, side, uh, um, dh, dm, v0h, v0m, v1h, v1m, v2h, v2m, t0, t1, t2, t3, t4, t5):
    one, two = weights(total, col)
    even = lax.rem(lax.axis_index("rows"), 2) == 0
    side[0:384] = jnp.where(even, x[640:1024], x[0:384])
    side[384:640] = jnp.where(even, p[768:1024], p[0:256])
    ends = {}
    for i in range(8):
        u, d = pair_blocks(one, two, onsite, coup, i, 2 * i)
        if i not in range(2, 6):
            ends[i] = packed(u, d)
        uh[i], um[i] = parts(u, 2)
        dh[i], dm[i] = parts(d, 2)
        s = slice(128 * i, 128 * i + 128)
        put(v0h, v0m, i, jnp.concatenate([x[s], p[s]], axis=1))
    for i in range(2):
        k = 640 + 192 * i
        side[k:k + 128], side[k + 128:k + 192] = [jnp.where(even, a, b) for a, b in zip(ends[6 + i], ends[i])]
    us = [[uh[i], um[i]] for i in range(8)]
    ds = [[dh[i], dm[i]] for i in range(8)]
    bands = {i: band([a.T for a in us[i - 1]], ds[i], us[i]) for i in range(1, 7)}
    for i in range(1, 7):
        s = slice((i - 1) * 128, (i + 2) * 128)
        put(v1h, v1m, i - 1, dot(bands[i], [v0h[s], v0m[s]], 2))
    for i in range(2, 6):
        s = slice((i - 2) * 128, (i + 1) * 128)
        put(v2h, v2m, i - 2, dot(bands[i], [v1h[s], v1m[s]], 2))
    w0 = [v0h[...], v0m[...]]
    w0i = [v0h[128:896], v0m[128:896]]
    w1 = [v1h[...], v1m[...]]
    w1i = [v1h[128:640], v1m[128:640]]
    w2 = [v2h[...], v2m[...]]
    w2x = [v2h[:, 0:128], v2m[:, 0:128]]
    t0[...] = dot(w0, w0, 2, 0, 0)
    t1[...] = dot(w0i, w1, 2, 0, 0)
    t2[...] = dot(w1, w1, 2, 0, 0)
    t3[...] = dot(w1i, w2, 2, 0, 0)
    t4[...] = dot(w2x, w2, 2, 0, 0)
    half = jnp.concatenate([half_product(ds[i], us[i], v2h, v2m, i - 2) for i in range(2, 5)], axis=0)
    t5[...] = dot([a[0:384] for a in w2x], half, 2, 0, 0)


def inner_call(total, columns, onsite, couplings, x, p):
    return pl.pallas_call(lambda *a: inner_kernel(total, *a), in_specs=[VM] * 5, out_specs=[VM] * 17,
        out_shape=[f32(1024, 128)] + [bf16(8, 128, 128)] * 4 + [bf16(1024, 256)] * 2 + [bf16(768, 256)] * 2 + [bf16(512, 256)] * 2
        + [f32(256, 256)] * 4 + [f32(128, 256), f32(128, 128)], name="inner",
        compiler_params=params(24))(columns, onsite, couplings, x, p)


def outer_kernel(ra, rb, uh, um, dh, dm, v0h, v0m, v1h, v1m, v2h, v2m, t0, t1, t2, t3, t4, t5, own, msg, f1h, f1m, f2h, f2m,
                 e0h, e0m, e1h, e1m, e2h, e2m):
    odd = lax.rem(lax.axis_index("rows"), 2)
    even = odd == 0
    def before(s):
        return jnp.where(even, rb[s], ra[s])
    def after(s):
        return jnp.where(even, ra[s], rb[s])
    def rows(at, n=1):
        return slice(at * 128, (at + n) * 128)
    for i in range(2):
        put(e0h, e0m, i, jnp.concatenate([before(rows(1 + i)), before(rows(3 + i))], axis=1))
    for i in range(3):
        last = after(rows(3 + i)) if i < 2 else jnp.zeros((128, 128), jnp.float32)
        put(e0h, e0m, i + 8, jnp.concatenate([after(rows(i)), last], axis=1))
    for e, v in ((e0h, v0h), (e0m, v0m)):
        e[rows(2, 3)] = v[rows(0, 3)]
        e[rows(5, 3)] = v[rows(5, 3)]
    us = {i: [uh[i], um[i]] for i in range(8)}
    ds = {i: [dh[i], dm[i]] for i in range(8)}
    for i, side, k in ((-2, before, 640), (-1, before, 832), (8, after, 640), (9, after, 832)):
        us[i], ds[i] = [parts(a, 2) for a in unpack_blocks(side(slice(k, k + 128)), side(slice(k + 128, k + 192)))]
    bands = {i: band([a.T for a in us[i - 1]], ds[i], us[i]) for i in (-1, 0, 1, 6, 7, 8, 9)}
    for i, at, src in ((-1, 0, 0), (0, 1, 1), (7, 6, 6), (8, 7, 7), (9, 8, 8)):
        s = rows(src, 3)
        put(e1h, e1m, at, dot(bands[i], [e0h[s], e0m[s]], 2))
    for e, v in ((e1h, v1h), (e1m, v1m)):
        e[rows(2, 2)] = v[rows(0, 2)]
        e[rows(4, 2)] = v[rows(4, 2)]
    for i, at, src in ((0, 0, 0), (1, 1, 1), (6, 4, 4), (7, 5, 5), (8, 6, 6)):
        s = rows(src, 3)
        put(e2h, e2m, at, dot(bands[i], [e1h[s], e1m[s]], 2))
    for e, v in ((e2h, v2h), (e2m, v2m)):
        e[rows(2)] = v[rows(0)]
        e[rows(3)] = v[rows(3)]
    def join(a, b, i, n, j, m):
        return [jnp.concatenate([q[rows(i, n)], q[rows(j, m)]], axis=0) for q in (a, b)]
    w0 = join(v0h, v0m, 0, 1, 7, 1)
    w1 = join(e1h, e1m, 1, 1, 6, 1)
    w1w = join(e1h, e1m, 1, 2, 5, 2)
    w2 = join(e2h, e2m, 0, 2, 4, 2)
    w2x = [a[:, 0:128] for a in w2]
    for f, v in ((f1h, w1[0]), (f1m, w1[1]), (f2h, w2x[0]), (f2m, w2x[1])):
        f[...] = v
    half = jnp.concatenate([half_product(ds[i], us[i], e2h, e2m, at) for i, at in ((0, 0), (1, 1), (5, 3), (6, 4), (7, 5))], axis=0)
    wh = [jnp.concatenate([q[rows(0, 2)], q[rows(3, 3)]], axis=0)[:, 0:128] for q in (e2h, e2m)]
    t = [t0[...], t1[...] + dot(w0, w1, 2, 0, 0), t2[...] + dot(w1, w1, 2, 0, 0), t3[...] + dot(w1w, w2, 2, 0, 0),
         t4[...] + dot(w2x, w2, 2, 0, 0)]
    m5 = t5[...] + dot(wh, half, 2, 0, 0)
    m5 = m5 + m5.T
    row, col = iotas(128, 128)
    pairs = [(b[:128, :128], b[128:, 128:]) for b in t[:4]] + [(t[4][:, :128], m5)]
    ex = [jnp.sum(jnp.where(row == col, b, 0.0), axis=0, keepdims=True) for _, b in pairs]
    ex = jnp.broadcast_to(jnp.concatenate(ex + [jnp.zeros((3, 128), jnp.float32)], axis=0)[None], (16, 8, 128))
    for i, (a, b) in enumerate(pairs):
        c = jnp.where(row <= col, a, b)
        d = t[i][:128, 128:]
        own[:, 8 * i:8 * i + 8] = jnp.where(even, c, d).reshape(16, 8, 128)
        msg[:, 8 * i:8 * i + 8] = jnp.where(even, d, c).reshape(16, 8, 128)
    own[:, 40:48] = ex
    msg[:, 40:48] = ex


def outer_call(*args):
    return pl.pallas_call(outer_kernel, in_specs=[VM] * 18, out_specs=[VM] * 6,
        out_shape=[f32(16, 48, 128)] * 2 + [bf16(256, 256)] * 2 + [bf16(512, 128)] * 2,
        scratch_shapes=[pltpu.VMEM((n * 128, 256), jnp.bfloat16) for n in (11, 11, 9, 9, 7, 7)],
        name="outer", compiler_params=params(24))(*args)


def groups(key):
    found = {}
    for i in range(N):
        found.setdefault(key(i), []).append(i)
    return list(found.values())


def next_chip(block):
    return lax.ppermute(block, "rows", [(i, (i + 1) % N if i % 2 else (i - 1) % N) for i in range(N)])


def across_chip(block):
    return lax.ppermute(block, "rows", [(i, i ^ 1) for i in range(N)])


def in_plane(block):
    return lax.all_to_all(block, "rows", 0, 0, axis_index_groups=groups(lambda i: i % 16))


def along_z(block):
    return lax.all_to_all(block, "rows", 0, 0, axis_index_groups=groups(lambda i: (i // 16, i % 2)))


def copies(block, n):
    return jnp.broadcast_to(block[None], (n,) + block.shape)


def reduce_all(own, msg):
    part = jnp.sum(in_plane(own + across_chip(msg)), axis=0)
    part = jnp.sum(along_z(copies(part, 8)), axis=0)
    own = in_plane(copies(part, 16))
    return own, across_chip(own)


def body(start_states, start_steps, onsite, couplings, columns):
    total = onsite.shape[0] * N
    arrays = (total, columns.T, onsite, couplings, start_states, start_steps)
    from_chip = next_chip(edge_call(*arrays))
    to_core, *made = inner_call(*arrays)
    from_core = across_chip(to_core)
    own, msg, *edges = outer_call(from_core, from_chip, *made)
    mine, other = reduce_all(own, msg)
    return tuple(dense_call(mine, other, *made[4:10], *edges))


def solution(mesh):
    in_specs = (P("rows", None), P("rows", None), P("rows", None, None), P("rows", None, None, None), P("rows", None))
    out_specs = (P("rows", None), P("rows", None))
    return jax.shard_map(body, mesh=mesh, in_specs=in_specs, out_specs=out_specs, check_vma=False)
```

```python
import functools

import jax
import jax.numpy as jnp
from jax import lax
from jax.sharding import PartitionSpec as P
from jax.experimental import pallas as pl
from jax.experimental.pallas import tpu as pltpu

N = 256

def parts(a, n):
    out = []
    for i in range(n):
        h = a.astype(jnp.bfloat16)
        out.append(h)
        if i < n - 1:
            a = a - h.astype(jnp.float32)
    return out

TERMS = {1: [(0, 0)], 2: [(0, 0), (0, 1), (1, 0)], 3: [(0, 0), (0, 1), (1, 0), (1, 1), (0, 2), (2, 0)]}

def square_terms(a, b, cb):
    rows = a[0].shape[0]
    both = lax.dot_general(jnp.concatenate(a[:2], axis=0), jnp.concatenate(b[:2], axis=1 - cb), (((1,), (cb,)), ((), ())),
                           preferred_element_type=jnp.float32)
    return both[:rows, :128] + (both[:rows, 128:] + both[rows:, :128] + both[rows:, 128:])

def dot(a, b, n=2, ca=1, cb=0):
    a = a if isinstance(a, list) else parts(a, n)
    b = b if isinstance(b, list) else parts(b, n)
    if ca == 0:
        a, ca = flipped(a[:n]), 1
    narrow = b[0].shape[1 - cb] == 128
    if n == 2 and narrow:
        return square_terms(a, b, cb)
    lhs = [a[i] for i, _ in TERMS[n]]
    rhs = [b[j] for _, j in TERMS[n]]
    lhs = lhs[0] if n == 1 else jnp.concatenate(lhs, axis=ca)
    rhs = rhs[0] if n == 1 else jnp.concatenate(rhs, axis=cb)
    return lax.dot_general(lhs, rhs, (((ca,), (cb,)), ((), ())), preferred_element_type=jnp.float32)

def flipped(a):
    return [q.T for q in a]

def iotas(n, m):
    return lax.broadcasted_iota(jnp.int32, (n, m), 0), lax.broadcasted_iota(jnp.int32, (n, m), 1)

def newton_factor(g, bad, panel=None, right=None):
    row, col = iotas(128, 128)
    diag = row == col
    weight = jnp.where(row > col, 1.0, jnp.where(diag, 0.5, 0.0))
    dg = jnp.where(diag, g, 0.0)
    dr = lax.rsqrt(jnp.sum(dg, axis=0, keepdims=True))
    dc = lax.rsqrt(jnp.sum(dg, axis=1, keepdims=True))
    one = jnp.where(diag, 1.0, 0.0)
    g = g * dr * dc
    f = jnp.where(row > col, g, 0.0)
    fp = parts(f, 1)
    z = one - f + dot(fp, fp, 1) + weight * dot(fp, fp, 1, 1, 1)
    zp = parts(z, 3)
    e = dot(dot(zp, g, 2), zp, 2, 1, 1) - one
    step = parts(weight * e, 1)
    if panel is not None:
        with_it = dot(panel * dr, zp, 3, 1, 1)
        with_it = with_it - dot(with_it, step, 1, 1, 1)
    if right is not None:
        with_it = dot(zp, right * dc, 2)
        with_it = with_it - dot(step, with_it, 1)
    z = z - dot(step, zp, 1)
    return z * dr, with_it, jnp.maximum(bad, jnp.sum(e * e, axis=0, keepdims=True))

def direct_factor(a_ref, z_ref, g, bad, panel=None, right=None):
    row, col = iotas(128, 128)
    a_ref[...] = g
    z_ref[...] = jnp.where(row == col, 1.0, 0.0)
    def step(j, _):
        r = a_ref[pl.ds(j, 1), :]
        zr = z_ref[pl.ds(j, 1), :]
        a = a_ref[...]
        c = jnp.sum(jnp.where(col == j, a, 0.0), axis=1, keepdims=True)
        d = jnp.sum(jnp.where(col[:1] == j, r, 0.0), axis=1, keepdims=True)
        f = jnp.where(row[:, :1] > j, c / d, 0.0)
        a_ref[...] = a - f * r
        z_ref[...] = z_ref[...] - f * zr
        return 0
    lax.fori_loop(0, 128, step, 0)
    d = jnp.sum(jnp.where(row == col, a_ref[...], 0.0), axis=1, keepdims=True)
    w = z_ref[...] / jnp.sqrt(d)
    return w, dot(w, right, 3) if panel is None else dot(panel, w, 3, 1, 1), bad

def cat(blocks):
    return jnp.concatenate([jnp.concatenate(r, axis=1) for r in blocks], axis=0)

def block_inverse(g, factor, bad):
    w1, l, bad = factor(g[0][0], bad, panel=jnp.concatenate([g[1][0], g[2][0]], axis=0))
    lp = parts(l, 3)
    p = dot(lp, lp, 3, 1, 1)
    w2, l32, bad = factor(g[1][1] - p[:128, :128], bad, panel=g[2][1] - p[128:, :128])
    m = dot(lp, w1)
    a21 = -dot(w2, m[:128])
    l32p = parts(l32, 3)
    t = m[128:] + dot(l32p, a21)
    s = dot(l32p, w2)
    w3, low, bad = factor(g[2][2] - p[128:, 128:] - dot(l32p, l32p, 3, 1, 1), bad, right=jnp.concatenate([t, s], axis=1))
    zero = jnp.zeros((128, 128), jnp.float32)
    return cat([[w1, zero, zero], [a21, w2, zero], [-low[:, :128], -low[:, 128:], w3]]), bad

def projected_filter(inv, a):
    def at(i, n=1):
        return slice(128 * i, 128 * i + 128 * n)
    ip = parts(inv, 2)
    ap = parts(a, 2)
    t = [dot([q[at(i), at(0, i + 1)] for q in ip], [q[at(0, i + 1)] for q in ap]) for i in range(3)]
    tp = parts(jnp.concatenate(t, axis=0), 2)
    c = [dot([q[at(j, 3 - j), at(0, j + 1)] for q in tp], [q[at(j), at(0, j + 1)] for q in ip], 2, 1, 1) for j in range(3)]
    p10, p20, p21 = c[0][at(1)], c[0][at(2)], c[1][at(1)]
    proj = cat([[sym(c[0][at(0)]), p10.T, p20.T], [p10, sym(c[1][at(0)]), p21.T], [p20, p21, sym(c[2])]])
    bound = jnp.max(jnp.sum(jnp.abs(proj), axis=0, keepdims=True), axis=1, keepdims=True)
    row, col = iotas(384, 384)
    s = jnp.where(row == col, 1.0, 0.0) - proj / bound
    sp = parts(s, 2)
    f = dot(sp, [q[:, :128] for q in sp])
    return proj, ip, dot(sp, f)

def back(ip, f):
    fp = parts(f, 2)
    it = flipped([q[128:] for q in ip])
    part = dot(it, [q[128:] for q in fp], 2)
    head = dot([q[:128, :128] for q in ip], [q[:128] for q in fp], 2, 0, 0)
    return jnp.concatenate([jnp.concatenate([part[:128] + head, part[128:]], axis=0), part], axis=1)

def sym(a):
    return 0.5 * (a + a.T)

def small(mk, nk, rk, factor, bad):
    def assemble(k):
        return [[mk[k], mk[k + 1], nk[k]], [mk[k + 1], mk[k + 2], nk[k + 1]], [nk[k].T, nk[k + 1].T, rk[k]]]
    inv, bad = block_inverse(assemble(0), factor, bad)
    proj, ip, f = projected_filter(inv, cat(assemble(1)))
    f2 = jnp.concatenate([jnp.zeros((128, 128), jnp.float32), f[128:]], axis=0)
    ff2 = jnp.concatenate([f, f2], axis=1)
    ffp = parts(ff2, 3)
    fp = [q[:, :128] for q in ffp]
    cq = back(ip, f)
    cqp = parts(cq, 3)
    cp = [q[:, :128] for q in cqp]
    fft, ct = flipped(ffp), flipped(cp)
    gram = dot(fft, ffp, 3)
    one = dot(fft, dot(proj, ffp), 2)
    two = dot(ct, dot(cat(assemble(2)), cqp), 2)
    three = dot(ct, dot(cat(assemble(3)), cp), 2)
    ftf, qq = gram[:128, :128], gram[128:, 128:]
    b1, c1q, q1q = one[:128, :128], one[:128, 128:], one[128:, 128:]
    c2c, c2q = sym(two[:, :128]), two[:, 128:]
    b1 = sym(b1)
    gu = [[ftf, None, None], [b1, c2c, None], [qq, c1q.T, qq]]
    au = cat([[b1, c2c, c1q], [c2c, sym(three), c2q], [c1q.T, c2q.T, sym(q1q)]])
    inv, bad = block_inverse(gu, factor, bad)
    _, ip, f = projected_filter(inv, au)
    fp = parts(f, 3)
    _, y, bad = factor(dot(fp, fp, 3, 0, 0), bad, panel=f)
    k = back(ip, y)
    kb = dot(cqp, jnp.concatenate([k[:128], k[256:]], axis=0))
    kh = dot(cp, k[128:256])
    return jnp.concatenate([kb[:128], kb[128:256] + kh[:128], kh[128:256], kb[256:], kh[256:]], axis=0), bad

def unpack(mine, other):
    row, col = iotas(128, 128)
    even = lax.rem(lax.axis_index("rows"), 2) == 0
    ex = mine[0, 40:48]
    mk, nk, rk = [], [], []
    for i in range(5):
        a, c = [q[:, 8 * i:8 * i + 8].reshape(128, 128) for q in (mine, other)]
        b = jnp.where(even, a, c)
        nk.append(jnp.where(even, c, a))
        bt = b.T
        mk.append(jnp.where(row <= col, b, bt))
        rk.append(jnp.where(row == col, ex[i:i + 1], jnp.where(row <= col, bt, b)))
    mk.append(rk.pop())
    return mk, nk, rk

def dense_kernel(*refs):
    mine, other = refs[:2]
    v0h, v0m, v1h, v1m, v2h, v2m, f1h, f1m, f2h, f2m = refs[2:12]
    states, steps = refs[12:14]
    k_ref, a_ref, z_ref, out_ref, out_sem = refs[14:19]
    res, bad = small(*unpack(mine, other), newton_factor, jnp.zeros((1, 128), jnp.float32))
    k_ref[...] = res
    worst = jnp.sum(bad)
    @pl.when(jnp.logical_not(worst < 4e-5))
    def _():
        k_ref[...] = small(*unpack(mine, other), functools.partial(direct_factor, a_ref, z_ref), None)[0]
    kk = parts(jnp.concatenate([k_ref[0:128], k_ref[384:512], k_ref[128:256], k_ref[512:640], k_ref[256:384]], axis=0), 2)
    def rows(at):
        return slice(128 * at, 128 * at + 128)
    def pair(i, v0, v1, v2, f1, f2):
        one = v1[rows(i - 1)] if 1 <= i <= 6 else f1[rows(i // 7)]
        two = v2[rows(i - 2), 0:128] if 2 <= i <= 5 else f2[rows(i if i < 2 else i - 4)]
        return jnp.concatenate([v0[rows(i)], one, two], axis=1)
    copies = []
    for i in range(4):
        v = [jnp.concatenate([pair(2 * i + j, *q) for j in range(2)], axis=0)
             for q in ((v0h, v1h, v2h, f1h, f2h), (v0m, v1m, v2m, f1m, f2m))]
        out = dot(v, kk, 2)
        for j, ref in enumerate((states, steps)):
            out_ref[j, 256 * i:256 * i + 256] = out[:, 128 * j:128 * j + 128]
            copies.append(pltpu.make_async_copy(out_ref.at[j, 256 * i:256 * i + 256], ref.at[256 * i:256 * i + 256], out_sem.at[len(copies)]))
            copies[-1].start()
    for c in copies:
        c.wait()

def dense_call(mine, other, *kept):
    vm = pl.BlockSpec(memory_space=pltpu.VMEM)
    hbm = pl.BlockSpec(memory_space=pl.ANY)
    square = pltpu.VMEM((128, 128), jnp.float32)
    return pl.pallas_call(dense_kernel, in_specs=[vm] * 12, out_specs=[hbm] * 2,
        out_shape=[jax.ShapeDtypeStruct((1024, 128), jnp.float32)] * 2,
        scratch_shapes=[pltpu.VMEM((640, 256), jnp.float32), square, square, pltpu.VMEM((2, 1024, 128), jnp.float32)]
        + [pltpu.SemaphoreType.DMA((8,))],
        name="dense", compiler_params=pltpu.CompilerParams(vmem_limit_bytes=24 * 2**20))(mine, other, *kept)


VM = pl.BlockSpec(memory_space=pltpu.VMEM)
ANY = pl.BlockSpec(memory_space=pl.ANY)
DMA = pltpu.SemaphoreType.DMA


def f32(*shape):
    return jax.ShapeDtypeStruct(shape, jnp.float32)


def bf16(*shape):
    return jax.ShapeDtypeStruct(shape, jnp.bfloat16)


def params(mib):
    return pltpu.CompilerParams(vmem_limit_bytes=mib * 2**20)


def weights(total, col):
    row = lax.axis_index("rows") * 16 + lax.broadcasted_iota(jnp.int32, (4, 16), 1)
    ahead = lax.rem(col[...] - row + total, total)
    return jnp.where(ahead == 1, 1.0, 0.0), jnp.where(ahead == 2, 1.0, 0.0)


def pair_blocks(one, two, onsite, coup, pair, at):
    def offsets(b, k):
        a1 = jnp.zeros((64, 64), jnp.float32)
        a2 = jnp.zeros((64, 64), jnp.float32)
        for j in range(4):
            c = coup[k, j]
            a1 = a1 + one[j:j + 1, b:b + 1] * c
            a2 = a2 + two[j:j + 1, b:b + 1] * c
        return a1, a2
    a1, a2 = offsets(2 * pair, at)
    b1, b2 = offsets(2 * pair + 1, at + 1)
    o0, o1 = onsite[at], onsite[at + 1]
    u = jnp.concatenate([jnp.concatenate([a2, jnp.zeros((64, 64), jnp.float32)], axis=1), jnp.concatenate([b1, b2], axis=1)], axis=0)
    d = jnp.concatenate([jnp.concatenate([o0 + o0.T, a1], axis=1), jnp.concatenate([a1.T, o1 + o1.T], axis=1)], axis=0)
    return u, d


def edge_kernel(total, col, onsite, coup, x, p, out, on_v, co_v, x_v, p_v, third, out_v, sem, out_sem):
    odd = lax.rem(lax.axis_index("rows"), 2)
    even = odd == 0
    pairs = [(onsite.at[pl.ds(odd * 12, 4)], on_v), (coup.at[pl.ds(odd * 12, 4)], co_v),
             (x.at[pl.ds(pl.multiple_of(odd * 768, 128), 256)], x_v), (p.at[pl.ds(pl.multiple_of(odd * 768, 128), 256)], p_v),
             (x.at[256:384], third)]
    fetch = [pltpu.make_async_copy(a, b, sem.at[i]) for i, (a, b) in enumerate(pairs)]
    for c in fetch:
        c.start()
    one, two = [jnp.where(even, w[:, 0:4], w[:, 12:16]) for w in weights(total, col)]
    for c in fetch:
        c.wait()
    outermost = pl.ds(pl.multiple_of(odd * 128, 128), 128)
    out_v[0:128] = x_v[outermost]
    out_v[128:256] = p_v[outermost]
    ua, da = pair_blocks(one, two, on_v, co_v, 0, 0)
    ub, db = pair_blocks(one, two, on_v, co_v, 1, 2)
    out_v[512:640] = jnp.where(even, da, ub)
    x01 = x_v[...]
    w = dot(jnp.concatenate([jnp.where(even, da, ua.T), jnp.where(even, ua, db)], axis=1), jnp.concatenate([x01, p_v[...]], axis=1), 2)
    out_v[256:384], out_v[384:512] = w[:, :128], w[:, 128:]
    store = [pltpu.make_async_copy(out_v.at[s], out.at[s], out_sem.at[i]) for i, s in enumerate((slice(0, 640), slice(640, 768)))]
    store[0].start()
    hx = dot(jnp.concatenate([ua.T, db, ub], axis=1), jnp.concatenate([x01, third[...]], axis=0), 2)
    out_v[640:768] = dot(ua, hx, 2)
    store[1].start()
    for c in store:
        c.wait()


def edge_call(total, columns, onsite, couplings, x, p):
    def scratch(*shape):
        return pltpu.VMEM(shape, jnp.float32)
    return pl.pallas_call(lambda *a: edge_kernel(total, *a), in_specs=[VM] + [ANY] * 4, out_specs=ANY, out_shape=f32(768, 128),
        scratch_shapes=[scratch(4, 64, 64), scratch(4, 4, 64, 64), scratch(256, 128), scratch(256, 128), scratch(128, 128),
                        scratch(768, 128), DMA((5,)), DMA((2,))], name="edge",
        compiler_params=params(60))(columns, onsite, couplings, x, p)


def put(h, l, at, val):
    a, b = parts(val, 2)
    h[at * 128:at * 128 + 128] = a
    l[at * 128:at * 128 + 128] = b


def band(lower, diag, upper):
    return [jnp.concatenate([lower[k], diag[k], upper[k]], axis=1) for k in range(2)]


def half_product(diag, upper, h, l, at):
    s = slice(at * 128, at * 128 + 256)
    b = [jnp.concatenate([diag[k] * jnp.bfloat16(0.5), upper[k]], axis=1) for k in range(2)]
    return dot(b, [h[s, 0:128], l[s, 0:128]], 2)


def inner_kernel(total, col, onsite, coup, x, p, side, uh, um, dh, dm, v0h, v0m, v1h, v1m, v2h, v2m, t0, t1, t2, t3, t4, t5):
    one, two = weights(total, col)
    even = lax.rem(lax.axis_index("rows"), 2) == 0
    side[0:128] = jnp.where(even, x[896:1024], x[0:128])
    side[128:256] = jnp.where(even, p[896:1024], p[0:128])
    for i in range(8):
        u, d = pair_blocks(one, two, onsite, coup, i, 2 * i)
        if i == 0:
            d0 = d
        if i == 7:
            side[512:640] = jnp.where(even, u, d0)
        uh[i], um[i] = parts(u, 2)
        dh[i], dm[i] = parts(d, 2)
        s = slice(128 * i, 128 * i + 128)
        put(v0h, v0m, i, jnp.concatenate([x[s], p[s]], axis=1))
    us = [[uh[i], um[i]] for i in range(8)]
    ds = [[dh[i], dm[i]] for i in range(8)]
    bands = {i: band([a.T for a in us[i - 1]], ds[i], us[i]) for i in range(1, 7)}
    for i in range(1, 7):
        s = slice((i - 1) * 128, (i + 2) * 128)
        put(v1h, v1m, i - 1, dot(bands[i], [v0h[s], v0m[s]], 2))
    for i in range(2, 6):
        s = slice((i - 2) * 128, (i + 1) * 128)
        put(v2h, v2m, i - 2, dot(bands[i], [v1h[s], v1m[s]], 2))
    first = dot([jnp.concatenate([a, b], axis=1) for a, b in zip(ds[0], us[0])], [v0h[0:256], v0m[0:256]], 2)
    last = dot([jnp.concatenate([a.T, b], axis=1) for a, b in zip(us[6], ds[7])], [v0h[768:1024], v0m[768:1024]], 2)
    w = jnp.where(even, last, first)
    side[256:384], side[384:512] = w[:, :128], w[:, 128:]
    side[640:768] = dot(us[0], [v1h[0:128, 0:128], v1m[0:128, 0:128]], 2)
    w0 = [v0h[...], v0m[...]]
    w0i = [v0h[128:896], v0m[128:896]]
    w1 = [v1h[...], v1m[...]]
    w1i = [v1h[128:640], v1m[128:640]]
    w2 = [v2h[...], v2m[...]]
    w2x = [v2h[:, 0:128], v2m[:, 0:128]]
    t0[...] = dot(w0, w0, 2, 0, 0)
    t1[...] = dot(w0i, w1, 2, 0, 0)
    t2[...] = dot(w1, w1, 2, 0, 0)
    t3[...] = dot(w1i, w2, 2, 0, 0)
    t4[...] = dot(w2x, w2, 2, 0, 0)
    half = jnp.concatenate([half_product(ds[i], us[i], v2h, v2m, i - 2) for i in range(2, 5)], axis=0)
    t5[...] = dot([a[0:384] for a in w2x], half, 2, 0, 0)


def inner_call(total, columns, onsite, couplings, x, p):
    return pl.pallas_call(lambda *a: inner_kernel(total, *a), in_specs=[VM] * 5, out_specs=[VM] * 17,
        out_shape=[f32(768, 128)] + [bf16(8, 128, 128)] * 4 + [bf16(1024, 256)] * 2 + [bf16(768, 256)] * 2 + [bf16(512, 256)] * 2
        + [f32(256, 256)] * 4 + [f32(128, 256), f32(128, 128)], name="inner",
        compiler_params=params(24))(columns, onsite, couplings, x, p)


def outer_kernel(ra, rb, uh, um, dh, dm, v0h, v0m, v1h, v1m, v2h, v2m, t0, t1, t2, t3, t4, t5, own, msg, f1h, f1m, f2h, f2m,
                 e0h, e0m, e1h, e1m, e2h, e2m):
    odd = lax.rem(lax.axis_index("rows"), 2)
    even = odd == 0
    def before(s):
        return jnp.where(even, rb[s], ra[s])
    def after(s):
        return jnp.where(even, ra[s], rb[s])
    def rows(at, n=1):
        return slice(at * 128, (at + n) * 128)
    def wide(side, at):
        return jnp.concatenate([side(rows(at)), side(rows(at + 1))], axis=1)
    put(e0h, e0m, 0, wide(before, 0))
    put(e0h, e0m, 5, wide(after, 0))
    for e, v in ((e0h, v0h), (e0m, v0m)):
        e[rows(1, 2)] = v[rows(0, 2)]
        e[rows(3, 2)] = v[rows(6, 2)]
    us = {i: [uh[i], um[i]] for i in range(8)}
    ds = {i: [dh[i], dm[i]] for i in range(8)}
    us[-1] = parts(before(rows(4)), 2)
    ds[8] = parts(after(rows(4)), 2)
    ut = {i: [a.T for a in us[i]] for i in (-1, 0, 5, 6, 7)}
    bands = {i: band(ut[i - 1], ds[i], us[i]) for i in (0, 1, 6, 7)}
    put(e1h, e1m, 0, wide(before, 2) + dot(us[-1], [v0h[rows(0)], v0m[rows(0)]], 2))
    put(e1h, e1m, 7, wide(after, 2) + dot(ut[7], [v0h[rows(7)], v0m[rows(7)]], 2))
    for i, at, src in ((0, 1, 0), (7, 6, 3)):
        s = rows(src, 3)
        put(e1h, e1m, at, dot(bands[i], [e0h[s], e0m[s]], 2))
    for e, v in ((e1h, v1h), (e1m, v1m)):
        e[rows(2, 2)] = v[rows(0, 2)]
        e[rows(4, 2)] = v[rows(4, 2)]
    for i, at, src in ((0, 0, 0), (1, 1, 1), (6, 4, 4), (7, 5, 5)):
        s = rows(src, 3)
        put(e2h, e2m, at, dot(bands[i], [e1h[s], e1m[s]], 2))
    eight = after(rows(5)) + dot([jnp.concatenate([a, b], axis=1) for a, b in zip(ut[7], ds[8])], [e[rows(6, 2), 0:128] for e in (e1h, e1m)], 2)
    put(e2h, e2m, 6, jnp.concatenate([eight, jnp.zeros((128, 128), jnp.float32)], axis=1))
    for e, v in ((e2h, v2h), (e2m, v2m)):
        e[rows(2)] = v[rows(0)]
        e[rows(3)] = v[rows(3)]
    def join(a, b, i, n, j, m):
        return [jnp.concatenate([q[rows(i, n)], q[rows(j, m)]], axis=0) for q in (a, b)]
    w0 = join(v0h, v0m, 0, 1, 7, 1)
    w1 = join(e1h, e1m, 1, 1, 6, 1)
    w1w = join(e1h, e1m, 1, 2, 5, 2)
    w2 = join(e2h, e2m, 0, 2, 4, 2)
    w2x = [a[:, 0:128] for a in w2]
    for f, v in ((f1h, w1[0]), (f1m, w1[1]), (f2h, w2x[0]), (f2m, w2x[1])):
        f[...] = v
    half = jnp.concatenate([half_product(ds[i], us[i], e2h, e2m, at) for i, at in ((0, 0), (1, 1), (5, 3), (6, 4), (7, 5))], axis=0)
    wh = [jnp.concatenate([q[rows(0, 2)], q[rows(3, 3)]], axis=0)[:, 0:128] for q in (e2h, e2m)]
    t = [t0[...], t1[...] + dot(w0, w1, 2, 0, 0), t2[...] + dot(w1, w1, 2, 0, 0), t3[...] + dot(w1w, w2, 2, 0, 0),
         t4[...] + dot(w2x, w2, 2, 0, 0)]
    m5 = t5[...] + dot(wh, half, 2, 0, 0)
    m5 = m5 + m5.T
    row, col = iotas(128, 128)
    pairs = [(b[:128, :128], b[128:, 128:]) for b in t[:4]] + [(t[4][:, :128], m5)]
    ex = [jnp.sum(jnp.where(row == col, b, 0.0), axis=0, keepdims=True) for _, b in pairs]
    ex = jnp.broadcast_to(jnp.concatenate(ex + [jnp.zeros((3, 128), jnp.float32)], axis=0)[None], (16, 8, 128))
    for i, (a, b) in enumerate(pairs):
        c = jnp.where(row <= col, a, b)
        d = t[i][:128, 128:]
        own[:, 8 * i:8 * i + 8] = jnp.where(even, c, d).reshape(16, 8, 128)
        msg[:, 8 * i:8 * i + 8] = jnp.where(even, d, c).reshape(16, 8, 128)
    own[:, 40:48] = ex
    msg[:, 40:48] = ex


def outer_call(*args):
    return pl.pallas_call(outer_kernel, in_specs=[VM] * 18, out_specs=[VM] * 6,
        out_shape=[f32(16, 48, 128)] * 2 + [bf16(256, 256)] * 2 + [bf16(512, 128)] * 2,
        scratch_shapes=[pltpu.VMEM((n * 128, 256), jnp.bfloat16) for n in (6, 6, 8, 8, 7, 7)],
        name="outer", compiler_params=params(24))(*args)


def groups(key):
    found = {}
    for i in range(N):
        found.setdefault(key(i), []).append(i)
    return list(found.values())


def next_chip(block):
    return lax.ppermute(block, "rows", [(i, (i + 1) % N if i % 2 else (i - 1) % N) for i in range(N)])


def across_chip(block):
    return lax.ppermute(block, "rows", [(i, i ^ 1) for i in range(N)])


def in_plane(block):
    return lax.all_to_all(block, "rows", 0, 0, axis_index_groups=groups(lambda i: i % 16))


def along_z(block):
    return lax.all_to_all(block, "rows", 0, 0, axis_index_groups=groups(lambda i: (i // 16, i % 2)))


def copies(block, n):
    return jnp.broadcast_to(block[None], (n,) + block.shape)


def reduce_all(own, msg):
    part = jnp.sum(in_plane(own + across_chip(msg)), axis=0)
    part = jnp.sum(along_z(copies(part, 8)), axis=0)
    own = in_plane(copies(part, 16))
    return own, across_chip(own)


def body(start_states, start_steps, onsite, couplings, columns):
    total = onsite.shape[0] * N
    arrays = (total, columns.T, onsite, couplings, start_states, start_steps)
    from_chip = next_chip(edge_call(*arrays))
    to_core, *made = inner_call(*arrays)
    from_core = across_chip(to_core)
    own, msg, *edges = outer_call(from_core, from_chip, *made)
    mine, other = reduce_all(own, msg)
    return tuple(dense_call(mine, other, *made[4:10], *edges))


def solution(mesh):
    in_specs = (P("rows", None), P("rows", None), P("rows", None, None), P("rows", None, None, None), P("rows", None))
    out_specs = (P("rows", None), P("rows", None))
    return jax.shard_map(body, mesh=mesh, in_specs=in_specs, out_specs=out_specs, check_vma=False)
```

```python
import functools

import jax
import jax.numpy as jnp
from jax import lax
from jax.sharding import PartitionSpec as P
from jax.experimental import pallas as pl
from jax.experimental.pallas import tpu as pltpu

N = 256

def parts(a, n):
    out = []
    for i in range(n):
        h = a.astype(jnp.bfloat16)
        out.append(h)
        if i < n - 1:
            a = a - h.astype(jnp.float32)
    return out

TERMS = {1: [(0, 0)], 2: [(0, 0), (0, 1), (1, 0)], 3: [(0, 0), (0, 1), (1, 0), (1, 1), (0, 2), (2, 0)]}

def square_terms(a, b, cb):
    rows = a[0].shape[0]
    both = lax.dot_general(jnp.concatenate(a[:2], axis=0), jnp.concatenate(b[:2], axis=1 - cb), (((1,), (cb,)), ((), ())),
                           preferred_element_type=jnp.float32)
    return both[:rows, :128] + (both[:rows, 128:] + both[rows:, :128] + both[rows:, 128:])

def dot(a, b, n=2, ca=1, cb=0):
    a = a if isinstance(a, list) else parts(a, n)
    b = b if isinstance(b, list) else parts(b, n)
    if ca == 0:
        a, ca = flipped(a[:n]), 1
    narrow = b[0].shape[1 - cb] == 128
    if n == 2 and narrow:
        return square_terms(a, b, cb)
    lhs = [a[i] for i, _ in TERMS[n]]
    rhs = [b[j] for _, j in TERMS[n]]
    lhs = lhs[0] if n == 1 else jnp.concatenate(lhs, axis=ca)
    rhs = rhs[0] if n == 1 else jnp.concatenate(rhs, axis=cb)
    return lax.dot_general(lhs, rhs, (((ca,), (cb,)), ((), ())), preferred_element_type=jnp.float32)

def flipped(a):
    return [q.T for q in a]

def iotas(n, m):
    return lax.broadcasted_iota(jnp.int32, (n, m), 0), lax.broadcasted_iota(jnp.int32, (n, m), 1)

def newton_factor(g, bad, panel=None, right=None):
    row, col = iotas(128, 128)
    diag = row == col
    weight = jnp.where(row > col, 1.0, jnp.where(diag, 0.5, 0.0))
    dg = jnp.where(diag, g, 0.0)
    dr = lax.rsqrt(jnp.sum(dg, axis=0, keepdims=True))
    dc = lax.rsqrt(jnp.sum(dg, axis=1, keepdims=True))
    one = jnp.where(diag, 1.0, 0.0)
    g = g * dr * dc
    f = jnp.where(row > col, g, 0.0)
    fp = parts(f, 1)
    z = one - f + dot(fp, fp, 1) + weight * dot(fp, fp, 1, 1, 1)
    zp = parts(z, 3)
    e = dot(dot(zp, g, 2), zp, 2, 1, 1) - one
    step = parts(weight * e, 1)
    if panel is not None:
        with_it = dot(panel * dr, zp, 3, 1, 1)
        with_it = with_it - dot(with_it, step, 1, 1, 1)
    if right is not None:
        with_it = dot(zp, right * dc, 2)
        with_it = with_it - dot(step, with_it, 1)
    z = z - dot(step, zp, 1)
    return z * dr, with_it, jnp.maximum(bad, jnp.sum(e * e, axis=0, keepdims=True))

def direct_factor(a_ref, z_ref, g, bad, panel=None, right=None):
    row, col = iotas(128, 128)
    a_ref[...] = g
    z_ref[...] = jnp.where(row == col, 1.0, 0.0)
    def step(j, _):
        r = a_ref[pl.ds(j, 1), :]
        zr = z_ref[pl.ds(j, 1), :]
        a = a_ref[...]
        c = jnp.sum(jnp.where(col == j, a, 0.0), axis=1, keepdims=True)
        d = jnp.sum(jnp.where(col[:1] == j, r, 0.0), axis=1, keepdims=True)
        f = jnp.where(row[:, :1] > j, c / d, 0.0)
        a_ref[...] = a - f * r
        z_ref[...] = z_ref[...] - f * zr
        return 0
    lax.fori_loop(0, 128, step, 0)
    d = jnp.sum(jnp.where(row == col, a_ref[...], 0.0), axis=1, keepdims=True)
    w = z_ref[...] / jnp.sqrt(d)
    return w, dot(w, right, 3) if panel is None else dot(panel, w, 3, 1, 1), bad

def cat(blocks):
    return jnp.concatenate([jnp.concatenate(r, axis=1) for r in blocks], axis=0)

def block_inverse(g, factor, bad):
    w1, l, bad = factor(g[0][0], bad, panel=jnp.concatenate([g[1][0], g[2][0]], axis=0))
    lp = parts(l, 3)
    p = dot(lp, lp, 3, 1, 1)
    w2, l32, bad = factor(g[1][1] - p[:128, :128], bad, panel=g[2][1] - p[128:, :128])
    m = dot(lp, w1)
    a21 = -dot(w2, m[:128])
    l32p = parts(l32, 3)
    t = m[128:] + dot(l32p, a21)
    s = dot(l32p, w2)
    w3, low, bad = factor(g[2][2] - p[128:, 128:] - dot(l32p, l32p, 3, 1, 1), bad, right=jnp.concatenate([t, s], axis=1))
    zero = jnp.zeros((128, 128), jnp.float32)
    return cat([[w1, zero, zero], [a21, w2, zero], [-low[:, :128], -low[:, 128:], w3]]), bad

def projected_filter(inv, a):
    def at(i, n=1):
        return slice(128 * i, 128 * i + 128 * n)
    ip = parts(inv, 2)
    ap = parts(a, 2)
    t = [dot([q[at(i), at(0, i + 1)] for q in ip], [q[at(0, i + 1)] for q in ap]) for i in range(3)]
    tp = parts(jnp.concatenate(t, axis=0), 2)
    c = [dot([q[at(j, 3 - j), at(0, j + 1)] for q in tp], [q[at(j), at(0, j + 1)] for q in ip], 2, 1, 1) for j in range(3)]
    p10, p20, p21 = c[0][at(1)], c[0][at(2)], c[1][at(1)]
    proj = cat([[sym(c[0][at(0)]), p10.T, p20.T], [p10, sym(c[1][at(0)]), p21.T], [p20, p21, sym(c[2])]])
    bound = jnp.max(jnp.sum(jnp.abs(proj), axis=0, keepdims=True), axis=1, keepdims=True)
    pp = parts(proj, 2)
    second = dot(pp, [q[:, :128] for q in pp])
    third = dot(pp, second)
    scale = 1.0 / bound
    row, col = iotas(384, 128)
    f = jnp.where(row == col, 1.0, 0.0) - scale * (3.0 * proj[:, :128] - scale * (3.0 * second - scale * third))
    return pp, ip, f

def back(ip, f):
    fp = parts(f, 2)
    it = flipped([q[128:] for q in ip])
    part = dot(it, [q[128:] for q in fp], 2)
    head = dot([q[:128, :128] for q in ip], [q[:128] for q in fp], 2, 0, 0)
    return jnp.concatenate([jnp.concatenate([part[:128] + head, part[128:]], axis=0), part], axis=1)

def sym(a):
    return 0.5 * (a + a.T)

def small(mk, nk, rk, factor, bad):
    def assemble(k):
        return [[mk[k], mk[k + 1], nk[k]], [mk[k + 1], mk[k + 2], nk[k + 1]], [nk[k].T, nk[k + 1].T, rk[k]]]
    inv, bad = block_inverse(assemble(0), factor, bad)
    pp, ip, f = projected_filter(inv, cat(assemble(1)))
    f2 = jnp.concatenate([jnp.zeros((128, 128), jnp.float32), f[128:]], axis=0)
    ff2 = jnp.concatenate([f, f2], axis=1)
    ffp = parts(ff2, 3)
    fp = [q[:, :128] for q in ffp]
    cq = back(ip, f)
    cqp = parts(cq, 3)
    cp = [q[:, :128] for q in cqp]
    fft, ct = flipped(ffp), flipped(cp)
    gram = dot(fft, ffp, 3)
    one = dot(fft, dot(pp, ffp), 2)
    two = dot(ct, dot(cat(assemble(2)), cqp), 2)
    three = dot(ct, dot(cat(assemble(3)), cp), 2)
    ftf, qq = gram[:128, :128], gram[128:, 128:]
    b1, c1q, q1q = one[:128, :128], one[:128, 128:], one[128:, 128:]
    c2c, c2q = sym(two[:, :128]), two[:, 128:]
    b1 = sym(b1)
    gu = [[ftf, None, None], [b1, c2c, None], [qq, c1q.T, qq]]
    au = cat([[b1, c2c, c1q], [c2c, sym(three), c2q], [c1q.T, c2q.T, sym(q1q)]])
    inv, bad = block_inverse(gu, factor, bad)
    _, ip, f = projected_filter(inv, au)
    fp = parts(f, 3)
    _, y, bad = factor(dot(fp, fp, 3, 0, 0), bad, panel=f)
    k = back(ip, y)
    kb = dot(cqp, jnp.concatenate([k[:128], k[256:]], axis=0))
    kh = dot(cp, k[128:256])
    return jnp.concatenate([kb[:128], kb[128:256] + kh[:128], kh[128:256], kb[256:], kh[256:]], axis=0), bad

def unpack(mine, other):
    row, col = iotas(128, 128)
    even = lax.rem(lax.axis_index("rows"), 2) == 0
    ex = mine[0, 40:48]
    mk, nk, rk = [], [], []
    for i in range(5):
        a, c = [q[:, 8 * i:8 * i + 8].reshape(128, 128) for q in (mine, other)]
        b = jnp.where(even, a, c)
        nk.append(jnp.where(even, c, a))
        bt = b.T
        mk.append(jnp.where(row <= col, b, bt))
        rk.append(jnp.where(row == col, ex[i:i + 1], jnp.where(row <= col, bt, b)))
    mk.append(rk.pop())
    return mk, nk, rk

def dense_kernel(*refs):
    mine, other = refs[:2]
    v0h, v0m, v1h, v1m, v2h, v2m, f1h, f1m, f2h, f2m = refs[2:12]
    states, steps = refs[12:14]
    k_ref, a_ref, z_ref, out_ref, out_sem = refs[14:19]
    res, bad = small(*unpack(mine, other), newton_factor, jnp.zeros((1, 128), jnp.float32))
    k_ref[...] = res
    worst = jnp.sum(bad)
    @pl.when(jnp.logical_not(worst < 4e-5))
    def _():
        k_ref[...] = small(*unpack(mine, other), functools.partial(direct_factor, a_ref, z_ref), None)[0]
    kk = parts(jnp.concatenate([k_ref[0:128], k_ref[384:512], k_ref[128:256], k_ref[512:640], k_ref[256:384]], axis=0), 2)
    def rows(at):
        return slice(128 * at, 128 * at + 128)
    def pair(i, v0, v1, v2, f1, f2):
        one = v1[rows(i - 1)] if 1 <= i <= 6 else f1[rows(i // 7)]
        two = v2[rows(i - 2), 0:128] if 2 <= i <= 5 else f2[rows(i if i < 2 else i - 4)]
        return jnp.concatenate([v0[rows(i)], one, two], axis=1)
    copies = []
    for i in range(4):
        v = [jnp.concatenate([pair(2 * i + j, *q) for j in range(2)], axis=0)
             for q in ((v0h, v1h, v2h, f1h, f2h), (v0m, v1m, v2m, f1m, f2m))]
        out = dot(v, kk, 2)
        for j, ref in enumerate((states, steps)):
            out_ref[j, 256 * i:256 * i + 256] = out[:, 128 * j:128 * j + 128]
            copies.append(pltpu.make_async_copy(out_ref.at[j, 256 * i:256 * i + 256], ref.at[256 * i:256 * i + 256], out_sem.at[len(copies)]))
            copies[-1].start()
    for c in copies:
        c.wait()

def dense_call(mine, other, *kept):
    vm = pl.BlockSpec(memory_space=pltpu.VMEM)
    hbm = pl.BlockSpec(memory_space=pl.ANY)
    square = pltpu.VMEM((128, 128), jnp.float32)
    return pl.pallas_call(dense_kernel, in_specs=[vm] * 12, out_specs=[hbm] * 2,
        out_shape=[jax.ShapeDtypeStruct((1024, 128), jnp.float32)] * 2,
        scratch_shapes=[pltpu.VMEM((640, 256), jnp.float32), square, square, pltpu.VMEM((2, 1024, 128), jnp.float32)]
        + [pltpu.SemaphoreType.DMA((8,))],
        name="dense", compiler_params=pltpu.CompilerParams(vmem_limit_bytes=24 * 2**20))(mine, other, *kept)


VM = pl.BlockSpec(memory_space=pltpu.VMEM)
ANY = pl.BlockSpec(memory_space=pl.ANY)
DMA = pltpu.SemaphoreType.DMA


def f32(*shape):
    return jax.ShapeDtypeStruct(shape, jnp.float32)


def bf16(*shape):
    return jax.ShapeDtypeStruct(shape, jnp.bfloat16)


def params(mib):
    return pltpu.CompilerParams(vmem_limit_bytes=mib * 2**20)


def weights(total, col):
    row = lax.axis_index("rows") * 16 + lax.broadcasted_iota(jnp.int32, (4, 16), 1)
    ahead = lax.rem(col[...] - row + total, total)
    return jnp.where(ahead == 1, 1.0, 0.0), jnp.where(ahead == 2, 1.0, 0.0)


def pair_blocks(one, two, onsite, coup, pair, at):
    def offsets(b, k):
        a1 = jnp.zeros((64, 64), jnp.float32)
        a2 = jnp.zeros((64, 64), jnp.float32)
        for j in range(4):
            c = coup[k, j]
            a1 = a1 + one[j:j + 1, b:b + 1] * c
            a2 = a2 + two[j:j + 1, b:b + 1] * c
        return a1, a2
    a1, a2 = offsets(2 * pair, at)
    b1, b2 = offsets(2 * pair + 1, at + 1)
    o0, o1 = onsite[at], onsite[at + 1]
    u = jnp.concatenate([jnp.concatenate([a2, jnp.zeros((64, 64), jnp.float32)], axis=1), jnp.concatenate([b1, b2], axis=1)], axis=0)
    d = jnp.concatenate([jnp.concatenate([o0 + o0.T, a1], axis=1), jnp.concatenate([a1.T, o1 + o1.T], axis=1)], axis=0)
    return u, d


def edge_kernel(total, col, onsite, coup, x, p, out, on_v, co_v, x_v, p_v, third, out_v, sem, out_sem):
    odd = lax.rem(lax.axis_index("rows"), 2)
    even = odd == 0
    pairs = [(onsite.at[pl.ds(odd * 12, 4)], on_v), (coup.at[pl.ds(odd * 12, 4)], co_v),
             (x.at[pl.ds(pl.multiple_of(odd * 768, 128), 256)], x_v), (p.at[pl.ds(pl.multiple_of(odd * 768, 128), 256)], p_v),
             (x.at[256:384], third)]
    fetch = [pltpu.make_async_copy(a, b, sem.at[i]) for i, (a, b) in enumerate(pairs)]
    for c in fetch:
        c.start()
    one, two = [jnp.where(even, w[:, 0:4], w[:, 12:16]) for w in weights(total, col)]
    for c in fetch:
        c.wait()
    outermost = pl.ds(pl.multiple_of(odd * 128, 128), 128)
    out_v[0:128] = x_v[outermost]
    out_v[128:256] = p_v[outermost]
    ua, da = pair_blocks(one, two, on_v, co_v, 0, 0)
    ub, db = pair_blocks(one, two, on_v, co_v, 1, 2)
    out_v[512:640] = jnp.where(even, da, ub)
    x01 = x_v[...]
    w = dot(jnp.concatenate([jnp.where(even, da, ua.T), jnp.where(even, ua, db)], axis=1), jnp.concatenate([x01, p_v[...]], axis=1), 2)
    out_v[256:384], out_v[384:512] = w[:, :128], w[:, 128:]
    store = [pltpu.make_async_copy(out_v.at[s], out.at[s], out_sem.at[i]) for i, s in enumerate((slice(0, 640), slice(640, 768)))]
    store[0].start()
    hx = dot(jnp.concatenate([ua.T, db, ub], axis=1), jnp.concatenate([x01, third[...]], axis=0), 2)
    out_v[640:768] = dot(ua, hx, 2)
    store[1].start()
    for c in store:
        c.wait()


def edge_call(total, columns, onsite, couplings, x, p):
    def scratch(*shape):
        return pltpu.VMEM(shape, jnp.float32)
    return pl.pallas_call(lambda *a: edge_kernel(total, *a), in_specs=[VM] + [ANY] * 4, out_specs=ANY, out_shape=f32(768, 128),
        scratch_shapes=[scratch(4, 64, 64), scratch(4, 4, 64, 64), scratch(256, 128), scratch(256, 128), scratch(128, 128),
                        scratch(768, 128), DMA((5,)), DMA((2,))], name="edge",
        compiler_params=params(60))(columns, onsite, couplings, x, p)


def put(h, l, at, val):
    a, b = parts(val, 2)
    h[at * 128:at * 128 + 128] = a
    l[at * 128:at * 128 + 128] = b


def band(lower, diag, upper):
    return [jnp.concatenate([lower[k], diag[k], upper[k]], axis=1) for k in range(2)]


def half_product(diag, upper, h, l, at):
    s = slice(at * 128, at * 128 + 256)
    b = [jnp.concatenate([diag[k] * jnp.bfloat16(0.5), upper[k]], axis=1) for k in range(2)]
    return dot(b, [h[s, 0:128], l[s, 0:128]], 2)


def inner_kernel(total, col, onsite, coup, x, p, side, uh, um, dh, dm, v0h, v0m, v1h, v1m, v2h, v2m, t0, t1, t2, t3, t4, t5):
    one, two = weights(total, col)
    even = lax.rem(lax.axis_index("rows"), 2) == 0
    side[0:128] = jnp.where(even, x[896:1024], x[0:128])
    side[128:256] = jnp.where(even, p[896:1024], p[0:128])
    for i in range(8):
        u, d = pair_blocks(one, two, onsite, coup, i, 2 * i)
        if i == 0:
            d0 = d
        if i == 7:
            side[512:640] = jnp.where(even, u, d0)
        uh[i], um[i] = parts(u, 2)
        dh[i], dm[i] = parts(d, 2)
        s = slice(128 * i, 128 * i + 128)
        put(v0h, v0m, i, jnp.concatenate([x[s], p[s]], axis=1))
    us = [[uh[i], um[i]] for i in range(8)]
    ds = [[dh[i], dm[i]] for i in range(8)]
    bands = {i: band([a.T for a in us[i - 1]], ds[i], us[i]) for i in range(1, 7)}
    for i in range(1, 7):
        s = slice((i - 1) * 128, (i + 2) * 128)
        put(v1h, v1m, i - 1, dot(bands[i], [v0h[s], v0m[s]], 2))
    for i in range(2, 6):
        s = slice((i - 2) * 128, (i + 1) * 128)
        put(v2h, v2m, i - 2, dot(bands[i], [v1h[s], v1m[s]], 2))
    first = dot([jnp.concatenate([a, b], axis=1) for a, b in zip(ds[0], us[0])], [v0h[0:256], v0m[0:256]], 2)
    last = dot([jnp.concatenate([a.T, b], axis=1) for a, b in zip(us[6], ds[7])], [v0h[768:1024], v0m[768:1024]], 2)
    w = jnp.where(even, last, first)
    side[256:384], side[384:512] = w[:, :128], w[:, 128:]
    side[640:768] = dot(us[0], [v1h[0:128, 0:128], v1m[0:128, 0:128]], 2)
    w0 = [v0h[...], v0m[...]]
    w0i = [v0h[128:896], v0m[128:896]]
    w1 = [v1h[...], v1m[...]]
    w1i = [v1h[128:640], v1m[128:640]]
    w2 = [v2h[...], v2m[...]]
    w2x = [v2h[:, 0:128], v2m[:, 0:128]]
    t0[...] = dot(w0, w0, 2, 0, 0)
    t1[...] = dot(w0i, w1, 2, 0, 0)
    t2[...] = dot(w1, w1, 2, 0, 0)
    t3[...] = dot(w1i, w2, 2, 0, 0)
    t4[...] = dot(w2x, w2, 2, 0, 0)
    half = jnp.concatenate([half_product(ds[i], us[i], v2h, v2m, i - 2) for i in range(2, 5)], axis=0)
    t5[...] = dot([a[0:384] for a in w2x], half, 2, 0, 0)


def inner_call(total, columns, onsite, couplings, x, p):
    return pl.pallas_call(lambda *a: inner_kernel(total, *a), in_specs=[VM] * 5, out_specs=[VM] * 17,
        out_shape=[f32(768, 128)] + [bf16(8, 128, 128)] * 4 + [bf16(1024, 256)] * 2 + [bf16(768, 256)] * 2 + [bf16(512, 256)] * 2
        + [f32(256, 256)] * 4 + [f32(128, 256), f32(128, 128)], name="inner",
        compiler_params=params(24))(columns, onsite, couplings, x, p)


def outer_kernel(ra, rb, uh, um, dh, dm, v0h, v0m, v1h, v1m, v2h, v2m, t0, t1, t2, t3, t4, t5, own, msg, f1h, f1m, f2h, f2m,
                 e0h, e0m, e1h, e1m, e2h, e2m):
    odd = lax.rem(lax.axis_index("rows"), 2)
    even = odd == 0
    def before(s):
        return jnp.where(even, rb[s], ra[s])
    def after(s):
        return jnp.where(even, ra[s], rb[s])
    def rows(at, n=1):
        return slice(at * 128, (at + n) * 128)
    def wide(side, at):
        return jnp.concatenate([side(rows(at)), side(rows(at + 1))], axis=1)
    put(e0h, e0m, 0, wide(before, 0))
    put(e0h, e0m, 5, wide(after, 0))
    for e, v in ((e0h, v0h), (e0m, v0m)):
        e[rows(1, 2)] = v[rows(0, 2)]
        e[rows(3, 2)] = v[rows(6, 2)]
    us = {i: [uh[i], um[i]] for i in range(8)}
    ds = {i: [dh[i], dm[i]] for i in range(8)}
    us[-1] = parts(before(rows(4)), 2)
    ds[8] = parts(after(rows(4)), 2)
    ut = {i: [a.T for a in us[i]] for i in (-1, 0, 5, 6, 7)}
    bands = {i: band(ut[i - 1], ds[i], us[i]) for i in (0, 1, 6, 7)}
    put(e1h, e1m, 0, wide(before, 2) + dot(us[-1], [v0h[rows(0)], v0m[rows(0)]], 2))
    put(e1h, e1m, 7, wide(after, 2) + dot(ut[7], [v0h[rows(7)], v0m[rows(7)]], 2))
    for i, at, src in ((0, 1, 0), (7, 6, 3)):
        s = rows(src, 3)
        put(e1h, e1m, at, dot(bands[i], [e0h[s], e0m[s]], 2))
    for e, v in ((e1h, v1h), (e1m, v1m)):
        e[rows(2, 2)] = v[rows(0, 2)]
        e[rows(4, 2)] = v[rows(4, 2)]
    for i, at, src in ((0, 0, 0), (1, 1, 1), (6, 4, 4), (7, 5, 5)):
        s = rows(src, 3)
        put(e2h, e2m, at, dot(bands[i], [e1h[s], e1m[s]], 2))
    eight = after(rows(5)) + dot([jnp.concatenate([a, b], axis=1) for a, b in zip(ut[7], ds[8])], [e[rows(6, 2), 0:128] for e in (e1h, e1m)], 2)
    put(e2h, e2m, 6, jnp.concatenate([eight, jnp.zeros((128, 128), jnp.float32)], axis=1))
    for e, v in ((e2h, v2h), (e2m, v2m)):
        e[rows(2)] = v[rows(0)]
        e[rows(3)] = v[rows(3)]
    def join(a, b, i, n, j, m):
        return [jnp.concatenate([q[rows(i, n)], q[rows(j, m)]], axis=0) for q in (a, b)]
    w0 = join(v0h, v0m, 0, 1, 7, 1)
    w1 = join(e1h, e1m, 1, 1, 6, 1)
    w1w = join(e1h, e1m, 1, 2, 5, 2)
    w2 = join(e2h, e2m, 0, 2, 4, 2)
    w2x = [a[:, 0:128] for a in w2]
    for f, v in ((f1h, w1[0]), (f1m, w1[1]), (f2h, w2x[0]), (f2m, w2x[1])):
        f[...] = v
    half = jnp.concatenate([half_product(ds[i], us[i], e2h, e2m, at) for i, at in ((0, 0), (1, 1), (5, 3), (6, 4), (7, 5))], axis=0)
    wh = [jnp.concatenate([q[rows(0, 2)], q[rows(3, 3)]], axis=0)[:, 0:128] for q in (e2h, e2m)]
    t = [t0[...], t1[...] + dot(w0, w1, 2, 0, 0), t2[...] + dot(w1, w1, 2, 0, 0), t3[...] + dot(w1w, w2, 2, 0, 0),
         t4[...] + dot(w2x, w2, 2, 0, 0)]
    m5 = t5[...] + dot(wh, half, 2, 0, 0)
    m5 = m5 + m5.T
    row, col = iotas(128, 128)
    pairs = [(b[:128, :128], b[128:, 128:]) for b in t[:4]] + [(t[4][:, :128], m5)]
    ex = [jnp.sum(jnp.where(row == col, b, 0.0), axis=0, keepdims=True) for _, b in pairs]
    ex = jnp.broadcast_to(jnp.concatenate(ex + [jnp.zeros((3, 128), jnp.float32)], axis=0)[None], (16, 8, 128))
    for i, (a, b) in enumerate(pairs):
        c = jnp.where(row <= col, a, b)
        d = t[i][:128, 128:]
        own[:, 8 * i:8 * i + 8] = jnp.where(even, c, d).reshape(16, 8, 128)
        msg[:, 8 * i:8 * i + 8] = jnp.where(even, d, c).reshape(16, 8, 128)
    own[:, 40:48] = ex
    msg[:, 40:48] = ex


def outer_call(*args):
    return pl.pallas_call(outer_kernel, in_specs=[VM] * 18, out_specs=[VM] * 6,
        out_shape=[f32(16, 48, 128)] * 2 + [bf16(256, 256)] * 2 + [bf16(512, 128)] * 2,
        scratch_shapes=[pltpu.VMEM((n * 128, 256), jnp.bfloat16) for n in (6, 6, 8, 8, 7, 7)],
        name="outer", compiler_params=params(24))(*args)


def groups(key):
    found = {}
    for i in range(N):
        found.setdefault(key(i), []).append(i)
    return list(found.values())


def next_chip(block):
    return lax.ppermute(block, "rows", [(i, (i + 1) % N if i % 2 else (i - 1) % N) for i in range(N)])


def across_chip(block):
    return lax.ppermute(block, "rows", [(i, i ^ 1) for i in range(N)])


def in_plane(block):
    return lax.all_to_all(block, "rows", 0, 0, axis_index_groups=groups(lambda i: i % 16))


def along_z(block):
    return lax.all_to_all(block, "rows", 0, 0, axis_index_groups=groups(lambda i: (i // 16, i % 2)))


def copies(block, n):
    return jnp.broadcast_to(block[None], (n,) + block.shape)


def reduce_all(own, msg):
    part = jnp.sum(in_plane(own + across_chip(msg)), axis=0)
    part = jnp.sum(along_z(copies(part, 8)), axis=0)
    own = in_plane(copies(part, 16))
    return own, across_chip(own)


def body(start_states, start_steps, onsite, couplings, columns):
    total = onsite.shape[0] * N
    arrays = (total, columns.T, onsite, couplings, start_states, start_steps)
    from_chip = next_chip(edge_call(*arrays))
    to_core, *made = inner_call(*arrays)
    from_core = across_chip(to_core)
    own, msg, *edges = outer_call(from_core, from_chip, *made)
    mine, other = reduce_all(own, msg)
    return tuple(dense_call(mine, other, *made[4:10], *edges))


def solution(mesh):
    in_specs = (P("rows", None), P("rows", None), P("rows", None, None), P("rows", None, None, None), P("rows", None))
    out_specs = (P("rows", None), P("rows", None))
    return jax.shard_map(body, mesh=mesh, in_specs=in_specs, out_specs=out_specs, check_vma=False)
```

```python
import functools

import jax
import jax.numpy as jnp
from jax import lax
from jax.sharding import PartitionSpec as P
from jax.experimental import pallas as pl
from jax.experimental.pallas import tpu as pltpu

N = 256

def parts(a, n):
    out = []
    for i in range(n):
        h = a.astype(jnp.bfloat16)
        out.append(h)
        if i < n - 1:
            a = a - h.astype(jnp.float32)
    return out

TERMS = {1: [(0, 0)], 2: [(0, 0), (0, 1), (1, 0)], 3: [(0, 0), (0, 1), (1, 0), (1, 1), (0, 2), (2, 0)]}

def square_terms(a, b, cb):
    rows = a[0].shape[0]
    both = lax.dot_general(jnp.concatenate(a[:2], axis=0), jnp.concatenate(b[:2], axis=1 - cb), (((1,), (cb,)), ((), ())),
                           preferred_element_type=jnp.float32)
    return both[:rows, :128] + (both[:rows, 128:] + both[rows:, :128] + both[rows:, 128:])

def dot(a, b, n=2, ca=1, cb=0):
    a = a if isinstance(a, list) else parts(a, n)
    b = b if isinstance(b, list) else parts(b, n)
    if ca == 0:
        a, ca = flipped(a[:n]), 1
    narrow = b[0].shape[1 - cb] == 128
    if n == 2 and narrow:
        return square_terms(a, b, cb)
    lhs = [a[i] for i, _ in TERMS[n]]
    rhs = [b[j] for _, j in TERMS[n]]
    lhs = lhs[0] if n == 1 else jnp.concatenate(lhs, axis=ca)
    rhs = rhs[0] if n == 1 else jnp.concatenate(rhs, axis=cb)
    return lax.dot_general(lhs, rhs, (((ca,), (cb,)), ((), ())), preferred_element_type=jnp.float32)

def flipped(a):
    return [q.T for q in a]

def iotas(n, m):
    return lax.broadcasted_iota(jnp.int32, (n, m), 0), lax.broadcasted_iota(jnp.int32, (n, m), 1)

def newton_factor(g, bad, panel=None, right=None):
    row, col = iotas(128, 128)
    diag = row == col
    weight = jnp.where(row > col, 1.0, jnp.where(diag, 0.5, 0.0))
    dg = jnp.where(diag, g, 0.0)
    dr = lax.rsqrt(jnp.sum(dg, axis=0, keepdims=True))
    dc = lax.rsqrt(jnp.sum(dg, axis=1, keepdims=True))
    one = jnp.where(diag, 1.0, 0.0)
    g = g * dr * dc
    f = jnp.where(row > col, g, 0.0)
    fp = parts(f, 1)
    z = one - f + dot(fp, fp, 1) + weight * dot(fp, fp, 1, 1, 1)
    zp = parts(z, 3)
    e = dot(dot(zp, g, 2), zp, 2, 1, 1) - one
    step = parts(weight * e, 1)
    if panel is not None:
        with_it = dot(panel * dr, zp, 3, 1, 1)
        with_it = with_it - dot(with_it, step, 1, 1, 1)
    if right is not None:
        with_it = dot(zp, right * dc, 2)
        with_it = with_it - dot(step, with_it, 1)
    z = z - dot(step, zp, 1)
    return z * dr, with_it, jnp.maximum(bad, jnp.sum(e * e, axis=0, keepdims=True))

def direct_factor(a_ref, z_ref, g, bad, panel=None, right=None):
    row, col = iotas(128, 128)
    a_ref[...] = g
    z_ref[...] = jnp.where(row == col, 1.0, 0.0)
    def step(j, _):
        r = a_ref[pl.ds(j, 1), :]
        zr = z_ref[pl.ds(j, 1), :]
        a = a_ref[...]
        c = jnp.sum(jnp.where(col == j, a, 0.0), axis=1, keepdims=True)
        d = jnp.sum(jnp.where(col[:1] == j, r, 0.0), axis=1, keepdims=True)
        f = jnp.where(row[:, :1] > j, c / d, 0.0)
        a_ref[...] = a - f * r
        z_ref[...] = z_ref[...] - f * zr
        return 0
    lax.fori_loop(0, 128, step, 0)
    d = jnp.sum(jnp.where(row == col, a_ref[...], 0.0), axis=1, keepdims=True)
    w = z_ref[...] / jnp.sqrt(d)
    return w, dot(w, right, 3) if panel is None else dot(panel, w, 3, 1, 1), bad

def cat(blocks):
    return jnp.concatenate([jnp.concatenate(r, axis=1) for r in blocks], axis=0)

def block_inverse(g, factor, bad):
    w1, l, bad = factor(g[0][0], bad, panel=jnp.concatenate([g[1][0], g[2][0]], axis=0))
    lp = parts(l, 3)
    p = dot(lp, lp, 3, 1, 1)
    w2, l32, bad = factor(g[1][1] - p[:128, :128], bad, panel=g[2][1] - p[128:, :128])
    m = dot(lp, w1)
    a21 = -dot(w2, m[:128])
    l32p = parts(l32, 3)
    t = m[128:] + dot(l32p, a21)
    s = dot(l32p, w2)
    w3, low, bad = factor(g[2][2] - p[128:, 128:] - dot(l32p, l32p, 3, 1, 1), bad, right=jnp.concatenate([t, s], axis=1))
    zero = jnp.zeros((128, 128), jnp.float32)
    return cat([[w1, zero, zero], [a21, w2, zero], [-low[:, :128], -low[:, 128:], w3]]), bad

def projected_filter(inv, a):
    def at(i, n=1):
        return slice(128 * i, 128 * i + 128 * n)
    ip = parts(inv, 2)
    ap = parts(a, 2)
    t = [dot([q[at(i), at(0, i + 1)] for q in ip], [q[at(0, i + 1)] for q in ap]) for i in range(3)]
    tp = parts(jnp.concatenate(t, axis=0), 2)
    c = [dot([q[at(j, 3 - j), at(0, j + 1)] for q in tp], [q[at(j), at(0, j + 1)] for q in ip], 2, 1, 1) for j in range(3)]
    p10, p20, p21 = c[0][at(1)], c[0][at(2)], c[1][at(1)]
    proj = cat([[sym(c[0][at(0)]), p10.T, p20.T], [p10, sym(c[1][at(0)]), p21.T], [p20, p21, sym(c[2])]])
    bound = jnp.max(jnp.sum(jnp.abs(proj), axis=0, keepdims=True), axis=1, keepdims=True)
    pp = parts(proj, 2)
    second = dot(pp, [q[:, :128] for q in pp])
    third = dot(pp, second)
    scale = 1.0 / bound
    row, col = iotas(384, 128)
    f = jnp.where(row == col, 1.0, 0.0) - scale * (3.0 * proj[:, :128] - scale * (3.0 * second - scale * third))
    return pp, ip, f

def back(ip, f):
    fp = parts(f, 2)
    it = flipped([q[128:] for q in ip])
    part = dot(it, [q[128:] for q in fp], 2)
    head = dot([q[:128, :128] for q in ip], [q[:128] for q in fp], 2, 0, 0)
    return jnp.concatenate([jnp.concatenate([part[:128] + head, part[128:]], axis=0), part], axis=1)

def sym(a):
    return 0.5 * (a + a.T)

def small(mk, nk, rk, factor, bad):
    def assemble(k):
        return [[mk[k], mk[k + 1], nk[k]], [mk[k + 1], mk[k + 2], nk[k + 1]], [nk[k].T, nk[k + 1].T, rk[k]]]
    inv, bad = block_inverse(assemble(0), factor, bad)
    pp, ip, f = projected_filter(inv, cat(assemble(1)))
    f2 = jnp.concatenate([jnp.zeros((128, 128), jnp.float32), f[128:]], axis=0)
    ff2 = jnp.concatenate([f, f2], axis=1)
    ffp = parts(ff2, 3)
    fp = [q[:, :128] for q in ffp]
    cq = back(ip, f)
    cqp = parts(cq, 3)
    cp = [q[:, :128] for q in cqp]
    fft, ct = flipped(ffp), flipped(cp)
    gram = dot(fft, ffp, 3)
    one = dot(fft, dot(pp, ffp), 2)
    two = dot(ct, dot(cat(assemble(2)), cqp), 2)
    three = dot(ct, dot(cat(assemble(3)), cp), 2)
    ftf, qq = gram[:128, :128], gram[128:, 128:]
    b1, c1q, q1q = one[:128, :128], one[:128, 128:], one[128:, 128:]
    c2c, c2q = sym(two[:, :128]), two[:, 128:]
    b1 = sym(b1)
    gu = [[ftf, None, None], [b1, c2c, None], [qq, c1q.T, qq]]
    au = cat([[b1, c2c, c1q], [c2c, sym(three), c2q], [c1q.T, c2q.T, sym(q1q)]])
    inv, bad = block_inverse(gu, factor, bad)
    _, ip, f = projected_filter(inv, au)
    fp = parts(f, 3)
    _, y, bad = factor(dot(fp, fp, 3, 0, 0), bad, panel=f)
    k = back(ip, y)
    kb = dot(cqp, jnp.concatenate([k[:128], k[256:]], axis=0))
    kh = dot(cp, k[128:256])
    return jnp.concatenate([kb[:128], kb[128:256] + kh[:128], kh[128:256], kb[256:], kh[256:]], axis=0), bad

def unpack(mine, other):
    row, col = iotas(128, 128)
    even = lax.rem(lax.axis_index("rows"), 2) == 0
    ex = mine[0, 40:48]
    mk, nk, rk = [], [], []
    for i in range(5):
        a, c = [q[:, 8 * i:8 * i + 8].reshape(128, 128) for q in (mine, other)]
        b = jnp.where(even, a, c)
        nk.append(jnp.where(even, c, a))
        bt = b.T
        mk.append(jnp.where(row <= col, b, bt))
        rk.append(jnp.where(row == col, ex[i:i + 1], jnp.where(row <= col, bt, b)))
    mk.append(rk.pop())
    return mk, nk, rk

def dense_kernel(*refs):
    mine, other = refs[:2]
    v0h, v0m, v1h, v1m, v2h, v2m, f1h, f1m, f2h, f2m = refs[2:12]
    states, steps = refs[12:14]
    k_ref, a_ref, z_ref, out_ref, out_sem = refs[14:19]
    res, bad = small(*unpack(mine, other), newton_factor, jnp.zeros((1, 128), jnp.float32))
    k_ref[...] = res
    worst = jnp.sum(bad)
    @pl.when(jnp.logical_not(worst < 4e-5))
    def _():
        k_ref[...] = small(*unpack(mine, other), functools.partial(direct_factor, a_ref, z_ref), None)[0]
    kk = parts(jnp.concatenate([k_ref[0:128], k_ref[384:512], k_ref[128:256], k_ref[512:640], k_ref[256:384]], axis=0), 2)
    def rows(at):
        return slice(128 * at, 128 * at + 128)
    def pair(i, v0, v1, v2, f1, f2):
        one = v1[rows(i - 1)] if 1 <= i <= 6 else f1[rows(i // 7)]
        two = v2[rows(i - 2), 0:128] if 2 <= i <= 5 else f2[rows(i if i < 2 else i - 4)]
        return jnp.concatenate([v0[rows(i)], one, two], axis=1)
    copies = []
    for i in range(4):
        v = [jnp.concatenate([pair(2 * i + j, *q) for j in range(2)], axis=0)
             for q in ((v0h, v1h, v2h, f1h, f2h), (v0m, v1m, v2m, f1m, f2m))]
        out = dot(v, kk, 2)
        for j, ref in enumerate((states, steps)):
            out_ref[j, 256 * i:256 * i + 256] = out[:, 128 * j:128 * j + 128]
            copies.append(pltpu.make_async_copy(out_ref.at[j, 256 * i:256 * i + 256], ref.at[256 * i:256 * i + 256], out_sem.at[len(copies)]))
            copies[-1].start()
    for c in copies:
        c.wait()

def dense_call(mine, other, *kept):
    vm = pl.BlockSpec(memory_space=pltpu.VMEM)
    hbm = pl.BlockSpec(memory_space=pl.ANY)
    square = pltpu.VMEM((128, 128), jnp.float32)
    return pl.pallas_call(dense_kernel, in_specs=[vm] * 12, out_specs=[hbm] * 2,
        out_shape=[jax.ShapeDtypeStruct((1024, 128), jnp.float32)] * 2,
        scratch_shapes=[pltpu.VMEM((640, 256), jnp.float32), square, square, pltpu.VMEM((2, 1024, 128), jnp.float32)]
        + [pltpu.SemaphoreType.DMA((8,))],
        name="dense", compiler_params=pltpu.CompilerParams(vmem_limit_bytes=24 * 2**20))(mine, other, *kept)


VM = pl.BlockSpec(memory_space=pltpu.VMEM)
ANY = pl.BlockSpec(memory_space=pl.ANY)
DMA = pltpu.SemaphoreType.DMA


def f32(*shape):
    return jax.ShapeDtypeStruct(shape, jnp.float32)


def bf16(*shape):
    return jax.ShapeDtypeStruct(shape, jnp.bfloat16)


def params(mib):
    return pltpu.CompilerParams(vmem_limit_bytes=mib * 2**20)


def weights(total, col):
    row = lax.axis_index("rows") * 16 + lax.broadcasted_iota(jnp.int32, (4, 16), 1)
    ahead = lax.rem(col[...] - row + total, total)
    return jnp.where(ahead == 1, 1.0, 0.0), jnp.where(ahead == 2, 1.0, 0.0)


def pair_blocks(one, two, onsite, coup, pair, at):
    def offsets(b, k):
        a1 = jnp.zeros((64, 64), jnp.float32)
        a2 = jnp.zeros((64, 64), jnp.float32)
        for j in range(4):
            c = coup[k, j]
            a1 = a1 + one[j:j + 1, b:b + 1] * c
            a2 = a2 + two[j:j + 1, b:b + 1] * c
        return a1, a2
    a1, a2 = offsets(2 * pair, at)
    b1, b2 = offsets(2 * pair + 1, at + 1)
    o0, o1 = onsite[at], onsite[at + 1]
    u = jnp.concatenate([jnp.concatenate([a2, jnp.zeros((64, 64), jnp.float32)], axis=1), jnp.concatenate([b1, b2], axis=1)], axis=0)
    d = jnp.concatenate([jnp.concatenate([o0 + o0.T, a1], axis=1), jnp.concatenate([a1.T, o1 + o1.T], axis=1)], axis=0)
    return u, d


def edge_kernel(total, col, onsite, coup, x, p, out, col_v, on_v, co_v, x_v, p_v, third, out_v, sem, out_sem):
    odd = lax.rem(lax.axis_index("rows"), 2)
    even = odd == 0
    pairs = [(col, col_v), (onsite.at[pl.ds(odd * 12, 4)], on_v), (coup.at[pl.ds(odd * 12, 4)], co_v),
             (x.at[pl.ds(pl.multiple_of(odd * 768, 128), 256)], x_v), (p.at[pl.ds(pl.multiple_of(odd * 768, 128), 256)], p_v),
             (x.at[256:384], third)]
    fetch = [pltpu.make_async_copy(a, b, sem.at[i]) for i, (a, b) in enumerate(pairs)]
    for c in fetch:
        c.start()
    for c in fetch[:3]:
        c.wait()
    one, two = [jnp.where(even, w[:, 0:4], w[:, 12:16]) for w in weights(total, col_v)]
    ua, da = pair_blocks(one, two, on_v, co_v, 0, 0)
    ub, db = pair_blocks(one, two, on_v, co_v, 1, 2)
    for c in fetch[3:]:
        c.wait()
    outermost = pl.ds(pl.multiple_of(odd * 128, 128), 128)
    out_v[0:128] = x_v[outermost]
    out_v[128:256] = p_v[outermost]
    out_v[512:640] = jnp.where(even, da, ub)
    x01 = x_v[...]
    w = dot(jnp.concatenate([jnp.where(even, da, ua.T), jnp.where(even, ua, db)], axis=1), jnp.concatenate([x01, p_v[...]], axis=1), 2)
    out_v[256:384], out_v[384:512] = w[:, :128], w[:, 128:]
    store = [pltpu.make_async_copy(out_v.at[s], out.at[s], out_sem.at[i]) for i, s in enumerate((slice(0, 640), slice(640, 768)))]
    store[0].start()
    hx = dot(jnp.concatenate([ua.T, db, ub], axis=1), jnp.concatenate([x01, third[...]], axis=0), 2)
    out_v[640:768] = dot(ua, hx, 2)
    store[1].start()
    for c in store:
        c.wait()


def edge_call(total, columns, onsite, couplings, x, p):
    def scratch(*shape):
        return pltpu.VMEM(shape, jnp.float32)
    return pl.pallas_call(lambda *a: edge_kernel(total, *a), in_specs=[ANY] * 5, out_specs=ANY, out_shape=f32(768, 128),
        scratch_shapes=[pltpu.VMEM((4, 16), jnp.int32), scratch(4, 64, 64), scratch(4, 4, 64, 64), scratch(256, 128), scratch(256, 128), scratch(128, 128),
                        scratch(768, 128), DMA((6,)), DMA((2,))], name="edge",
        compiler_params=params(60))(columns, onsite, couplings, x, p)


def put(h, l, at, val):
    a, b = parts(val, 2)
    h[at * 128:at * 128 + 128] = a
    l[at * 128:at * 128 + 128] = b


def band(lower, diag, upper):
    return [jnp.concatenate([lower[k], diag[k], upper[k]], axis=1) for k in range(2)]


def half_product(diag, upper, h, l, at):
    s = slice(at * 128, at * 128 + 256)
    b = [jnp.concatenate([diag[k] * jnp.bfloat16(0.5), upper[k]], axis=1) for k in range(2)]
    return dot(b, [h[s, 0:128], l[s, 0:128]], 2)


def inner_kernel(total, col, onsite, coup, x, p, side, uh, um, dh, dm, v0h, v0m, v1h, v1m, v2h, v2m, t0, t1, t2, t3, t4, t5):
    one, two = weights(total, col)
    even = lax.rem(lax.axis_index("rows"), 2) == 0
    side[0:128] = jnp.where(even, x[896:1024], x[0:128])
    side[128:256] = jnp.where(even, p[896:1024], p[0:128])
    for i in range(8):
        u, d = pair_blocks(one, two, onsite, coup, i, 2 * i)
        if i == 0:
            d0 = d
        if i == 7:
            side[512:640] = jnp.where(even, u, d0)
        uh[i], um[i] = parts(u, 2)
        dh[i], dm[i] = parts(d, 2)
        s = slice(128 * i, 128 * i + 128)
        put(v0h, v0m, i, jnp.concatenate([x[s], p[s]], axis=1))
    us = [[uh[i], um[i]] for i in range(8)]
    ds = [[dh[i], dm[i]] for i in range(8)]
    bands = {i: band([a.T for a in us[i - 1]], ds[i], us[i]) for i in range(1, 7)}
    for i in range(1, 7):
        s = slice((i - 1) * 128, (i + 2) * 128)
        put(v1h, v1m, i - 1, dot(bands[i], [v0h[s], v0m[s]], 2))
    for i in range(2, 6):
        s = slice((i - 2) * 128, (i + 1) * 128)
        put(v2h, v2m, i - 2, dot(bands[i], [v1h[s], v1m[s]], 2))
    first = dot([jnp.concatenate([a, b], axis=1) for a, b in zip(ds[0], us[0])], [v0h[0:256], v0m[0:256]], 2)
    last = dot([jnp.concatenate([a.T, b], axis=1) for a, b in zip(us[6], ds[7])], [v0h[768:1024], v0m[768:1024]], 2)
    w = jnp.where(even, last, first)
    side[256:384], side[384:512] = w[:, :128], w[:, 128:]
    side[640:768] = dot(us[0], [v1h[0:128, 0:128], v1m[0:128, 0:128]], 2)
    w0 = [v0h[...], v0m[...]]
    w0i = [v0h[128:896], v0m[128:896]]
    w1 = [v1h[...], v1m[...]]
    w1i = [v1h[128:640], v1m[128:640]]
    w2 = [v2h[...], v2m[...]]
    w2x = [v2h[:, 0:128], v2m[:, 0:128]]
    t0[...] = dot(w0, w0, 2, 0, 0)
    t1[...] = dot(w0i, w1, 2, 0, 0)
    t2[...] = dot(w1, w1, 2, 0, 0)
    t3[...] = dot(w1i, w2, 2, 0, 0)
    t4[...] = dot(w2x, w2, 2, 0, 0)
    half = jnp.concatenate([half_product(ds[i], us[i], v2h, v2m, i - 2) for i in range(2, 5)], axis=0)
    t5[...] = dot([a[0:384] for a in w2x], half, 2, 0, 0)


def inner_call(total, columns, onsite, couplings, x, p):
    return pl.pallas_call(lambda *a: inner_kernel(total, *a), in_specs=[VM] * 5, out_specs=[VM] * 17,
        out_shape=[f32(768, 128)] + [bf16(8, 128, 128)] * 4 + [bf16(1024, 256)] * 2 + [bf16(768, 256)] * 2 + [bf16(512, 256)] * 2
        + [f32(256, 256)] * 4 + [f32(128, 256), f32(128, 128)], name="inner",
        compiler_params=params(24))(columns, onsite, couplings, x, p)


def outer_kernel(ra, rb, uh, um, dh, dm, v0h, v0m, v1h, v1m, v2h, v2m, t0, t1, t2, t3, t4, t5, own, msg, f1h, f1m, f2h, f2m,
                 e0h, e0m, e1h, e1m, e2h, e2m):
    odd = lax.rem(lax.axis_index("rows"), 2)
    even = odd == 0
    def before(s):
        return jnp.where(even, rb[s], ra[s])
    def after(s):
        return jnp.where(even, ra[s], rb[s])
    def rows(at, n=1):
        return slice(at * 128, (at + n) * 128)
    def wide(side, at):
        return jnp.concatenate([side(rows(at)), side(rows(at + 1))], axis=1)
    put(e0h, e0m, 0, wide(before, 0))
    put(e0h, e0m, 5, wide(after, 0))
    for e, v in ((e0h, v0h), (e0m, v0m)):
        e[rows(1, 2)] = v[rows(0, 2)]
        e[rows(3, 2)] = v[rows(6, 2)]
    us = {i: [uh[i], um[i]] for i in range(8)}
    ds = {i: [dh[i], dm[i]] for i in range(8)}
    us[-1] = parts(before(rows(4)), 2)
    ds[8] = parts(after(rows(4)), 2)
    ut = {i: [a.T for a in us[i]] for i in (-1, 0, 5, 6, 7)}
    bands = {i: band(ut[i - 1], ds[i], us[i]) for i in (0, 1, 6, 7)}
    put(e1h, e1m, 0, wide(before, 2) + dot(us[-1], [v0h[rows(0)], v0m[rows(0)]], 2))
    put(e1h, e1m, 7, wide(after, 2) + dot(ut[7], [v0h[rows(7)], v0m[rows(7)]], 2))
    for i, at, src in ((0, 1, 0), (7, 6, 3)):
        s = rows(src, 3)
        put(e1h, e1m, at, dot(bands[i], [e0h[s], e0m[s]], 2))
    for e, v in ((e1h, v1h), (e1m, v1m)):
        e[rows(2, 2)] = v[rows(0, 2)]
        e[rows(4, 2)] = v[rows(4, 2)]
    for i, at, src in ((0, 0, 0), (1, 1, 1), (6, 4, 4), (7, 5, 5)):
        s = rows(src, 3)
        put(e2h, e2m, at, dot(bands[i], [e1h[s], e1m[s]], 2))
    eight = after(rows(5)) + dot([jnp.concatenate([a, b], axis=1) for a, b in zip(ut[7], ds[8])], [e[rows(6, 2), 0:128] for e in (e1h, e1m)], 2)
    put(e2h, e2m, 6, jnp.concatenate([eight, jnp.zeros((128, 128), jnp.float32)], axis=1))
    for e, v in ((e2h, v2h), (e2m, v2m)):
        e[rows(2)] = v[rows(0)]
        e[rows(3)] = v[rows(3)]
    def join(a, b, i, n, j, m):
        return [jnp.concatenate([q[rows(i, n)], q[rows(j, m)]], axis=0) for q in (a, b)]
    w0 = join(v0h, v0m, 0, 1, 7, 1)
    w1 = join(e1h, e1m, 1, 1, 6, 1)
    w1w = join(e1h, e1m, 1, 2, 5, 2)
    w2 = join(e2h, e2m, 0, 2, 4, 2)
    w2x = [a[:, 0:128] for a in w2]
    for f, v in ((f1h, w1[0]), (f1m, w1[1]), (f2h, w2x[0]), (f2m, w2x[1])):
        f[...] = v
    half = jnp.concatenate([half_product(ds[i], us[i], e2h, e2m, at) for i, at in ((0, 0), (1, 1), (5, 3), (6, 4), (7, 5))], axis=0)
    wh = [jnp.concatenate([q[rows(0, 2)], q[rows(3, 3)]], axis=0)[:, 0:128] for q in (e2h, e2m)]
    t = [t0[...], t1[...] + dot(w0, w1, 2, 0, 0), t2[...] + dot(w1, w1, 2, 0, 0), t3[...] + dot(w1w, w2, 2, 0, 0),
         t4[...] + dot(w2x, w2, 2, 0, 0)]
    m5 = t5[...] + dot(wh, half, 2, 0, 0)
    m5 = m5 + m5.T
    row, col = iotas(128, 128)
    pairs = [(b[:128, :128], b[128:, 128:]) for b in t[:4]] + [(t[4][:, :128], m5)]
    ex = [jnp.sum(jnp.where(row == col, b, 0.0), axis=0, keepdims=True) for _, b in pairs]
    ex = jnp.broadcast_to(jnp.concatenate(ex + [jnp.zeros((3, 128), jnp.float32)], axis=0)[None], (16, 8, 128))
    for i, (a, b) in enumerate(pairs):
        c = jnp.where(row <= col, a, b)
        d = t[i][:128, 128:]
        own[:, 8 * i:8 * i + 8] = jnp.where(even, c, d).reshape(16, 8, 128)
        msg[:, 8 * i:8 * i + 8] = jnp.where(even, d, c).reshape(16, 8, 128)
    own[:, 40:48] = ex
    msg[:, 40:48] = ex


def outer_call(*args):
    return pl.pallas_call(outer_kernel, in_specs=[VM] * 18, out_specs=[VM] * 6,
        out_shape=[f32(16, 48, 128)] * 2 + [bf16(256, 256)] * 2 + [bf16(512, 128)] * 2,
        scratch_shapes=[pltpu.VMEM((n * 128, 256), jnp.bfloat16) for n in (6, 6, 8, 8, 7, 7)],
        name="outer", compiler_params=params(24))(*args)


def groups(key):
    found = {}
    for i in range(N):
        found.setdefault(key(i), []).append(i)
    return list(found.values())


def next_chip(block):
    return lax.ppermute(block, "rows", [(i, (i + 1) % N if i % 2 else (i - 1) % N) for i in range(N)])


def across_chip(block):
    return lax.ppermute(block, "rows", [(i, i ^ 1) for i in range(N)])


def in_plane(block):
    return lax.all_to_all(block, "rows", 0, 0, axis_index_groups=groups(lambda i: i % 16))


def along_z(block):
    return lax.all_to_all(block, "rows", 0, 0, axis_index_groups=groups(lambda i: (i // 16, i % 2)))


def copies(block, n):
    return jnp.broadcast_to(block[None], (n,) + block.shape)


def reduce_all(own, msg):
    part = jnp.sum(in_plane(own + across_chip(msg)), axis=0)
    part = jnp.sum(along_z(copies(part, 8)), axis=0)
    own = in_plane(copies(part, 16))
    return own, across_chip(own)


def body(start_states, start_steps, onsite, couplings, columns):
    total = onsite.shape[0] * N
    arrays = (total, columns.T, onsite, couplings, start_states, start_steps)
    from_chip = next_chip(edge_call(*arrays))
    to_core, *made = inner_call(*arrays)
    from_core = across_chip(to_core)
    own, msg, *edges = outer_call(from_core, from_chip, *made)
    mine, other = reduce_all(own, msg)
    return tuple(dense_call(mine, other, *made[4:10], *edges))


def solution(mesh):
    in_specs = (P("rows", None), P("rows", None), P("rows", None, None), P("rows", None, None, None), P("rows", None))
    out_specs = (P("rows", None), P("rows", None))
    return jax.shard_map(body, mesh=mesh, in_specs=in_specs, out_specs=out_specs, check_vma=False)
```

```python
import functools

import jax
import jax.numpy as jnp
from jax import lax
from jax.sharding import PartitionSpec as P
from jax.experimental import pallas as pl
from jax.experimental.pallas import tpu as pltpu

N = 256

def parts(a, n):
    out = []
    for i in range(n):
        h = a.astype(jnp.bfloat16)
        out.append(h)
        if i < n - 1:
            a = a - h.astype(jnp.float32)
    return out

TERMS = {1: [(0, 0)], 2: [(0, 0), (0, 1), (1, 0)], 3: [(0, 0), (0, 1), (1, 0), (1, 1), (0, 2), (2, 0)]}

def square_terms(a, b, cb):
    rows = a[0].shape[0]
    both = lax.dot_general(jnp.concatenate(a[:2], axis=0), jnp.concatenate(b[:2], axis=1 - cb), (((1,), (cb,)), ((), ())),
                           preferred_element_type=jnp.float32)
    return both[:rows, :128] + (both[:rows, 128:] + both[rows:, :128] + both[rows:, 128:])

def dot(a, b, n=2, ca=1, cb=0):
    a = a if isinstance(a, list) else parts(a, n)
    b = b if isinstance(b, list) else parts(b, n)
    if ca == 0:
        a, ca = flipped(a[:n]), 1
    narrow = b[0].shape[1 - cb] == 128
    if n == 2 and narrow:
        return square_terms(a, b, cb)
    lhs = [a[i] for i, _ in TERMS[n]]
    rhs = [b[j] for _, j in TERMS[n]]
    lhs = lhs[0] if n == 1 else jnp.concatenate(lhs, axis=ca)
    rhs = rhs[0] if n == 1 else jnp.concatenate(rhs, axis=cb)
    return lax.dot_general(lhs, rhs, (((ca,), (cb,)), ((), ())), preferred_element_type=jnp.float32)

def flipped(a):
    return [q.T for q in a]

def iotas(n, m):
    return lax.broadcasted_iota(jnp.int32, (n, m), 0), lax.broadcasted_iota(jnp.int32, (n, m), 1)

def newton_factor(g, bad, panel=None, right=None):
    row, col = iotas(128, 128)
    diag = row == col
    weight = jnp.where(row > col, 1.0, jnp.where(diag, 0.5, 0.0))
    dg = jnp.where(diag, g, 0.0)
    dr = lax.rsqrt(jnp.sum(dg, axis=0, keepdims=True))
    dc = lax.rsqrt(jnp.sum(dg, axis=1, keepdims=True))
    one = jnp.where(diag, 1.0, 0.0)
    g = g * dr * dc
    f = jnp.where(row > col, g, 0.0)
    fp = parts(f, 1)
    z = one - f + dot(fp, fp, 1) + weight * dot(fp, fp, 1, 1, 1)
    zp = parts(z, 2)
    e = dot(dot(zp, g, 2), zp, 2, 1, 1) - one
    step = parts(weight * e, 1)
    if panel is not None:
        with_it = dot(panel * dr, zp, 2, 1, 1)
        with_it = with_it - dot(with_it, step, 1, 1, 1)
    if right is not None:
        with_it = dot(zp, right * dc, 2)
        with_it = with_it - dot(step, with_it, 1)
    z = z - dot(step, zp, 1)
    return z * dr, with_it, jnp.maximum(bad, jnp.sum(e * e, axis=0, keepdims=True))

def direct_factor(a_ref, z_ref, g, bad, panel=None, right=None):
    row, col = iotas(128, 128)
    a_ref[...] = g
    z_ref[...] = jnp.where(row == col, 1.0, 0.0)
    def step(j, _):
        r = a_ref[pl.ds(j, 1), :]
        zr = z_ref[pl.ds(j, 1), :]
        a = a_ref[...]
        c = jnp.sum(jnp.where(col == j, a, 0.0), axis=1, keepdims=True)
        d = jnp.sum(jnp.where(col[:1] == j, r, 0.0), axis=1, keepdims=True)
        f = jnp.where(row[:, :1] > j, c / d, 0.0)
        a_ref[...] = a - f * r
        z_ref[...] = z_ref[...] - f * zr
        return 0
    lax.fori_loop(0, 128, step, 0)
    d = jnp.sum(jnp.where(row == col, a_ref[...], 0.0), axis=1, keepdims=True)
    w = z_ref[...] / jnp.sqrt(d)
    return w, dot(w, right, 3) if panel is None else dot(panel, w, 3, 1, 1), bad

def cat(blocks):
    return jnp.concatenate([jnp.concatenate(r, axis=1) for r in blocks], axis=0)

def block_inverse(g, factor, bad):
    w1, l, bad = factor(g[0][0], bad, panel=jnp.concatenate([g[1][0], g[2][0]], axis=0))
    lp = parts(l, 2)
    p = dot(lp, lp, 2, 1, 1)
    w2, l32, bad = factor(g[1][1] - p[:128, :128], bad, panel=g[2][1] - p[128:, :128])
    m = dot(lp, w1)
    a21 = -dot(w2, m[:128])
    l32p = parts(l32, 2)
    t = m[128:] + dot(l32p, a21)
    s = dot(l32p, w2)
    w3, low, bad = factor(g[2][2] - p[128:, 128:] - dot(l32p, l32p, 2, 1, 1), bad, right=jnp.concatenate([t, s], axis=1))
    zero = jnp.zeros((128, 128), jnp.float32)
    return cat([[w1, zero, zero], [a21, w2, zero], [-low[:, :128], -low[:, 128:], w3]]), bad

def projected_filter(inv, a):
    def at(i, n=1):
        return slice(128 * i, 128 * i + 128 * n)
    ip = parts(inv, 2)
    ap = parts(a, 2)
    t = [dot([q[at(i), at(0, i + 1)] for q in ip], [q[at(0, i + 1)] for q in ap]) for i in range(3)]
    tp = parts(jnp.concatenate(t, axis=0), 2)
    c = [dot([q[at(j, 3 - j), at(0, j + 1)] for q in tp], [q[at(j), at(0, j + 1)] for q in ip], 2, 1, 1) for j in range(3)]
    p10, p20, p21 = c[0][at(1)], c[0][at(2)], c[1][at(1)]
    proj = cat([[sym(c[0][at(0)]), p10.T, p20.T], [p10, sym(c[1][at(0)]), p21.T], [p20, p21, sym(c[2])]])
    bound = jnp.max(jnp.sum(jnp.abs(proj), axis=0, keepdims=True), axis=1, keepdims=True)
    pp = parts(proj, 2)
    second = dot(pp, [q[:, :128] for q in pp])
    third = dot(pp, second)
    scale = 1.0 / bound
    row, col = iotas(384, 128)
    f = jnp.where(row == col, 1.0, 0.0) - scale * (3.0 * proj[:, :128] - scale * (3.0 * second - scale * third))
    return pp, ip, f

def back(ip, f):
    fp = parts(f, 2)
    it = flipped([q[128:] for q in ip])
    part = dot(it, [q[128:] for q in fp], 2)
    head = dot([q[:128, :128] for q in ip], [q[:128] for q in fp], 2, 0, 0)
    return jnp.concatenate([jnp.concatenate([part[:128] + head, part[128:]], axis=0), part], axis=1)

def sym(a):
    return 0.5 * (a + a.T)

def small(mk, nk, rk, factor, bad):
    def assemble(k):
        return [[mk[k], mk[k + 1], nk[k]], [mk[k + 1], mk[k + 2], nk[k + 1]], [nk[k].T, nk[k + 1].T, rk[k]]]
    inv, bad = block_inverse(assemble(0), factor, bad)
    pp, ip, f = projected_filter(inv, cat(assemble(1)))
    f2 = jnp.concatenate([jnp.zeros((128, 128), jnp.float32), f[128:]], axis=0)
    ff2 = jnp.concatenate([f, f2], axis=1)
    ffp = parts(ff2, 3)
    fp = [q[:, :128] for q in ffp]
    cq = back(ip, f)
    cqp = parts(cq, 3)
    cp = [q[:, :128] for q in cqp]
    fft, ct = flipped(ffp), flipped(cp)
    gram = dot(fft, ffp, 3)
    one = dot(fft, dot(pp, ffp), 2)
    two = dot(ct, dot(cat(assemble(2)), cqp), 2)
    three = dot(ct, dot(cat(assemble(3)), cp), 2)
    ftf, qq = gram[:128, :128], gram[128:, 128:]
    b1, c1q, q1q = one[:128, :128], one[:128, 128:], one[128:, 128:]
    c2c, c2q = sym(two[:, :128]), two[:, 128:]
    b1 = sym(b1)
    gu = [[ftf, None, None], [b1, c2c, None], [qq, c1q.T, qq]]
    au = cat([[b1, c2c, c1q], [c2c, sym(three), c2q], [c1q.T, c2q.T, sym(q1q)]])
    inv, bad = block_inverse(gu, factor, bad)
    _, ip, f = projected_filter(inv, au)
    fp = parts(f, 3)
    _, y, bad = factor(dot(fp, fp, 3, 0, 0), bad, panel=f)
    k = back(ip, y)
    kb = dot(cqp, jnp.concatenate([k[:128], k[256:]], axis=0))
    kh = dot(cp, k[128:256])
    return jnp.concatenate([kb[:128], kb[128:256] + kh[:128], kh[128:256], kb[256:], kh[256:]], axis=0), bad

def unpack(mine, other):
    row, col = iotas(128, 128)
    even = lax.rem(lax.axis_index("rows"), 2) == 0
    ex = mine[0, 40:48]
    mk, nk, rk = [], [], []
    for i in range(5):
        a, c = [q[:, 8 * i:8 * i + 8].reshape(128, 128) for q in (mine, other)]
        b = jnp.where(even, a, c)
        nk.append(jnp.where(even, c, a))
        bt = b.T
        mk.append(jnp.where(row <= col, b, bt))
        rk.append(jnp.where(row == col, ex[i:i + 1], jnp.where(row <= col, bt, b)))
    mk.append(rk.pop())
    return mk, nk, rk

def dense_kernel(*refs):
    mine, other = refs[:2]
    v0h, v0m, v1h, v1m, v2h, v2m, f1h, f1m, f2h, f2m = refs[2:12]
    states, steps = refs[12:14]
    k_ref, a_ref, z_ref, out_ref, out_sem = refs[14:19]
    res, bad = small(*unpack(mine, other), newton_factor, jnp.zeros((1, 128), jnp.float32))
    k_ref[...] = res
    worst = jnp.sum(bad)
    @pl.when(jnp.logical_not(worst < 4e-5))
    def _():
        k_ref[...] = small(*unpack(mine, other), functools.partial(direct_factor, a_ref, z_ref), None)[0]
    kk = parts(jnp.concatenate([k_ref[0:128], k_ref[384:512], k_ref[128:256], k_ref[512:640], k_ref[256:384]], axis=0), 2)
    def rows(at):
        return slice(128 * at, 128 * at + 128)
    def pair(i, v0, v1, v2, f1, f2):
        one = v1[rows(i - 1)] if 1 <= i <= 6 else f1[rows(i // 7)]
        two = v2[rows(i - 2), 0:128] if 2 <= i <= 5 else f2[rows(i if i < 2 else i - 4)]
        return jnp.concatenate([v0[rows(i)], one, two], axis=1)
    copies = []
    for i in range(4):
        v = [jnp.concatenate([pair(2 * i + j, *q) for j in range(2)], axis=0)
             for q in ((v0h, v1h, v2h, f1h, f2h), (v0m, v1m, v2m, f1m, f2m))]
        out = dot(v, kk, 2)
        for j, ref in enumerate((states, steps)):
            out_ref[j, 256 * i:256 * i + 256] = out[:, 128 * j:128 * j + 128]
            copies.append(pltpu.make_async_copy(out_ref.at[j, 256 * i:256 * i + 256], ref.at[256 * i:256 * i + 256], out_sem.at[len(copies)]))
            copies[-1].start()
    for c in copies:
        c.wait()

def dense_call(mine, other, *kept):
    vm = pl.BlockSpec(memory_space=pltpu.VMEM)
    hbm = pl.BlockSpec(memory_space=pl.ANY)
    square = pltpu.VMEM((128, 128), jnp.float32)
    return pl.pallas_call(dense_kernel, in_specs=[vm] * 12, out_specs=[hbm] * 2,
        out_shape=[jax.ShapeDtypeStruct((1024, 128), jnp.float32)] * 2,
        scratch_shapes=[pltpu.VMEM((640, 256), jnp.float32), square, square, pltpu.VMEM((2, 1024, 128), jnp.float32)]
        + [pltpu.SemaphoreType.DMA((8,))],
        name="dense", compiler_params=pltpu.CompilerParams(vmem_limit_bytes=24 * 2**20))(mine, other, *kept)


VM = pl.BlockSpec(memory_space=pltpu.VMEM)
ANY = pl.BlockSpec(memory_space=pl.ANY)
DMA = pltpu.SemaphoreType.DMA


def f32(*shape):
    return jax.ShapeDtypeStruct(shape, jnp.float32)


def bf16(*shape):
    return jax.ShapeDtypeStruct(shape, jnp.bfloat16)


def params(mib):
    return pltpu.CompilerParams(vmem_limit_bytes=mib * 2**20)


def weights(total, col):
    row = lax.axis_index("rows") * 16 + lax.broadcasted_iota(jnp.int32, (4, 16), 1)
    ahead = lax.rem(col[...] - row + total, total)
    return jnp.where(ahead == 1, 1.0, 0.0), jnp.where(ahead == 2, 1.0, 0.0)


def pair_blocks(one, two, onsite, coup, pair, at):
    def offsets(b, k):
        a1 = jnp.zeros((64, 64), jnp.float32)
        a2 = jnp.zeros((64, 64), jnp.float32)
        for j in range(4):
            c = coup[k, j]
            a1 = a1 + one[j:j + 1, b:b + 1] * c
            a2 = a2 + two[j:j + 1, b:b + 1] * c
        return a1, a2
    a1, a2 = offsets(2 * pair, at)
    b1, b2 = offsets(2 * pair + 1, at + 1)
    o0, o1 = onsite[at], onsite[at + 1]
    u = jnp.concatenate([jnp.concatenate([a2, jnp.zeros((64, 64), jnp.float32)], axis=1), jnp.concatenate([b1, b2], axis=1)], axis=0)
    d = jnp.concatenate([jnp.concatenate([o0 + o0.T, a1], axis=1), jnp.concatenate([a1.T, o1 + o1.T], axis=1)], axis=0)
    return u, d


def edge_kernel(total, col, onsite, coup, x, p, out, col_v, on_v, co_v, x_v, p_v, third, out_v, sem, out_sem):
    odd = lax.rem(lax.axis_index("rows"), 2)
    even = odd == 0
    pairs = [(col, col_v), (onsite.at[pl.ds(odd * 12, 4)], on_v), (coup.at[pl.ds(odd * 12, 4)], co_v),
             (x.at[pl.ds(pl.multiple_of(odd * 768, 128), 256)], x_v), (p.at[pl.ds(pl.multiple_of(odd * 768, 128), 256)], p_v),
             (x.at[256:384], third)]
    fetch = [pltpu.make_async_copy(a, b, sem.at[i]) for i, (a, b) in enumerate(pairs)]
    for c in fetch:
        c.start()
    for c in fetch[:3]:
        c.wait()
    one, two = [jnp.where(even, w[:, 0:4], w[:, 12:16]) for w in weights(total, col_v)]
    ua, da = pair_blocks(one, two, on_v, co_v, 0, 0)
    ub, db = pair_blocks(one, two, on_v, co_v, 1, 2)
    for c in fetch[3:]:
        c.wait()
    outermost = pl.ds(pl.multiple_of(odd * 128, 128), 128)
    out_v[0:128] = x_v[outermost]
    out_v[128:256] = p_v[outermost]
    out_v[512:640] = jnp.where(even, da, ub)
    x01 = x_v[...]
    w = dot(jnp.concatenate([jnp.where(even, da, ua.T), jnp.where(even, ua, db)], axis=1), jnp.concatenate([x01, p_v[...]], axis=1), 2)
    out_v[256:384], out_v[384:512] = w[:, :128], w[:, 128:]
    store = [pltpu.make_async_copy(out_v.at[s], out.at[s], out_sem.at[i]) for i, s in enumerate((slice(0, 640), slice(640, 768)))]
    store[0].start()
    hx = dot(jnp.concatenate([ua.T, db, ub], axis=1), jnp.concatenate([x01, third[...]], axis=0), 2)
    out_v[640:768] = dot(ua, hx, 2)
    store[1].start()
    for c in store:
        c.wait()


def edge_call(total, columns, onsite, couplings, x, p):
    def scratch(*shape):
        return pltpu.VMEM(shape, jnp.float32)
    return pl.pallas_call(lambda *a: edge_kernel(total, *a), in_specs=[ANY] * 5, out_specs=ANY, out_shape=f32(768, 128),
        scratch_shapes=[pltpu.VMEM((4, 16), jnp.int32), scratch(4, 64, 64), scratch(4, 4, 64, 64), scratch(256, 128), scratch(256, 128), scratch(128, 128),
                        scratch(768, 128), DMA((6,)), DMA((2,))], name="edge",
        compiler_params=params(60))(columns, onsite, couplings, x, p)


def put(h, l, at, val):
    a, b = parts(val, 2)
    h[at * 128:at * 128 + 128] = a
    l[at * 128:at * 128 + 128] = b


def band(lower, diag, upper):
    return [jnp.concatenate([lower[k], diag[k], upper[k]], axis=1) for k in range(2)]


def half_product(diag, upper, h, l, at):
    s = slice(at * 128, at * 128 + 256)
    b = [jnp.concatenate([diag[k] * jnp.bfloat16(0.5), upper[k]], axis=1) for k in range(2)]
    return dot(b, [h[s, 0:128], l[s, 0:128]], 2)


def inner_kernel(total, col, onsite, coup, x, p, side, uh, um, dh, dm, v0h, v0m, v1h, v1m, v2h, v2m, t0, t1, t2, t3, t4, t5):
    one, two = weights(total, col)
    even = lax.rem(lax.axis_index("rows"), 2) == 0
    side[0:128] = jnp.where(even, x[896:1024], x[0:128])
    side[128:256] = jnp.where(even, p[896:1024], p[0:128])
    for i in range(8):
        u, d = pair_blocks(one, two, onsite, coup, i, 2 * i)
        if i == 0:
            d0 = d
        if i == 7:
            side[512:640] = jnp.where(even, u, d0)
        uh[i], um[i] = parts(u, 2)
        dh[i], dm[i] = parts(d, 2)
        s = slice(128 * i, 128 * i + 128)
        put(v0h, v0m, i, jnp.concatenate([x[s], p[s]], axis=1))
    us = [[uh[i], um[i]] for i in range(8)]
    ds = [[dh[i], dm[i]] for i in range(8)]
    bands = {i: band([a.T for a in us[i - 1]], ds[i], us[i]) for i in range(1, 7)}
    for i in range(1, 7):
        s = slice((i - 1) * 128, (i + 2) * 128)
        put(v1h, v1m, i - 1, dot(bands[i], [v0h[s], v0m[s]], 2))
    for i in range(2, 6):
        s = slice((i - 2) * 128, (i + 1) * 128)
        put(v2h, v2m, i - 2, dot(bands[i], [v1h[s], v1m[s]], 2))
    first = dot([jnp.concatenate([a, b], axis=1) for a, b in zip(ds[0], us[0])], [v0h[0:256], v0m[0:256]], 2)
    last = dot([jnp.concatenate([a.T, b], axis=1) for a, b in zip(us[6], ds[7])], [v0h[768:1024], v0m[768:1024]], 2)
    w = jnp.where(even, last, first)
    side[256:384], side[384:512] = w[:, :128], w[:, 128:]
    side[640:768] = dot(us[0], [v1h[0:128, 0:128], v1m[0:128, 0:128]], 2)
    w0 = [v0h[...], v0m[...]]
    w0i = [v0h[128:896], v0m[128:896]]
    w1 = [v1h[...], v1m[...]]
    w1i = [v1h[128:640], v1m[128:640]]
    w2 = [v2h[...], v2m[...]]
    w2x = [v2h[:, 0:128], v2m[:, 0:128]]
    t0[...] = dot(w0, w0, 2, 0, 0)
    t1[...] = dot(w0i, w1, 2, 0, 0)
    t2[...] = dot(w1, w1, 2, 0, 0)
    t3[...] = dot(w1i, w2, 2, 0, 0)
    t4[...] = dot(w2x, w2, 2, 0, 0)
    half = jnp.concatenate([half_product(ds[i], us[i], v2h, v2m, i - 2) for i in range(2, 5)], axis=0)
    t5[...] = dot([a[0:384] for a in w2x], half, 2, 0, 0)


def inner_call(total, columns, onsite, couplings, x, p):
    return pl.pallas_call(lambda *a: inner_kernel(total, *a), in_specs=[VM] * 5, out_specs=[VM] * 17,
        out_shape=[f32(768, 128)] + [bf16(8, 128, 128)] * 4 + [bf16(1024, 256)] * 2 + [bf16(768, 256)] * 2 + [bf16(512, 256)] * 2
        + [f32(256, 256)] * 4 + [f32(128, 256), f32(128, 128)], name="inner",
        compiler_params=params(24))(columns, onsite, couplings, x, p)


def outer_kernel(ra, rb, uh, um, dh, dm, v0h, v0m, v1h, v1m, v2h, v2m, t0, t1, t2, t3, t4, t5, own, msg, f1h, f1m, f2h, f2m,
                 e0h, e0m, e1h, e1m, e2h, e2m):
    odd = lax.rem(lax.axis_index("rows"), 2)
    even = odd == 0
    def before(s):
        return jnp.where(even, rb[s], ra[s])
    def after(s):
        return jnp.where(even, ra[s], rb[s])
    def rows(at, n=1):
        return slice(at * 128, (at + n) * 128)
    def wide(side, at):
        return jnp.concatenate([side(rows(at)), side(rows(at + 1))], axis=1)
    put(e0h, e0m, 0, wide(before, 0))
    put(e0h, e0m, 5, wide(after, 0))
    for e, v in ((e0h, v0h), (e0m, v0m)):
        e[rows(1, 2)] = v[rows(0, 2)]
        e[rows(3, 2)] = v[rows(6, 2)]
    us = {i: [uh[i], um[i]] for i in range(8)}
    ds = {i: [dh[i], dm[i]] for i in range(8)}
    us[-1] = parts(before(rows(4)), 2)
    ds[8] = parts(after(rows(4)), 2)
    ut = {i: [a.T for a in us[i]] for i in (-1, 0, 5, 6, 7)}
    bands = {i: band(ut[i - 1], ds[i], us[i]) for i in (0, 1, 6, 7)}
    put(e1h, e1m, 0, wide(before, 2) + dot(us[-1], [v0h[rows(0)], v0m[rows(0)]], 2))
    put(e1h, e1m, 7, wide(after, 2) + dot(ut[7], [v0h[rows(7)], v0m[rows(7)]], 2))
    for i, at, src in ((0, 1, 0), (7, 6, 3)):
        s = rows(src, 3)
        put(e1h, e1m, at, dot(bands[i], [e0h[s], e0m[s]], 2))
    for e, v in ((e1h, v1h), (e1m, v1m)):
        e[rows(2, 2)] = v[rows(0, 2)]
        e[rows(4, 2)] = v[rows(4, 2)]
    for i, at, src in ((0, 0, 0), (1, 1, 1), (6, 4, 4), (7, 5, 5)):
        s = rows(src, 3)
        put(e2h, e2m, at, dot(bands[i], [e1h[s], e1m[s]], 2))
    eight = after(rows(5)) + dot([jnp.concatenate([a, b], axis=1) for a, b in zip(ut[7], ds[8])], [e[rows(6, 2), 0:128] for e in (e1h, e1m)], 2)
    put(e2h, e2m, 6, jnp.concatenate([eight, jnp.zeros((128, 128), jnp.float32)], axis=1))
    for e, v in ((e2h, v2h), (e2m, v2m)):
        e[rows(2)] = v[rows(0)]
        e[rows(3)] = v[rows(3)]
    def join(a, b, i, n, j, m):
        return [jnp.concatenate([q[rows(i, n)], q[rows(j, m)]], axis=0) for q in (a, b)]
    w0 = join(v0h, v0m, 0, 1, 7, 1)
    w1 = join(e1h, e1m, 1, 1, 6, 1)
    w1w = join(e1h, e1m, 1, 2, 5, 2)
    w2 = join(e2h, e2m, 0, 2, 4, 2)
    w2x = [a[:, 0:128] for a in w2]
    for f, v in ((f1h, w1[0]), (f1m, w1[1]), (f2h, w2x[0]), (f2m, w2x[1])):
        f[...] = v
    half = jnp.concatenate([half_product(ds[i], us[i], e2h, e2m, at) for i, at in ((0, 0), (1, 1), (5, 3), (6, 4), (7, 5))], axis=0)
    wh = [jnp.concatenate([q[rows(0, 2)], q[rows(3, 3)]], axis=0)[:, 0:128] for q in (e2h, e2m)]
    t = [t0[...], t1[...] + dot(w0, w1, 2, 0, 0), t2[...] + dot(w1, w1, 2, 0, 0), t3[...] + dot(w1w, w2, 2, 0, 0),
         t4[...] + dot(w2x, w2, 2, 0, 0)]
    m5 = t5[...] + dot(wh, half, 2, 0, 0)
    m5 = m5 + m5.T
    row, col = iotas(128, 128)
    pairs = [(b[:128, :128], b[128:, 128:]) for b in t[:4]] + [(t[4][:, :128], m5)]
    ex = [jnp.sum(jnp.where(row == col, b, 0.0), axis=0, keepdims=True) for _, b in pairs]
    ex = jnp.broadcast_to(jnp.concatenate(ex + [jnp.zeros((3, 128), jnp.float32)], axis=0)[None], (16, 8, 128))
    for i, (a, b) in enumerate(pairs):
        c = jnp.where(row <= col, a, b)
        d = t[i][:128, 128:]
        own[:, 8 * i:8 * i + 8] = jnp.where(even, c, d).reshape(16, 8, 128)
        msg[:, 8 * i:8 * i + 8] = jnp.where(even, d, c).reshape(16, 8, 128)
    own[:, 40:48] = ex
    msg[:, 40:48] = ex


def outer_call(*args):
    return pl.pallas_call(outer_kernel, in_specs=[VM] * 18, out_specs=[VM] * 6,
        out_shape=[f32(16, 48, 128)] * 2 + [bf16(256, 256)] * 2 + [bf16(512, 128)] * 2,
        scratch_shapes=[pltpu.VMEM((n * 128, 256), jnp.bfloat16) for n in (6, 6, 8, 8, 7, 7)],
        name="outer", compiler_params=params(24))(*args)


def groups(key):
    found = {}
    for i in range(N):
        found.setdefault(key(i), []).append(i)
    return list(found.values())


def next_chip(block):
    return lax.ppermute(block, "rows", [(i, (i + 1) % N if i % 2 else (i - 1) % N) for i in range(N)])


def across_chip(block):
    return lax.ppermute(block, "rows", [(i, i ^ 1) for i in range(N)])


def in_plane(block):
    return lax.all_to_all(block, "rows", 0, 0, axis_index_groups=groups(lambda i: i % 16))


def along_z(block):
    return lax.all_to_all(block, "rows", 0, 0, axis_index_groups=groups(lambda i: (i // 16, i % 2)))


def copies(block, n):
    return jnp.broadcast_to(block[None], (n,) + block.shape)


def reduce_all(own, msg):
    part = jnp.sum(in_plane(own + across_chip(msg)), axis=0)
    part = jnp.sum(along_z(copies(part, 8)), axis=0)
    own = in_plane(copies(part, 16))
    return own, across_chip(own)


def body(start_states, start_steps, onsite, couplings, columns):
    total = onsite.shape[0] * N
    arrays = (total, columns.T, onsite, couplings, start_states, start_steps)
    from_chip = next_chip(edge_call(*arrays))
    to_core, *made = inner_call(*arrays)
    from_core = across_chip(to_core)
    own, msg, *edges = outer_call(from_core, from_chip, *made)
    mine, other = reduce_all(own, msg)
    return tuple(dense_call(mine, other, *made[4:10], *edges))


def solution(mesh):
    in_specs = (P("rows", None), P("rows", None), P("rows", None, None), P("rows", None, None, None), P("rows", None))
    out_specs = (P("rows", None), P("rows", None))
    return jax.shard_map(body, mesh=mesh, in_specs=in_specs, out_specs=out_specs, check_vma=False)
```
